256 devices in a mesh: axial: 128 (over x, z_lo, y, core), radial: 2 (over z_hi).
Axes of the slice: x: 4, y: 4, z: 8 (z_hi: 2, z_lo: 4; z = z_hi * 4 + z_lo), core: 2. Of those that a mesh axis runs over, the one named last changes fastest.
Arguments:
- parcel_load: float32 [5, 4194304], P(None, ('axial', 'radial')), may hold values from -6 to 6
- parcel_offset: float32 [3, 4194304], P(None, ('axial', 'radial')), may hold values from 0 to 1
- parcel_cell: int32 [4194304], P(('axial', 'radial')), may hold values from 0 to 63
- cross_rows: int32 [2, 2097152], P(None, ('axial', 'radial')), may hold values from -1 to 16383, as said below
- block_brick: int32 [65536], P(('axial', 'radial')), may hold values from 0 to 1023
- gas: float32 [5, 512, 128, 256], P(None, 'axial', 'radial'), may hold values from -6 to 6
Outputs:
- source: float32 [5, 512, 128, 256], P(None, 'axial', 'radial')
- parcel_gas: bfloat16 [5, 8388608], P(None, ('axial', 'radial'))
The draws below stay inside these ranges and needn't reach their ends.
Inputs may be any that keep to these rules, and one draw needn't show every extreme that they name: `cross_rows`: on each half slab the non-empty entries of a list come first, and all rows named in both lists are distinct; the upward lists of some half slabs are full with 8192 rows in every draw.
All inputs are finite; a program needn't handle non-finite values.
Results may differ from the reference program's by a relative error of at most 0.001.
Values sent between devices are 32-bit elements; how exact they have to be, the bound alone decides.
A program may use at most 64 MiB of HBM per device.

```python
import jax
import jax.numpy as jnp
from jax import lax

CX = 4
CY = 64
CZ = 256
PAR_DEV = 16384
MIG = 8192
NX = 512
NY = 128
BLK_DEV = 256
BRICKS_DEV = 1024
PARCELS = 4194304
N_AXIAL = 128
DEVICES = 256


def draw_cross_rows(key, part):
    device_keys = jax.random.split(jax.random.fold_in(key, 11), DEVICES)

    def choose_rows(device_key):
        return jax.random.permutation(device_key, PAR_DEV)[:2 * MIG]
    chosen = jax.vmap(choose_rows)(device_keys).astype(jnp.int32).reshape(DEVICES, 2, MIG)
    axial_index = jnp.arange(DEVICES, dtype=jnp.int32) // (DEVICES // N_AXIAL)
    low_count = jax.random.randint(jax.random.fold_in(key, 12), (DEVICES,), MIG // 8, MIG // 4 + 1)
    up_count = jnp.where(axial_index < max(N_AXIAL // 8, 1), MIG, low_count)
    down_count = jax.random.randint(jax.random.fold_in(key, 13), (DEVICES,), MIG // 8, MIG // 4 + 1)
    slot_index = jnp.arange(MIG, dtype=jnp.int32)[None, :]
    upward = jnp.where(slot_index < up_count[:, None], chosen[:, 0], -1)
    downward = jnp.where(slot_index < down_count[:, None], chosen[:, 1], -1)
    return jnp.stack([upward, downward], 0).reshape(2, DEVICES * MIG).astype(jnp.int32)


def place_ends(values, rng, low, high):
    longest = values.shape.index(max(values.shape))
    spots = []
    for shift in (0, 1):
        where = [jax.random.randint(jax.random.fold_in(rng, axis), (), 0, length) for axis, length in enumerate(values.shape)]
        where[longest] = (where[longest] + shift) % values.shape[longest]
        spots.append(tuple(where))
    return values.at[spots[0]].set(low).at[spots[1]].set(high)


def block_levels(own_key, shape, shards, least, top_value):
    gain = 1.0
    for position, parts in shards:
        draws = jax.random.uniform(jax.random.fold_in(jax.random.fold_in(own_key, 6), position), (parts,), jnp.float32, least / len(shards), top_value / len(shards))
        gain = gain * jnp.repeat(jnp.exp(draws), shape[position] // parts).reshape((-1,) + (1,) * (len(shape) - 1 - position))
    return gain


def normal_values(key, dims, width, bound, cuts=(), kind=jnp.bfloat16):
    entries = jax.random.normal(key, dims, jnp.float32) * width
    if len(cuts) > 0:
        entries = block_levels(key, dims, cuts, -0.22, 0.18) * entries
    return jnp.clip(entries, min=-bound, max=bound).astype(kind)


def setup_inputs(seed: int = 0) -> dict:
    keys = jax.random.split(jax.random.key(seed), 7)
    parcel_load = normal_values(keys[0], (5, PARCELS), 1.0, 6.0, ((1, 256),), jnp.float32)
    parcel_offset = jnp.clip(1.0 * jax.random.uniform(keys[1], (3, PARCELS), jnp.float32) ** block_levels(keys[1], (3, PARCELS), ((1, 256),), -0.2, 0.2), 0.0, 1.0)
    parcel_cell = place_ends(jax.random.randint(keys[2], (PARCELS,), 0, 64), jax.random.fold_in(keys[2], 1), 0, 63).astype(jnp.int32)
    cross_rows = draw_cross_rows(jax.random.fold_in(keys[6], 71), 0)
    block_brick = place_ends(jax.random.randint(keys[4], (BLK_DEV * DEVICES,), 0, BRICKS_DEV), jax.random.fold_in(keys[4], 1), 0, BRICKS_DEV - 1).astype(jnp.int32)
    gas = normal_values(keys[5], (5, NX, NY, CZ), 1.0, 6.0, ((1, 128), (2, 2)), jnp.float32)
    return {"parcel_load": parcel_load, "parcel_offset": parcel_offset, "parcel_cell": parcel_cell, "cross_rows": cross_rows, "block_brick": block_brick, "gas": gas}


COUPLE = 0.5


def kernel_weights(cell_index, offsets):
    extent = jnp.arange(128, dtype=jnp.int32)
    brick_x = extent // 25
    brick_y = (extent // 5) % 5
    brick_z = extent % 5
    inside = (extent < 125).astype(jnp.float32)

    def factor(cell_coord, brick_coord, fraction):
        cell_coord = cell_coord[:, :, None]
        fraction = fraction[:, :, None]
        return jnp.where(brick_coord == cell_coord, 1.0 - fraction, jnp.where(brick_coord == cell_coord + 1, fraction, 0.0))

    cell_x = cell_index // 16
    cell_y = (cell_index // 4) % 4
    cell_z = cell_index % 4
    return factor(cell_x, brick_x, offsets[0]) * factor(cell_y, brick_y, offsets[1]) * factor(cell_z, brick_z, offsets[2]) * inside


def brick_index(brick_ids, span_y, span_z):
    row_bricks = span_z // 4
    plane_bricks = (span_y // 4) * row_bricks
    slab_x = brick_ids // plane_bricks
    slab_y = (brick_ids // row_bricks) % (span_y // 4)
    slab_z = brick_ids % row_bricks
    extent = jnp.arange(128, dtype=jnp.int32)
    coord_x = 4 * slab_x[:, None] + extent // 25
    coord_y = 4 * slab_y[:, None] + (extent // 5) % 5
    coord_z = 4 * slab_z[:, None] + extent % 5
    inside = (extent < 125) & (coord_z < span_z)
    flat_index = (coord_x * (span_y + 1) + coord_y) * span_z + coord_z
    return flat_index, inside


def deposit_blocks(parcel_part, brick_ids, span_y, span_z, deposit_grid):
    block_count = brick_ids.shape[0]
    block_rows = parcel_part.reshape(9, block_count, 128)
    weights = kernel_weights(block_rows[8].astype(jnp.int32), block_rows[5:8])
    spread = jnp.einsum("fgp,gpe->fge", block_rows[:5], weights, precision=lax.Precision.HIGHEST)
    flat_index, inside = brick_index(brick_ids, span_y, span_z)
    target_rows = jnp.where(inside, flat_index, deposit_grid.shape[1])
    return deposit_grid.at[:, target_rows.reshape(-1)].add(spread.reshape(5, -1), mode="drop")


def sample_blocks(parcel_part, brick_ids, span_y, span_z, gas_field):
    block_count = brick_ids.shape[0]
    block_rows = parcel_part.reshape(9, block_count, 128)
    weights = kernel_weights(block_rows[8].astype(jnp.int32), block_rows[5:8])
    flat_index, inside = brick_index(brick_ids, span_y, span_z)
    picked = gas_field[:, jnp.where(inside, flat_index, 0)] * inside.astype(jnp.float32)
    values = jnp.einsum("fge,gpe->fgp", picked, weights, precision=lax.Precision.HIGHEST)
    return values.reshape(5, block_count * 128)


def reference(parcel_load, parcel_offset, parcel_cell, cross_rows, block_brick, gas):
    device_count = DEVICES
    radial_count = DEVICES // N_AXIAL
    rows_total = PAR_DEV + 2 * MIG
    attributes = jnp.concatenate([parcel_load, parcel_offset, parcel_cell[None].astype(jnp.float32)], 0).reshape(9, device_count, PAR_DEV)
    row_lists = cross_rows.reshape(2, device_count, MIG)
    usable = row_lists >= 0
    safe_rows = jnp.maximum(row_lists, 0)
    upward = jnp.take_along_axis(attributes, safe_rows[0][None], axis=2) * usable[0][None].astype(jnp.float32)
    downward = jnp.take_along_axis(attributes, safe_rows[1][None], axis=2) * usable[1][None].astype(jnp.float32)
    hollow = jnp.zeros((9, radial_count, MIG), jnp.float32)
    from_lower = jnp.concatenate([hollow, upward[:, :device_count - radial_count]], 1)
    from_upper = jnp.concatenate([downward[:, radial_count:], hollow], 1)
    target_rows = jnp.where(usable, row_lists, PAR_DEV)
    owner_rows = jnp.broadcast_to(jnp.arange(device_count, dtype=jnp.int32)[:, None], (device_count, MIG))
    departed = jnp.zeros((device_count, PAR_DEV), jnp.float32)
    departed = departed.at[owner_rows, target_rows[0]].set(1.0, mode="drop")
    departed = departed.at[owner_rows, target_rows[1]].set(1.0, mode="drop")
    staying = jnp.concatenate([attributes[:8] * (1.0 - departed)[None], attributes[8:]], 0)
    parcels = jnp.concatenate([staying, from_lower, from_upper], 2)
    stacked = jnp.transpose(parcels, (1, 0, 2))
    brick_table = block_brick.reshape(device_count, rows_total // 128)
    device_ids = jnp.arange(device_count, dtype=jnp.int32)
    anchor = jnp.zeros((), jnp.int32)

    def deposit_device(accumulated, device_item):
        device_index, parcel_part, brick_ids = device_item
        local_grid = deposit_blocks(parcel_part, brick_ids, CY, CZ, jnp.zeros((5, (CX + 1) * (CY + 1) * CZ), jnp.float32))
        local_grid = local_grid.reshape(5, CX + 1, CY + 1, CZ)
        corner = (anchor, (device_index // radial_count) * CX, (device_index % radial_count) * CY, anchor)
        window = lax.dynamic_slice(accumulated, corner, (5, CX + 1, CY + 1, CZ))
        return lax.dynamic_update_slice(accumulated, window + local_grid, corner), None

    accumulated = jnp.zeros((5, NX + 1, NY + 1, CZ), jnp.float32)
    accumulated, _ = lax.scan(deposit_device, accumulated, (device_ids, stacked, brick_table))
    source = accumulated[:, :NX, :NY, :]
    updated_gas = gas + COUPLE * source
    padded = jnp.pad(updated_gas, ((0, 0), (0, 1), (0, 1), (0, 0)))

    def sample_device(device_item):
        device_index, parcel_part, brick_ids = device_item
        corner = (anchor, (device_index // radial_count) * CX, (device_index % radial_count) * CY, anchor)
        gas_field = lax.dynamic_slice(padded, corner, (5, CX + 1, CY + 1, CZ)).reshape(5, -1)
        return sample_blocks(parcel_part, brick_ids, CY, CZ, gas_field)

    sampled = lax.map(sample_device, (device_ids, stacked, brick_table))
    parcel_gas = jnp.transpose(sampled, (1, 0, 2)).reshape(5, device_count * rows_total).astype(jnp.bfloat16)
    return (source, parcel_gas)
```

```python
import functools

import jax
import jax.numpy as jnp
from jax import lax
from jax.experimental import pallas as pl
from jax.experimental.pallas import tpu as pltpu
from jax.sharding import PartitionSpec as P

COUPLE = 0.5
LANES = 128
TILE = 256
FIELDS = 5
GROUP = 6
SPAN = 4 * GROUP
NT = (((1,), (1,)), ((), ()))
F32 = jnp.float32
BF16 = jnp.bfloat16


def split(x):
    high = x.astype(BF16).astype(F32)
    return high, x - high


def hat(x):
    return jnp.maximum(1.0 - jnp.abs(x), 0.0)


def row_numbers(shape):
    return lax.broadcasted_iota(jnp.int32, shape, 0)


def gather_kernel(load, offset, cell, rows, up, down, stay, table, base, corner, gone):
    count = load.shape[1]
    blocks = count // LANES
    slots = rows.shape[1]
    axis_row = row_numbers((3, count))
    coords = lax.shift_right_logical(
        jnp.broadcast_to(cell[...], (3, count)), 4 - 2 * axis_row
    ) & 3
    corner[...] = jnp.concatenate([jnp.zeros((5, count), F32), coords.astype(F32)], 0)
    base[...] = jnp.concatenate([load[...], offset[...]], 0)

    def fill(step, carry):
        at = pl.multiple_of(step * 2 * LANES, 2 * LANES)
        pair = base[:, pl.ds(at, 2 * LANES)] + corner[:, pl.ds(at, 2 * LANES)]
        both = jnp.concatenate([pair[:, :LANES], pair[:, LANES:]], 0)
        high, low = split(both)
        place = pl.multiple_of(step * 16, 16)
        table[pl.ds(place, 16), :] = jnp.concatenate([high, low], 1).astype(BF16)
        return carry

    lax.fori_loop(0, blocks // 2, fill, 0, unroll=8)
    gone[...] = jnp.zeros_like(gone)

    for side, out in ((0, up), (1, down)):
        out[...] = jnp.zeros_like(out)
        named = jnp.sum((rows[side : side + 1, :] >= 0).astype(F32)).astype(jnp.int32)

        def tile_step(step, carry, side=side, out=out):
            at = pl.multiple_of(step * TILE, TILE)
            row = rows[side : side + 1, pl.ds(at, TILE)]
            lane = row & (LANES - 1)
            block = lax.shift_right_arithmetic(row, 7)
            number = row_numbers((LANES, TILE))
            lane_hot = jnp.where(number == lane, 1.0, 0.0).astype(BF16)
            block_hot = jnp.where(number == block, 1.0, 0.0).astype(BF16)
            gone[...] += lax.dot_general(block_hot, lane_hot, NT, preferred_element_type=F32)
            wanted = jnp.concatenate([lane_hot, lane_hot], 0)
            block8 = jnp.broadcast_to(block, (8, TILE))
            found = jnp.zeros((8, TILE), F32)
            for chunk in range(blocks // 16):
                part = jnp.dot(
                    table[chunk * 128 : chunk * 128 + 128, :], wanted,
                    preferred_element_type=F32,
                )
                for i in range(16):
                    found = jnp.where(
                        block8 == chunk * 16 + i, part[8 * i : 8 * i + 8, :], found
                    )
            out[:, pl.ds(at, TILE)] = found
            return carry

        lax.fori_loop(0, (named + TILE - 1) // TILE, tile_step, 0)

    def keep(step, carry):
        at = pl.multiple_of(step * LANES, LANES)
        left = 1.0 - gone[pl.ds(step, 1), :]
        stay[:, pl.ds(at, LANES)] = (
            base[:, pl.ds(at, LANES)] * left + corner[:, pl.ds(at, LANES)]
        )
        return carry

    lax.fori_loop(0, blocks, keep, 0, unroll=8)


def gather_call(load, offset, cell, rows):
    count = load.shape[1]
    slots = rows.shape[1]
    moved = jax.ShapeDtypeStruct((8, slots), F32)
    return pl.pallas_call(
        gather_kernel,
        out_shape=(moved, moved, jax.ShapeDtypeStruct((8, count), F32)),
        scratch_shapes=[
            pltpu.VMEM((8 * (count // LANES), 2 * LANES), BF16),
            pltpu.VMEM((8, count), F32),
            pltpu.VMEM((8, count), F32),
            pltpu.VMEM((count // LANES, LANES), F32),
        ],
        compiler_params=pltpu.CompilerParams(vmem_limit_bytes=24 * 2**20),
        name="gather_rows",
    )(load, offset, cell.reshape(1, count), rows)


class Grid:
    def __init__(self, span_y, span_z):
        self.span_y = span_y
        self.span_z = span_z
        self.per_row = span_z // 4
        self.bricks_y = span_y // 4
        self.groups = -(-self.bricks_y // GROUP)
        self.rows_z = span_z + 8
        self.rows = self.groups * FIELDS * self.rows_z
        self.pad_y = self.groups * SPAN

    def place(self, brick):
        z = brick % self.per_row
        y = (brick // self.per_row) % self.bricks_y
        group = y // GROUP
        first = group * (FIELDS * self.rows_z) + 4 * z
        return first, (4 * (y - group * GROUP)).astype(F32)


def plane_weights(block, shift_y):
    number = row_numbers((8, LANES)).astype(F32)
    x = hat(number - block[5:6])
    y = block[6:7] + shift_y
    parts = [hat(number + 8.0 * k - y) for k in range(SPAN // 8)]
    last = hat(float(SPAN) - y)
    pieces = [x[i : i + 1] * part for i in range(5) for part in parts]
    return split(jnp.concatenate(pieces + [x * last], 0))


def depth_weights(block):
    return hat(row_numbers((8, LANES)).astype(F32) - block[7:8])


def doubled(x):
    high, low = split(x)
    both = jnp.concatenate([high, low], 0).astype(BF16)
    return jnp.concatenate([both, both], 1)


def deposit_block(grid, block, brick, total):
    first, shift_y = grid.place(brick)
    high, low = plane_weights(block, shift_y)
    plane = jnp.concatenate([high.astype(BF16), low.astype(BF16)], 1)
    depth = depth_weights(block)
    loads = jnp.concatenate([block[f : f + 1] * depth for f in range(FIELDS)], 0)
    both = lax.dot_general(doubled(loads), plane, NT, preferred_element_type=F32)
    summed = both[: 8 * FIELDS] + both[8 * FIELDS :]
    for f in range(FIELDS):
        rows = pl.ds(first + f * grid.rows_z, 8)
        total[rows, :] += summed[8 * f : 8 * f + 8]


def sample_block(grid, block, brick, held):
    first, shift_y = grid.place(brick)
    high, low = plane_weights(block, shift_y)
    plane = jnp.concatenate([high.astype(BF16), low.astype(BF16)], 0)
    fields = jnp.concatenate(
        [held[pl.ds(first + f * grid.rows_z, 8), :] for f in range(FIELDS)], 0
    )
    both = jnp.dot(doubled(fields), plane, preferred_element_type=F32)
    summed = both[: 8 * FIELDS] + both[8 * FIELDS :]
    depth = depth_weights(block)
    return jnp.concatenate(
        [
            jnp.sum(summed[8 * f : 8 * f + 8] * depth, axis=0, keepdims=True)
            for f in range(FIELDS)
        ],
        0,
    )


UNROLL = 4


def deposit_loop(grid, parcels, bricks, offset, count, total):
    def step(turn, carry):
        for i in range(UNROLL):
            at = turn * UNROLL + i
            block = parcels[:, pl.ds(pl.multiple_of(at * LANES, LANES), LANES)]
            deposit_block(grid, block, bricks[offset + at], total)
        return carry

    lax.fori_loop(0, count // UNROLL, step, 0)


def deposit_stay_kernel(grid, bricks, parcels, total):
    total[...] = jnp.zeros_like(total)
    deposit_loop(grid, parcels, bricks, 0, parcels.shape[1] // LANES, total)


def deposit_moved_kernel(
    grid, bricks, place, lower, upper, held, gas, sums, up, down, row, total
):
    total[...] = held[...]
    blocks = lower.shape[1] // LANES
    start = bricks.shape[0] - 2 * blocks
    deposit_loop(grid, lower, bricks, start, blocks, total)
    deposit_loop(grid, upper, bricks, start + blocks, blocks, total)
    picked = row_numbers((160, LANES))
    lane = lax.broadcasted_iota(jnp.int32, (160, LANES), 1)
    edge = picked - 5 * SPAN
    wanted = jnp.where(
        picked < 5 * SPAN, picked, jnp.where(edge % 8 == 0, 5 * SPAN + edge // 8, -1)
    )
    select = jnp.where(lane == wanted, 1.0, 0.0).astype(BF16)
    select = jnp.concatenate([select, select], 1)
    for f in range(FIELDS):
        carried = None
        for group in range(grid.groups):
            first = (group * FIELDS + f) * grid.rows_z
            high, low = split(total[first : first + grid.span_z, :])
            both = jnp.concatenate([high.astype(BF16), low.astype(BF16)], 1)
            turned = lax.dot_general(select, both, NT, preferred_element_type=F32)
            for x in range(5):
                piece = turned[x * SPAN : (x + 1) * SPAN]
                if carried is not None:
                    head = piece[:8] + carried[8 * x : 8 * x + 8]
                    piece = jnp.concatenate([head, piece[8:]], 0)
                sums[f, x, group * SPAN : (group + 1) * SPAN, :] = piece
            carried = turned[5 * SPAN :]
    second_half = place[1] == 1
    ny = grid.span_y
    for f in range(FIELDS):
        up[f] = sums[f, 4]
        down[f, :ny] = COUPLE * sums[f, 0, :ny] + gas[f, 0]
        down[f, ny:] = COUPLE * sums[f, 0, ny:]
        for x in range(5):
            low_row = COUPLE * sums[f, x, 0:1, :]
            if x < 4:
                low_row = low_row + gas[f, x, 0:1, :]
            high_row = COUPLE * sums[f, x, ny : ny + 1, :]
            row[x, f : f + 1, :] = jnp.where(second_half, low_row, high_row)
    for x in range(5):
        row[x, FIELDS:, :] = jnp.zeros((8 - FIELDS, grid.span_z), F32)


def sample_kernel(
    grid, last, bricks, place, stay, lower, upper, gas, sums, from_up, from_down,
    from_row, corner_low, corner_high, source, sampled, field, held
):
    ny = grid.span_y
    second_half = place[1] == 1
    at_end = place[0] == last
    face = jnp.where(second_half, 1.0, 0.0)
    for f in range(FIELDS):
        for x in range(5):
            extra = from_row[x, f : f + 1, :]
            if x == 0:
                extra = extra + corner_low[f : f + 1, :]
            if x == 4:
                extra = extra + corner_high[f : f + 1, :]
            first = row_numbers((8, grid.span_z)) == 0
            head = jnp.where(first, 2.0 * face * extra, 0.0)
            mine = sums[f, x, :ny, :]
            if x == 0:
                mine = mine + from_up[f, :ny, :]
            mine = jnp.concatenate([mine[:8] + head, mine[8:]], 0)
            tail = COUPLE * sums[f, x, ny : ny + 8, :]
            if x == 0:
                tail = tail + COUPLE * from_up[f, ny : ny + 8, :]
            if x < 4:
                source[f, x] = mine
                mine = gas[f, x] + COUPLE * mine
            else:
                mine = COUPLE * mine + from_down[f, :ny, :]
                mine = jnp.where(at_end, 0.0, mine)
                tail = tail + from_down[f, ny : ny + 8, :]
                tail = jnp.where(at_end, 0.0, tail)
                extra = jnp.where(at_end, 0.0, extra)
            tail = jnp.where(first & jnp.logical_not(second_half), tail + extra, 0.0)
            field[f, x, :ny, :] = mine
            field[f, x, ny : ny + 8, :] = tail
    for f in range(FIELDS):
        for group in range(grid.groups):
            edge = SPAN * (group + 1)
            pieces = [field[f, x, edge - SPAN : edge, :] for x in range(5)]
            if edge < grid.pad_y:
                pieces += [field[f, x, edge : edge + 1, :] for x in range(5)]
                pieces.append(jnp.zeros((3, grid.span_z), F32))
            else:
                pieces.append(jnp.zeros((8, grid.span_z), F32))
            turned = jnp.concatenate(pieces, 0).T
            at = (group * FIELDS + f) * grid.rows_z
            held[at : at + grid.span_z, :] = turned
            held[at + grid.span_z : at + grid.rows_z, :] = jnp.zeros((8, LANES), F32)

    offset = 0
    for part in (stay, lower, upper):
        blocks = part.shape[1] // LANES

        def step(turn, carry, part=part, offset=offset):
            for i in range(UNROLL):
                at = turn * UNROLL + i
                block = part[:, pl.ds(pl.multiple_of(at * LANES, LANES), LANES)]
                values = sample_block(grid, block, bricks[offset + at], held)
                lanes = pl.ds(pl.multiple_of((offset + at) * LANES, LANES), LANES)
                sampled[:, lanes] = values.astype(BF16)
            return carry

        lax.fori_loop(0, blocks // UNROLL, step, 0)
        offset += blocks


SMEM = pl.BlockSpec(memory_space=pltpu.SMEM)
VMEM = pl.BlockSpec(memory_space=pltpu.VMEM)


def shift(block, route):
    return lax.ppermute(block, ("axial", "radial"), route)


def per_device(load, offset, cell, rows, bricks, gas):
    axial = lax.axis_size("axial")
    radial = lax.axis_size("radial")
    span_y, span_z = gas.shape[2], gas.shape[3]
    grid = Grid(span_y, span_z)
    place = jnp.stack([lax.axis_index("axial"), lax.axis_index("radial")]).astype(jnp.int32)
    everyone = [(a, r) for a in range(axial) for r in range(radial)]

    def route(step_a, flip):
        return [
            (a * radial + r, (a + step_a) * radial + (radial - 1 - r if flip else r))
            for a, r in everyone
            if 0 <= a + step_a < axial
        ]

    up, down, stay = gather_call(load, offset, cell, rows)
    lower = shift(up, route(1, False))
    upper = shift(down, route(-1, False))
    big = pltpu.CompilerParams(vmem_limit_bytes=40 * 2**20)
    total = jax.ShapeDtypeStruct((grid.rows, LANES), F32)
    held = pl.pallas_call(
        functools.partial(deposit_stay_kernel, grid),
        out_shape=total,
        in_specs=[SMEM, VMEM],
        compiler_params=big,
        cost_estimate=pl.CostEstimate(flops=10**9, bytes_accessed=10**7, transcendentals=0),
        name="deposit_stay",
    )(bricks, stay)
    plane = jax.ShapeDtypeStruct((FIELDS, grid.pad_y, span_z), F32)
    sums, plane_up, plane_down, edge = pl.pallas_call(
        functools.partial(deposit_moved_kernel, grid),
        out_shape=(
            jax.ShapeDtypeStruct((FIELDS, 5, grid.pad_y, span_z), F32),
            plane,
            plane,
            jax.ShapeDtypeStruct((5, 8, span_z), F32),
        ),
        in_specs=[SMEM, SMEM, VMEM, VMEM, VMEM, VMEM],
        scratch_shapes=[pltpu.VMEM((grid.rows, LANES), F32)],
        compiler_params=big,
        name="deposit_moved",
    )(bricks, place, lower, upper, held, gas)
    from_up = shift(plane_up, route(1, False))
    from_down = shift(plane_down, route(-1, False))
    from_row = shift(edge, route(0, True))
    corner_low = shift(edge[4], route(1, True))
    corner_high = shift(edge[0], route(-1, True))
    return pl.pallas_call(
        functools.partial(sample_kernel, grid, axial - 1),
        out_shape=(
            jax.ShapeDtypeStruct(gas.shape, F32),
            jax.ShapeDtypeStruct((FIELDS, bricks.shape[0] * LANES), BF16),
        ),
        in_specs=[SMEM, SMEM] + [VMEM] * 10,
        scratch_shapes=[
            pltpu.VMEM((FIELDS, 5, grid.pad_y, span_z), F32),
            pltpu.VMEM((grid.rows, LANES), F32),
        ],
        compiler_params=big,
        name="sample",
    )(
        bricks, place, stay, lower, upper, gas, sums, from_up, from_down, from_row,
        corner_low, corner_high,
    )


def solution(mesh):
    return jax.shard_map(
        per_device,
        mesh=mesh,
        in_specs=(
            P(None, ("axial", "radial")),
            P(None, ("axial", "radial")),
            P(("axial", "radial")),
            P(None, ("axial", "radial")),
            P(("axial", "radial")),
            P(None, "axial", "radial", None),
        ),
        out_specs=(P(None, "axial", "radial", None), P(None, ("axial", "radial"))),
        check_vma=False,
    )
```

```python
import functools

import jax
import jax.numpy as jnp
from jax import lax
from jax.experimental import pallas as pl
from jax.experimental.pallas import tpu as pltpu
from jax.sharding import PartitionSpec as P

COUPLE = 0.5
LANES = 128
TILE = 2048
CHUNK = 32
FIELDS = 5
GROUP = 6
SPAN = 4 * GROUP
NT = (((1,), (1,)), ((), ()))
F32 = jnp.float32
BF16 = jnp.bfloat16


def split(x):
    high = x.astype(BF16).astype(F32)
    return high, x - high


def hat(x):
    return jnp.maximum(1.0 - jnp.abs(x), 0.0)


def row_numbers(shape):
    return lax.broadcasted_iota(jnp.int32, shape, 0)


def gather_kernel(load, offset, cell, rows, up, down, stay, table, base, corner, gone):
    count = load.shape[1]
    blocks = count // LANES
    slots = rows.shape[1]
    axis_row = row_numbers((3, count))
    coords = lax.shift_right_logical(
        jnp.broadcast_to(cell[...], (3, count)), 4 - 2 * axis_row
    ) & 3
    corner[...] = jnp.concatenate([jnp.zeros((5, count), F32), coords.astype(F32)], 0)
    base[...] = jnp.concatenate([load[...], offset[...]], 0)

    def fill(step, carry):
        at = pl.multiple_of(step * 2 * LANES, 2 * LANES)
        pair = base[:, pl.ds(at, 2 * LANES)] + corner[:, pl.ds(at, 2 * LANES)]
        both = jnp.concatenate([pair[:, :LANES], pair[:, LANES:]], 0)
        high, low = split(both)
        place = pl.multiple_of(step * 16, 16)
        table[pl.ds(place, 16), :] = jnp.concatenate([high, low], 1).astype(BF16)
        return carry

    lax.fori_loop(0, blocks // 2, fill, 0, unroll=8)
    gone[...] = jnp.zeros_like(gone)

    for side, out in ((0, up), (1, down)):
        out[...] = jnp.zeros_like(out)
        named = jnp.sum((rows[side : side + 1, :] >= 0).astype(F32)).astype(jnp.int32)

        def tile_step(step, carry, side=side, out=out):
            at = pl.multiple_of(step * TILE, TILE)
            row = rows[side : side + 1, pl.ds(at, TILE)]
            lane = row & (LANES - 1)
            block = lax.shift_right_arithmetic(row, 7)
            number = row_numbers((LANES, TILE))
            lane_hot = jnp.where(number == lane, 1.0, 0.0).astype(BF16)
            block_hot = jnp.where(number == block, 1.0, 0.0).astype(BF16)
            gone[...] += lax.dot_general(block_hot, lane_hot, NT, preferred_element_type=F32)
            wanted = jnp.concatenate([lane_hot, lane_hot], 0)
            block8 = jnp.broadcast_to(block, (8, TILE))
            found = jnp.zeros((8, TILE), F32)
            for chunk in range(blocks // CHUNK):
                part = jnp.dot(
                    table[8 * CHUNK * chunk : 8 * CHUNK * (chunk + 1), :], wanted,
                    preferred_element_type=F32,
                )
                for i in range(CHUNK):
                    found = jnp.where(
                        block8 == chunk * CHUNK + i, part[8 * i : 8 * i + 8, :], found
                    )
            out[:, pl.ds(at, TILE)] = found
            return carry

        lax.fori_loop(0, (named + TILE - 1) // TILE, tile_step, 0)

    def keep(step, carry):
        at = pl.multiple_of(step * LANES, LANES)
        left = 1.0 - gone[pl.ds(step, 1), :]
        stay[:, pl.ds(at, LANES)] = (
            base[:, pl.ds(at, LANES)] * left + corner[:, pl.ds(at, LANES)]
        )
        return carry

    lax.fori_loop(0, blocks, keep, 0, unroll=8)


def gather_call(load, offset, cell, rows):
    count = load.shape[1]
    slots = rows.shape[1]
    moved = jax.ShapeDtypeStruct((8, slots), F32)
    return pl.pallas_call(
        gather_kernel,
        out_shape=(moved, moved, jax.ShapeDtypeStruct((8, count), F32)),
        scratch_shapes=[
            pltpu.VMEM((8 * (count // LANES), 2 * LANES), BF16),
            pltpu.VMEM((8, count), F32),
            pltpu.VMEM((8, count), F32),
            pltpu.VMEM((count // LANES, LANES), F32),
        ],
        compiler_params=pltpu.CompilerParams(vmem_limit_bytes=24 * 2**20),
        name="gather_rows",
    )(load, offset, cell.reshape(1, count), rows)


class Grid:
    def __init__(self, span_y, span_z):
        self.span_y = span_y
        self.span_z = span_z
        self.per_row = span_z // 4
        self.bricks_y = span_y // 4
        self.groups = -(-self.bricks_y // GROUP)
        self.rows_z = span_z + 8
        self.rows = self.groups * FIELDS * self.rows_z
        self.pad_y = self.groups * SPAN

    def place(self, brick):
        z = brick % self.per_row
        y = (brick // self.per_row) % self.bricks_y
        group = y // GROUP
        first = group * (FIELDS * self.rows_z) + 4 * z
        return first, (4 * (y - group * GROUP)).astype(F32)


def plane_weights(block, shift_y):
    number = row_numbers((8, LANES)).astype(F32)
    x = hat(number - block[5:6])
    y = block[6:7] + shift_y
    parts = [hat(number + 8.0 * k - y) for k in range(SPAN // 8)]
    last = hat(float(SPAN) - y)
    pieces = [x[i : i + 1] * part for i in range(5) for part in parts]
    return split(jnp.concatenate(pieces + [x * last], 0))


def depth_weights(block):
    return hat(row_numbers((8, LANES)).astype(F32) - block[7:8])


def doubled(x):
    high, low = split(x)
    both = jnp.concatenate([high, low], 0).astype(BF16)
    return jnp.concatenate([both, both], 1)


def deposit_block(grid, block, brick, total):
    first, shift_y = grid.place(brick)
    high, low = plane_weights(block, shift_y)
    plane = jnp.concatenate([high.astype(BF16), low.astype(BF16)], 1)
    depth = depth_weights(block)
    loads = jnp.concatenate([block[f : f + 1] * depth for f in range(FIELDS)], 0)
    both = lax.dot_general(doubled(loads), plane, NT, preferred_element_type=F32)
    summed = both[: 8 * FIELDS] + both[8 * FIELDS :]
    for f in range(FIELDS):
        rows = pl.ds(first + f * grid.rows_z, 8)
        total[rows, :] += summed[8 * f : 8 * f + 8]


def sample_block(grid, block, brick, held):
    first, shift_y = grid.place(brick)
    high, low = plane_weights(block, shift_y)
    plane = jnp.concatenate([high.astype(BF16), low.astype(BF16)], 0)
    fields = jnp.concatenate(
        [held[pl.ds(first + f * grid.rows_z, 8), :] for f in range(FIELDS)], 0
    )
    both = jnp.dot(doubled(fields), plane, preferred_element_type=F32)
    summed = both[: 8 * FIELDS] + both[8 * FIELDS :]
    depth = depth_weights(block)
    return jnp.concatenate(
        [
            jnp.sum(summed[8 * f : 8 * f + 8] * depth, axis=0, keepdims=True)
            for f in range(FIELDS)
        ],
        0,
    )


UNROLL = 32


def deposit_loop(grid, parcels, bricks, offset, count, total):
    def step(turn, carry):
        for i in range(UNROLL):
            at = turn * UNROLL + i
            block = parcels[:, pl.ds(pl.multiple_of(at * LANES, LANES), LANES)]
            deposit_block(grid, block, bricks[offset + at], total)
        return carry

    lax.fori_loop(0, count // UNROLL, step, 0)


def deposit_stay_kernel(grid, bricks, parcels, total):
    total[...] = jnp.zeros_like(total)
    deposit_loop(grid, parcels, bricks, 0, parcels.shape[1] // LANES, total)


def deposit_moved_kernel(
    grid, bricks, place, lower, upper, held, gas, sums, up, down, row, total
):
    total[...] = held[...]
    blocks = lower.shape[1] // LANES
    start = bricks.shape[0] - 2 * blocks
    deposit_loop(grid, lower, bricks, start, blocks, total)
    deposit_loop(grid, upper, bricks, start + blocks, blocks, total)
    picked = row_numbers((160, LANES))
    lane = lax.broadcasted_iota(jnp.int32, (160, LANES), 1)
    edge = picked - 5 * SPAN
    wanted = jnp.where(
        picked < 5 * SPAN, picked, jnp.where(edge % 8 == 0, 5 * SPAN + edge // 8, -1)
    )
    select = jnp.where(lane == wanted, 1.0, 0.0).astype(BF16)
    select = jnp.concatenate([select, select], 1)
    for f in range(FIELDS):
        carried = None
        for group in range(grid.groups):
            first = (group * FIELDS + f) * grid.rows_z
            high, low = split(total[first : first + grid.span_z, :])
            both = jnp.concatenate([high.astype(BF16), low.astype(BF16)], 1)
            turned = lax.dot_general(select, both, NT, preferred_element_type=F32)
            for x in range(5):
                piece = turned[x * SPAN : (x + 1) * SPAN]
                if carried is not None:
                    head = piece[:8] + carried[8 * x : 8 * x + 8]
                    piece = jnp.concatenate([head, piece[8:]], 0)
                sums[f, x, group * SPAN : (group + 1) * SPAN, :] = piece
            carried = turned[5 * SPAN :]
    second_half = place[1] == 1
    ny = grid.span_y
    for f in range(FIELDS):
        up[f] = sums[f, 4]
        down[f, :ny] = COUPLE * sums[f, 0, :ny] + gas[f, 0]
        down[f, ny:] = COUPLE * sums[f, 0, ny:]
        for x in range(5):
            low_row = COUPLE * sums[f, x, 0:1, :]
            if x < 4:
                low_row = low_row + gas[f, x, 0:1, :]
            high_row = COUPLE * sums[f, x, ny : ny + 1, :]
            row[x, f : f + 1, :] = jnp.where(second_half, low_row, high_row)
    for x in range(5):
        row[x, FIELDS:, :] = jnp.zeros((8 - FIELDS, grid.span_z), F32)


def sample_kernel(
    grid, last, bricks, place, stay, lower, upper, gas, sums, from_up, from_down,
    from_row, corner_low, corner_high, source, sampled, field, held
):
    ny = grid.span_y
    second_half = place[1] == 1
    at_end = place[0] == last
    face = jnp.where(second_half, 1.0, 0.0)
    for f in range(FIELDS):
        for x in range(5):
            extra = from_row[x, f : f + 1, :]
            if x == 0:
                extra = extra + corner_low[f : f + 1, :]
            if x == 4:
                extra = extra + corner_high[f : f + 1, :]
            first = row_numbers((8, grid.span_z)) == 0
            head = jnp.where(first, 2.0 * face * extra, 0.0)
            mine = sums[f, x, :ny, :]
            if x == 0:
                mine = mine + from_up[f, :ny, :]
            mine = jnp.concatenate([mine[:8] + head, mine[8:]], 0)
            tail = COUPLE * sums[f, x, ny : ny + 8, :]
            if x == 0:
                tail = tail + COUPLE * from_up[f, ny : ny + 8, :]
            if x < 4:
                source[f, x] = mine
                mine = gas[f, x] + COUPLE * mine
            else:
                mine = COUPLE * mine + from_down[f, :ny, :]
                mine = jnp.where(at_end, 0.0, mine)
                tail = tail + from_down[f, ny : ny + 8, :]
                tail = jnp.where(at_end, 0.0, tail)
                extra = jnp.where(at_end, 0.0, extra)
            tail = jnp.where(first & jnp.logical_not(second_half), tail + extra, 0.0)
            field[f, x, :ny, :] = mine
            field[f, x, ny : ny + 8, :] = tail
    for f in range(FIELDS):
        for group in range(grid.groups):
            edge = SPAN * (group + 1)
            pieces = [field[f, x, edge - SPAN : edge, :] for x in range(5)]
            if edge < grid.pad_y:
                pieces += [field[f, x, edge : edge + 1, :] for x in range(5)]
                pieces.append(jnp.zeros((3, grid.span_z), F32))
            else:
                pieces.append(jnp.zeros((8, grid.span_z), F32))
            turned = jnp.concatenate(pieces, 0).T
            at = (group * FIELDS + f) * grid.rows_z
            held[at : at + grid.span_z, :] = turned
            held[at + grid.span_z : at + grid.rows_z, :] = jnp.zeros((8, LANES), F32)

    offset = 0
    for part in (stay, lower, upper):
        blocks = part.shape[1] // LANES

        def step(turn, carry, part=part, offset=offset):
            for i in range(UNROLL):
                at = turn * UNROLL + i
                block = part[:, pl.ds(pl.multiple_of(at * LANES, LANES), LANES)]
                values = sample_block(grid, block, bricks[offset + at], held)
                lanes = pl.ds(pl.multiple_of((offset + at) * LANES, LANES), LANES)
                sampled[:, lanes] = values.astype(BF16)
            return carry

        lax.fori_loop(0, blocks // UNROLL, step, 0)
        offset += blocks


SMEM = pl.BlockSpec(memory_space=pltpu.SMEM)
VMEM = pl.BlockSpec(memory_space=pltpu.VMEM)


def shift(block, route):
    return lax.ppermute(block, ("axial", "radial"), route)


BIG = pltpu.CompilerParams(vmem_limit_bytes=24 * 2**20)


def deposit_stay_call(grid, bricks, stay):
    return pl.pallas_call(
        functools.partial(deposit_stay_kernel, grid),
        out_shape=jax.ShapeDtypeStruct((grid.rows, LANES), F32),
        in_specs=[SMEM, VMEM],
        compiler_params=BIG,
        cost_estimate=pl.CostEstimate(flops=10**9, bytes_accessed=10**7, transcendentals=0),
        name="deposit_stay",
    )(bricks, stay)


def deposit_moved_call(grid, bricks, place, lower, upper, held, gas):
    plane = jax.ShapeDtypeStruct((FIELDS, grid.pad_y, grid.span_z), F32)
    return pl.pallas_call(
        functools.partial(deposit_moved_kernel, grid),
        out_shape=(
            jax.ShapeDtypeStruct((FIELDS, 5, grid.pad_y, grid.span_z), F32),
            plane,
            plane,
            jax.ShapeDtypeStruct((5, 8, grid.span_z), F32),
        ),
        in_specs=[SMEM, SMEM, VMEM, VMEM, VMEM, VMEM],
        scratch_shapes=[pltpu.VMEM((grid.rows, LANES), F32)],
        compiler_params=BIG,
        name="deposit_moved",
    )(bricks, place, lower, upper, held, gas)


def exchange_kernel(
    last, up, down, edge, from_up, from_down, from_row, corner_low, corner_high, sent, got
):
    a = lax.axis_index("axial")
    r = lax.axis_index("radial")
    has_above = a < last
    has_below = a > 0
    barrier = pltpu.get_barrier_semaphore()

    def greet(axial_at, radial_at):
        pl.semaphore_signal(
            barrier, inc=1, device_id=(axial_at, radial_at),
            device_id_type=pl.DeviceIdType.MESH,
        )

    greet(a, 1 - r)

    @pl.when(has_above)
    def _():
        greet(a + 1, r)
        greet(a + 1, 1 - r)

    @pl.when(has_below)
    def _():
        greet(a - 1, r)
        greet(a - 1, 1 - r)

    peers = 1 + 2 * has_above.astype(jnp.int32) + 2 * has_below.astype(jnp.int32)
    pl.semaphore_wait(barrier, peers)

    def copy(number, source, target, axial_at, radial_at):
        return pltpu.make_async_remote_copy(
            src_ref=source, dst_ref=target, send_sem=sent.at[number],
            recv_sem=got.at[number], device_id=(axial_at, radial_at),
            device_id_type=pl.DeviceIdType.MESH,
        )

    row = copy(0, edge, from_row, a, 1 - r)
    above = (
        copy(1, up, from_up, a + 1, r),
        copy(2, edge.at[4], corner_low, a + 1, 1 - r),
    )
    below = (
        copy(3, down, from_down, a - 1, r),
        copy(4, edge.at[0], corner_high, a - 1, 1 - r),
    )

    @pl.when(has_above)
    def _():
        for each in above:
            each.start()

    @pl.when(has_below)
    def _():
        for each in below:
            each.start()

    row.start()

    @pl.when(jnp.logical_not(has_below))
    def _():
        from_up[...] = jnp.zeros_like(from_up)
        corner_low[...] = jnp.zeros_like(corner_low)

    @pl.when(jnp.logical_not(has_above))
    def _():
        from_down[...] = jnp.zeros_like(from_down)
        corner_high[...] = jnp.zeros_like(corner_high)

    row.wait()

    @pl.when(has_above)
    def _():
        for each in above:
            each.wait_send()
        for each in below:
            each.wait_recv()

    @pl.when(has_below)
    def _():
        for each in below:
            each.wait_send()
        for each in above:
            each.wait_recv()


def exchange_call(last, up, down, edge):
    corner = jax.ShapeDtypeStruct(edge.shape[1:], F32)
    return pl.pallas_call(
        functools.partial(exchange_kernel, last),
        out_shape=(
            jax.ShapeDtypeStruct(up.shape, F32),
            jax.ShapeDtypeStruct(down.shape, F32),
            jax.ShapeDtypeStruct(edge.shape, F32),
            corner,
            corner,
        ),
        in_specs=[VMEM] * 3,
        out_specs=(VMEM,) * 5,
        scratch_shapes=[pltpu.SemaphoreType.DMA((5,)), pltpu.SemaphoreType.DMA((5,))],
        compiler_params=pltpu.CompilerParams(
            collective_id=0, has_side_effects=True, vmem_limit_bytes=4 * 2**20
        ),
        name="exchange",
    )(up, down, edge)


def sample_call(grid, last, bricks, place, *arrays):
    gas = arrays[3]
    return pl.pallas_call(
        functools.partial(sample_kernel, grid, last),
        out_shape=(
            jax.ShapeDtypeStruct(gas.shape, F32),
            jax.ShapeDtypeStruct((FIELDS, bricks.shape[0] * LANES), BF16),
        ),
        in_specs=[SMEM, SMEM] + [VMEM] * 10,
        scratch_shapes=[
            pltpu.VMEM((FIELDS, 5, grid.pad_y, grid.span_z), F32),
            pltpu.VMEM((grid.rows, LANES), F32),
        ],
        compiler_params=BIG,
        name="sample",
    )(bricks, place, *arrays)


def per_device(load, offset, cell, rows, bricks, gas):
    axial = lax.axis_size("axial")
    radial = lax.axis_size("radial")
    span_y, span_z = gas.shape[2], gas.shape[3]
    grid = Grid(span_y, span_z)
    place = jnp.stack([lax.axis_index("axial"), lax.axis_index("radial")]).astype(jnp.int32)
    everyone = [(a, r) for a in range(axial) for r in range(radial)]

    def route(step_a, flip):
        return [
            (a * radial + r, (a + step_a) * radial + (radial - 1 - r if flip else r))
            for a, r in everyone
            if 0 <= a + step_a < axial
        ]

    up, down, stay = gather_call(load, offset, cell, rows)
    lower = shift(up, route(1, False))
    upper = shift(down, route(-1, False))
    held = deposit_stay_call(grid, bricks, stay)
    sums, plane_up, plane_down, edge = deposit_moved_call(
        grid, bricks, place, lower, upper, held, gas
    )
    arrived = exchange_call(axial - 1, plane_up, plane_down, edge)
    return sample_call(
        grid, axial - 1, bricks, place, stay, lower, upper, gas, sums, *arrived
    )


def solution(mesh):
    return jax.shard_map(
        per_device,
        mesh=mesh,
        in_specs=(
            P(None, ("axial", "radial")),
            P(None, ("axial", "radial")),
            P(("axial", "radial")),
            P(None, ("axial", "radial")),
            P(("axial", "radial")),
            P(None, "axial", "radial", None),
        ),
        out_specs=(P(None, "axial", "radial", None), P(None, ("axial", "radial"))),
        check_vma=False,
    )
```

```python
import functools

import jax
import jax.numpy as jnp
from jax import lax
from jax.experimental import pallas as pl
from jax.experimental.pallas import tpu as pltpu
from jax.sharding import PartitionSpec as P

COUPLE = 0.5
LANES = 128
TILE = 2048
CHUNK = 32
FIELDS = 5
GROUP = 6
SPAN = 4 * GROUP
NT = (((1,), (1,)), ((), ()))
F32 = jnp.float32
BF16 = jnp.bfloat16


def split(x):
    high = x.astype(BF16).astype(F32)
    return high, x - high


def hat(x):
    return jnp.maximum(1.0 - jnp.abs(x), 0.0)


def row_numbers(shape):
    return lax.broadcasted_iota(jnp.int32, shape, 0)


def gather_kernel(
    load_in, offset_in, cell_in, rows_in, bricks_in, up, down, stay, bricks, load, offset,
    cell, rows, table, base, corner, gone, arrived
):
    pairs = (
        (cell_in, cell), (load_in, load), (offset_in, offset), (rows_in, rows),
        (bricks_in, bricks),
    )
    copies = [
        pltpu.make_async_copy(source, target, arrived.at[i])
        for i, (source, target) in enumerate(pairs)
    ]
    for each in copies:
        each.start()
    for each in copies:
        each.wait()
    count = load.shape[1]
    blocks = count // LANES
    slots = rows.shape[1]
    axis_row = row_numbers((3, count))
    coords = lax.shift_right_logical(
        jnp.broadcast_to(cell[...], (3, count)), 4 - 2 * axis_row
    ) & 3
    corner[...] = jnp.concatenate([jnp.zeros((5, count), F32), coords.astype(F32)], 0)
    base[...] = jnp.concatenate([load[...], offset[...]], 0)

    def fill(step, carry):
        at = pl.multiple_of(step * 2 * LANES, 2 * LANES)
        pair = base[:, pl.ds(at, 2 * LANES)] + corner[:, pl.ds(at, 2 * LANES)]
        both = jnp.concatenate([pair[:, :LANES], pair[:, LANES:]], 0)
        high, low = split(both)
        place = pl.multiple_of(step * 16, 16)
        table[pl.ds(place, 16), :] = jnp.concatenate([high, low], 1).astype(BF16)
        return carry

    lax.fori_loop(0, blocks // 2, fill, 0, unroll=8)
    gone[...] = jnp.zeros_like(gone)

    for side, out in ((0, up), (1, down)):
        out[...] = jnp.zeros_like(out)
        named = jnp.sum((rows[side : side + 1, :] >= 0).astype(F32)).astype(jnp.int32)

        def tile_step(step, carry, side=side, out=out):
            at = pl.multiple_of(step * TILE, TILE)
            row = rows[side : side + 1, pl.ds(at, TILE)]
            lane = row & (LANES - 1)
            block = lax.shift_right_arithmetic(row, 7)
            number = row_numbers((LANES, TILE))
            lane_hot = jnp.where(number == lane, 1.0, 0.0).astype(BF16)
            block_hot = jnp.where(number == block, 1.0, 0.0).astype(BF16)
            gone[...] += lax.dot_general(block_hot, lane_hot, NT, preferred_element_type=F32)
            wanted = jnp.concatenate([lane_hot, lane_hot], 0)
            block8 = jnp.broadcast_to(block, (8, TILE))
            found = jnp.zeros((8, TILE), F32)
            for chunk in range(blocks // CHUNK):
                part = jnp.dot(
                    table[8 * CHUNK * chunk : 8 * CHUNK * (chunk + 1), :], wanted,
                    preferred_element_type=F32,
                )
                for i in range(CHUNK):
                    found = jnp.where(
                        block8 == chunk * CHUNK + i, part[8 * i : 8 * i + 8, :], found
                    )
            out[:, pl.ds(at, TILE)] = found
            return carry

        lax.fori_loop(0, (named + TILE - 1) // TILE, tile_step, 0)

    def keep(step, carry):
        at = pl.multiple_of(step * LANES, LANES)
        left = 1.0 - gone[pl.ds(step, 1), :]
        stay[:, pl.ds(at, LANES)] = (
            base[:, pl.ds(at, LANES)] * left + corner[:, pl.ds(at, LANES)]
        )
        return carry

    lax.fori_loop(0, blocks, keep, 0, unroll=8)


def gather_call(load, offset, cell, rows, bricks):
    count = load.shape[1]
    slots = rows.shape[1]
    moved = jax.ShapeDtypeStruct((8, slots), F32)
    return pl.pallas_call(
        gather_kernel,
        out_shape=(
            moved,
            moved,
            jax.ShapeDtypeStruct((8, count), F32),
            jax.ShapeDtypeStruct(bricks.shape, jnp.int32),
        ),
        in_specs=[pl.BlockSpec(memory_space=pltpu.HBM)] * 5,
        scratch_shapes=[
            pltpu.VMEM(load.shape, F32),
            pltpu.VMEM(offset.shape, F32),
            pltpu.VMEM((1, count), jnp.int32),
            pltpu.VMEM(rows.shape, jnp.int32),
            pltpu.VMEM((8 * (count // LANES), 2 * LANES), BF16),
            pltpu.VMEM((8, count), F32),
            pltpu.VMEM((8, count), F32),
            pltpu.VMEM((count // LANES, LANES), F32),
            pltpu.SemaphoreType.DMA((5,)),
        ],
        compiler_params=pltpu.CompilerParams(vmem_limit_bytes=16 * 2**20),
        name="gather_rows",
    )(load, offset, cell.reshape(1, count), rows, bricks)


class Grid:
    def __init__(self, span_y, span_z):
        self.span_y = span_y
        self.span_z = span_z
        self.per_row = span_z // 4
        self.bricks_y = span_y // 4
        self.groups = -(-self.bricks_y // GROUP)
        self.rows_z = span_z + 8
        self.rows = self.groups * FIELDS * self.rows_z
        self.pad_y = self.groups * SPAN

    def place(self, brick):
        z = brick % self.per_row
        y = (brick // self.per_row) % self.bricks_y
        group = y // GROUP
        first = group * (FIELDS * self.rows_z) + 4 * z
        return first, (4 * (y - group * GROUP)).astype(F32)


def plane_weights(block, shift_y):
    number = row_numbers((8, LANES)).astype(F32)
    x = hat(number - block[5:6])
    y = block[6:7] + shift_y
    parts = [hat(number + 8.0 * k - y) for k in range(SPAN // 8)]
    last = hat(float(SPAN) - y)
    pieces = [x[i : i + 1] * part for i in range(5) for part in parts]
    return split(jnp.concatenate(pieces + [x * last], 0))


def depth_weights(block):
    return hat(row_numbers((8, LANES)).astype(F32) - block[7:8])


def doubled(x):
    high, low = split(x)
    both = jnp.concatenate([high, low], 0).astype(BF16)
    return jnp.concatenate([both, both], 1)


def deposit_block(grid, block, brick, total):
    first, shift_y = grid.place(brick)
    high, low = plane_weights(block, shift_y)
    plane = jnp.concatenate([high.astype(BF16), low.astype(BF16)], 1)
    depth = depth_weights(block)
    loads = jnp.concatenate([block[f : f + 1] * depth for f in range(FIELDS)], 0)
    both = lax.dot_general(doubled(loads), plane, NT, preferred_element_type=F32)
    summed = both[: 8 * FIELDS] + both[8 * FIELDS :]
    for f in range(FIELDS):
        rows = pl.ds(first + f * grid.rows_z, 8)
        total[rows, :] += summed[8 * f : 8 * f + 8]


def sample_block(grid, block, brick, plane, held):
    first, _ = grid.place(brick)
    fields = jnp.concatenate(
        [held[pl.ds(first + f * grid.rows_z, 8), :] for f in range(FIELDS)], 0
    )
    both = jnp.dot(doubled(fields), plane, preferred_element_type=F32)
    summed = both[: 8 * FIELDS] + both[8 * FIELDS :]
    depth = depth_weights(block)
    return jnp.concatenate(
        [
            jnp.sum(summed[8 * f : 8 * f + 8] * depth, axis=0, keepdims=True)
            for f in range(FIELDS)
        ],
        0,
    )


UNROLL = 32


def deposit_loop(grid, parcels, bricks, offset, count, total):
    def step(turn, carry):
        for i in range(UNROLL):
            at = turn * UNROLL + i
            block = parcels[:, pl.ds(pl.multiple_of(at * LANES, LANES), LANES)]
            deposit_block(grid, block, bricks[offset + at], total)
        return carry

    lax.fori_loop(0, count // UNROLL, step, 0)


def deposit_stay_kernel(grid, bricks, parcels, total):
    total[...] = jnp.zeros_like(total)
    deposit_loop(grid, parcels, bricks, 0, parcels.shape[1] // LANES, total)


def deposit_moved_kernel(grid, bricks, lower, upper, held, total):
    total[...] = held[...]
    blocks = lower.shape[1] // LANES
    start = bricks.shape[0] - 2 * blocks
    deposit_loop(grid, lower, bricks, start, blocks, total)
    deposit_loop(grid, upper, bricks, start + blocks, blocks, total)


def merge_selector():
    picked = row_numbers((160, LANES))
    lane = lax.broadcasted_iota(jnp.int32, (160, LANES), 1)
    edge = picked - 5 * SPAN
    wanted = jnp.where(
        picked < 5 * SPAN, picked, jnp.where(edge % 8 == 0, 5 * SPAN + edge // 8, -1)
    )
    select = jnp.where(lane == wanted, 1.0, 0.0).astype(BF16)
    return jnp.concatenate([select, select], 1)


def merge_field(grid, f, select, total, sums):
    carried = None
    for group in range(grid.groups):
        first = (group * FIELDS + f) * grid.rows_z
        high, low = split(total[first : first + grid.span_z, :])
        both = jnp.concatenate([high.astype(BF16), low.astype(BF16)], 1)
        turned = lax.dot_general(select, both, NT, preferred_element_type=F32)
        for x in range(5):
            piece = turned[x * SPAN : (x + 1) * SPAN]
            if carried is not None:
                head = piece[:8] + carried[8 * x : 8 * x + 8]
                piece = jnp.concatenate([head, piece[8:]], 0)
            sums[f, x, group * SPAN : (group + 1) * SPAN, :] = piece
        carried = turned[5 * SPAN :]


def fill_faces(grid, f, second_half, gas, sums, up, down, row):
    ny = grid.span_y
    up[f] = sums[f, 4]
    down[f, :ny] = COUPLE * sums[f, 0, :ny] + gas[f, 0]
    down[f, ny:] = COUPLE * sums[f, 0, ny:]
    for x in range(5):
        low_row = COUPLE * sums[f, x, 0:1, :]
        if x < 4:
            low_row = low_row + gas[f, x, 0:1, :]
        high_row = COUPLE * sums[f, x, ny : ny + 1, :]
        row[x, f : f + 1, :] = jnp.where(second_half, low_row, high_row)


def sample_kernel(
    grid, last, bricks, place, stay, lower, upper, gas, sums, from_up, from_down,
    from_row, corner_low, corner_high, weights, source, sampled, field, held
):
    ny = grid.span_y
    second_half = place[1] == 1
    at_end = place[0] == last
    face = jnp.where(second_half, 1.0, 0.0)
    for f in range(FIELDS):
        for x in range(5):
            extra = from_row[x, f : f + 1, :]
            if x == 0:
                extra = extra + corner_low[f : f + 1, :]
            if x == 4:
                extra = extra + corner_high[f : f + 1, :]
            first = row_numbers((8, grid.span_z)) == 0
            head = jnp.where(first, 2.0 * face * extra, 0.0)
            mine = sums[f, x, :ny, :]
            if x == 0:
                mine = mine + from_up[f, :ny, :]
            mine = jnp.concatenate([mine[:8] + head, mine[8:]], 0)
            tail = COUPLE * sums[f, x, ny : ny + 8, :]
            if x == 0:
                tail = tail + COUPLE * from_up[f, ny : ny + 8, :]
            if x < 4:
                source[f, x] = mine
                mine = gas[f, x] + COUPLE * mine
            else:
                mine = COUPLE * mine + from_down[f, :ny, :]
                mine = jnp.where(at_end, 0.0, mine)
                tail = tail + from_down[f, ny : ny + 8, :]
                tail = jnp.where(at_end, 0.0, tail)
                extra = jnp.where(at_end, 0.0, extra)
            tail = jnp.where(first & jnp.logical_not(second_half), tail + extra, 0.0)
            field[f, x, :ny, :] = mine
            field[f, x, ny : ny + 8, :] = tail
    for f in range(FIELDS):
        for group in range(grid.groups):
            edge = SPAN * (group + 1)
            pieces = [field[f, x, edge - SPAN : edge, :] for x in range(5)]
            if edge < grid.pad_y:
                pieces += [field[f, x, edge : edge + 1, :] for x in range(5)]
                pieces.append(jnp.zeros((3, grid.span_z), F32))
            else:
                pieces.append(jnp.zeros((8, grid.span_z), F32))
            turned = jnp.concatenate(pieces, 0).T
            at = (group * FIELDS + f) * grid.rows_z
            held[at : at + grid.span_z, :] = turned
            held[at + grid.span_z : at + grid.rows_z, :] = jnp.zeros((8, LANES), F32)

    offset = 0
    for part in (stay, lower, upper):
        blocks = part.shape[1] // LANES

        def step(turn, carry, part=part, offset=offset):
            for i in range(UNROLL):
                at = turn * UNROLL + i
                block = part[:, pl.ds(pl.multiple_of(at * LANES, LANES), LANES)]
                place_at = pl.multiple_of((offset + at) * 2 * LANES, 2 * LANES)
                plane = weights[pl.ds(place_at, 2 * LANES), :]
                values = sample_block(grid, block, bricks[offset + at], plane, held)
                lanes = pl.ds(pl.multiple_of((offset + at) * LANES, LANES), LANES)
                sampled[:, lanes] = values.astype(BF16)
            return carry

        lax.fori_loop(0, blocks // UNROLL, step, 0)
        offset += blocks


SMEM = pl.BlockSpec(memory_space=pltpu.SMEM)
VMEM = pl.BlockSpec(memory_space=pltpu.VMEM)


def shift(block, route):
    return lax.ppermute(block, ("axial", "radial"), route)


BIG = pltpu.CompilerParams(vmem_limit_bytes=12 * 2**20)


def deposit_stay_call(grid, bricks, stay):
    return pl.pallas_call(
        functools.partial(deposit_stay_kernel, grid),
        out_shape=jax.ShapeDtypeStruct((grid.rows, LANES), F32),
        in_specs=[SMEM, VMEM],
        compiler_params=BIG,
        cost_estimate=pl.CostEstimate(flops=10**9, bytes_accessed=10**7, transcendentals=0),
        name="deposit_stay",
    )(bricks, stay)


def deposit_moved_call(grid, bricks, lower, upper, held):
    return pl.pallas_call(
        functools.partial(deposit_moved_kernel, grid),
        out_shape=jax.ShapeDtypeStruct((grid.rows, LANES), F32),
        in_specs=[SMEM, VMEM, VMEM, VMEM],
        compiler_params=BIG,
        name="deposit_moved",
    )(bricks, lower, upper, held)


WEIGHT_UNROLL = 8


def exchange_kernel(
    grid, last, bricks, stay, lower, upper, gas, total, sums, from_up, from_down, from_row,
    corner_low, corner_high, weights, up, down, edge, sent, got
):
    a = lax.axis_index("axial")
    r = lax.axis_index("radial")
    has_above = a < last
    has_below = a > 0
    barrier = pltpu.get_barrier_semaphore()

    def greet(axial_at, radial_at):
        pl.semaphore_signal(
            barrier, inc=1, device_id=(axial_at, radial_at),
            device_id_type=pl.DeviceIdType.MESH,
        )

    greet(a, 1 - r)

    @pl.when(has_above)
    def _():
        greet(a + 1, r)
        greet(a + 1, 1 - r)

    @pl.when(has_below)
    def _():
        greet(a - 1, r)
        greet(a - 1, 1 - r)

    peers = 1 + 2 * has_above.astype(jnp.int32) + 2 * has_below.astype(jnp.int32)

    def copy(number, source, target, axial_at, radial_at):
        return pltpu.make_async_remote_copy(
            src_ref=source, dst_ref=target, send_sem=sent.at[number],
            recv_sem=got.at[number], device_id=(axial_at, radial_at),
            device_id_type=pl.DeviceIdType.MESH,
        )

    row = copy(0, edge, from_row, a, 1 - r)
    corner_up = copy(1, edge.at[4], corner_low, a + 1, 1 - r)
    corner_down = copy(2, edge.at[0], corner_high, a - 1, 1 - r)
    faces_up = [copy(3 + f, up.at[f], from_up.at[f], a + 1, r) for f in range(FIELDS)]
    faces_down = [
        copy(3 + FIELDS + f, down.at[f], from_down.at[f], a - 1, r) for f in range(FIELDS)
    ]
    select = merge_selector()
    for x in range(5):
        edge[x, FIELDS:, :] = jnp.zeros((8 - FIELDS, grid.span_z), F32)
    for f in range(FIELDS):
        merge_field(grid, f, select, total, sums)
        fill_faces(grid, f, r == 1, gas, sums, up, down, edge)
        if f == 0:
            pl.semaphore_wait(barrier, peers)

        @pl.when(has_above)
        def _(f=f):
            faces_up[f].start()

        @pl.when(has_below)
        def _(f=f):
            faces_down[f].start()

    row.start()

    @pl.when(has_above)
    def _():
        corner_up.start()

    @pl.when(has_below)
    def _():
        corner_down.start()

    @pl.when(jnp.logical_not(has_below))
    def _():
        from_up[...] = jnp.zeros_like(from_up)
        corner_low[...] = jnp.zeros_like(corner_low)

    @pl.when(jnp.logical_not(has_above))
    def _():
        from_down[...] = jnp.zeros_like(from_down)
        corner_high[...] = jnp.zeros_like(corner_high)

    offset = 0
    for part in (stay, lower, upper):
        blocks = part.shape[1] // LANES

        def step(turn, carry, part=part, offset=offset):
            for i in range(WEIGHT_UNROLL):
                at = turn * WEIGHT_UNROLL + i
                block = part[:, pl.ds(pl.multiple_of(at * LANES, LANES), LANES)]
                _, shift_y = grid.place(bricks[offset + at])
                both = jnp.concatenate(plane_weights(block, shift_y), 0)
                place_at = pl.multiple_of((offset + at) * 2 * LANES, 2 * LANES)
                weights[pl.ds(place_at, 2 * LANES), :] = both.astype(BF16)
            return carry

        lax.fori_loop(0, blocks // WEIGHT_UNROLL, step, 0)
        offset += blocks

    row.wait()

    @pl.when(has_above)
    def _():
        for each in faces_up + [corner_up]:
            each.wait_send()
        for each in faces_down + [corner_down]:
            each.wait_recv()

    @pl.when(has_below)
    def _():
        for each in faces_down + [corner_down]:
            each.wait_send()
        for each in faces_up + [corner_up]:
            each.wait_recv()


def exchange_call(grid, last, bricks, stay, lower, upper, gas, total):
    plane = (FIELDS, grid.pad_y, grid.span_z)
    edge = (5, 8, grid.span_z)
    corner = jax.ShapeDtypeStruct(edge[1:], F32)
    copies = 3 + 2 * FIELDS
    return pl.pallas_call(
        functools.partial(exchange_kernel, grid, last),
        out_shape=(
            jax.ShapeDtypeStruct((FIELDS, 5, grid.pad_y, grid.span_z), F32),
            jax.ShapeDtypeStruct(plane, F32),
            jax.ShapeDtypeStruct(plane, F32),
            jax.ShapeDtypeStruct(edge, F32),
            corner,
            corner,
            jax.ShapeDtypeStruct((bricks.shape[0] * 2 * LANES, LANES), BF16),
        ),
        in_specs=[SMEM] + [VMEM] * 5,
        out_specs=(VMEM,) * 7,
        scratch_shapes=[
            pltpu.VMEM(plane, F32),
            pltpu.VMEM(plane, F32),
            pltpu.VMEM(edge, F32),
            pltpu.SemaphoreType.DMA((copies,)),
            pltpu.SemaphoreType.DMA((copies,)),
        ],
        compiler_params=pltpu.CompilerParams(
            collective_id=0, has_side_effects=True, vmem_limit_bytes=8 * 2**20
        ),
        name="exchange",
    )(bricks, stay, lower, upper, gas, total)


def sample_call(grid, last, bricks, place, *arrays):
    gas = arrays[3]
    return pl.pallas_call(
        functools.partial(sample_kernel, grid, last),
        out_shape=(
            jax.ShapeDtypeStruct(gas.shape, F32),
            jax.ShapeDtypeStruct((FIELDS, bricks.shape[0] * LANES), BF16),
        ),
        in_specs=[SMEM, SMEM] + [VMEM] * 11,
        scratch_shapes=[
            pltpu.VMEM((FIELDS, 5, grid.pad_y, grid.span_z), F32),
            pltpu.VMEM((grid.rows, LANES), F32),
        ],
        compiler_params=BIG,
        name="sample",
    )(bricks, place, *arrays)


def per_device(load, offset, cell, rows, bricks, gas):
    axial = lax.axis_size("axial")
    radial = lax.axis_size("radial")
    span_y, span_z = gas.shape[2], gas.shape[3]
    grid = Grid(span_y, span_z)
    place = jnp.stack([lax.axis_index("axial"), lax.axis_index("radial")]).astype(jnp.int32)
    everyone = [(a, r) for a in range(axial) for r in range(radial)]

    def route(step_a, flip):
        return [
            (a * radial + r, (a + step_a) * radial + (radial - 1 - r if flip else r))
            for a, r in everyone
            if 0 <= a + step_a < axial
        ]

    up, down, stay, bricks = gather_call(load, offset, cell, rows, bricks)
    lower = shift(up, route(1, False))
    upper = shift(down, route(-1, False))
    held = deposit_stay_call(grid, bricks, stay)
    total = deposit_moved_call(grid, bricks, lower, upper, held)
    arrived = exchange_call(grid, axial - 1, bricks, stay, lower, upper, gas, total)
    return sample_call(
        grid, axial - 1, bricks, place, stay, lower, upper, gas, *arrived
    )


def solution(mesh):
    return jax.shard_map(
        per_device,
        mesh=mesh,
        in_specs=(
            P(None, ("axial", "radial")),
            P(None, ("axial", "radial")),
            P(("axial", "radial")),
            P(None, ("axial", "radial")),
            P(("axial", "radial")),
            P(None, "axial", "radial", None),
        ),
        out_specs=(P(None, "axial", "radial", None), P(None, ("axial", "radial"))),
        check_vma=False,
    )
```

```python
import functools

import jax
import jax.numpy as jnp
from jax import lax
from jax.experimental import pallas as pl
from jax.experimental.pallas import tpu as pltpu
from jax.sharding import PartitionSpec as P

COUPLE = 0.5
LANES = 128
TILE = 2048
CHUNK = 32
FIELDS = 5
GROUP = 6
SPAN = 4 * GROUP
NT = (((1,), (1,)), ((), ()))
F32 = jnp.float32
BF16 = jnp.bfloat16


def split(x):
    high = x.astype(BF16).astype(F32)
    return high, x - high


def hat(x):
    return jnp.maximum(1.0 - jnp.abs(x), 0.0)


def row_numbers(shape):
    return lax.broadcasted_iota(jnp.int32, shape, 0)


def gather_kernel(
    load_in, offset_in, cell_in, rows_in, bricks_in, up, down, stay, bricks, load, offset,
    cell, rows, table, base, corner, gone, arrived
):
    pairs = (
        (cell_in, cell), (load_in, load), (offset_in, offset), (rows_in, rows),
        (bricks_in, bricks),
    )
    copies = [
        pltpu.make_async_copy(source, target, arrived.at[i])
        for i, (source, target) in enumerate(pairs)
    ]
    for each in copies:
        each.start()
    for each in copies:
        each.wait()
    count = load.shape[1]
    blocks = count // LANES
    slots = rows.shape[1]
    axis_row = row_numbers((3, count))
    coords = lax.shift_right_logical(
        jnp.broadcast_to(cell[...], (3, count)), 4 - 2 * axis_row
    ) & 3
    corner[...] = jnp.concatenate([jnp.zeros((5, count), F32), coords.astype(F32)], 0)
    base[...] = jnp.concatenate([load[...], offset[...]], 0)

    def fill(step, carry):
        at = pl.multiple_of(step * 2 * LANES, 2 * LANES)
        pair = base[:, pl.ds(at, 2 * LANES)] + corner[:, pl.ds(at, 2 * LANES)]
        both = jnp.concatenate([pair[:, :LANES], pair[:, LANES:]], 0)
        high, low = split(both)
        place = pl.multiple_of(step * 16, 16)
        table[pl.ds(place, 16), :] = jnp.concatenate([high, low], 1).astype(BF16)
        return carry

    lax.fori_loop(0, blocks // 2, fill, 0, unroll=8)
    gone[...] = jnp.zeros_like(gone)

    for side, out in ((0, up), (1, down)):
        out[...] = jnp.zeros_like(out)
        named = jnp.sum((rows[side : side + 1, :] >= 0).astype(F32)).astype(jnp.int32)

        def tile_step(step, carry, side=side, out=out):
            at = pl.multiple_of(step * TILE, TILE)
            row = rows[side : side + 1, pl.ds(at, TILE)]
            lane = row & (LANES - 1)
            block = lax.shift_right_arithmetic(row, 7)
            number = row_numbers((LANES, TILE))
            lane_hot = jnp.where(number == lane, 1.0, 0.0).astype(BF16)
            block_hot = jnp.where(number == block, 1.0, 0.0).astype(BF16)
            gone[...] += lax.dot_general(block_hot, lane_hot, NT, preferred_element_type=F32)
            wanted = jnp.concatenate([lane_hot, lane_hot], 0)
            block8 = jnp.broadcast_to(block, (8, TILE))
            found = jnp.zeros((8, TILE), F32)
            for chunk in range(blocks // CHUNK):
                part = jnp.dot(
                    table[8 * CHUNK * chunk : 8 * CHUNK * (chunk + 1), :], wanted,
                    preferred_element_type=F32,
                )
                for i in range(CHUNK):
                    found = jnp.where(
                        block8 == chunk * CHUNK + i, part[8 * i : 8 * i + 8, :], found
                    )
            out[:, pl.ds(at, TILE)] = found
            return carry

        lax.fori_loop(0, (named + TILE - 1) // TILE, tile_step, 0)

    def keep(step, carry):
        at = pl.multiple_of(step * LANES, LANES)
        left = 1.0 - gone[pl.ds(step, 1), :]
        stay[:, pl.ds(at, LANES)] = (
            base[:, pl.ds(at, LANES)] * left + corner[:, pl.ds(at, LANES)]
        )
        return carry

    lax.fori_loop(0, blocks, keep, 0, unroll=8)


def gather_call(load, offset, cell, rows, bricks):
    count = load.shape[1]
    slots = rows.shape[1]
    moved = jax.ShapeDtypeStruct((8, slots), F32)
    return pl.pallas_call(
        gather_kernel,
        out_shape=(
            moved,
            moved,
            jax.ShapeDtypeStruct((8, count), F32),
            jax.ShapeDtypeStruct(bricks.shape, jnp.int32),
        ),
        in_specs=[pl.BlockSpec(memory_space=pltpu.HBM)] * 5,
        scratch_shapes=[
            pltpu.VMEM(load.shape, F32),
            pltpu.VMEM(offset.shape, F32),
            pltpu.VMEM((1, count), jnp.int32),
            pltpu.VMEM(rows.shape, jnp.int32),
            pltpu.VMEM((8 * (count // LANES), 2 * LANES), BF16),
            pltpu.VMEM((8, count), F32),
            pltpu.VMEM((8, count), F32),
            pltpu.VMEM((count // LANES, LANES), F32),
            pltpu.SemaphoreType.DMA((5,)),
        ],
        compiler_params=pltpu.CompilerParams(vmem_limit_bytes=16 * 2**20),
        name="gather_rows",
    )(load, offset, cell.reshape(1, count), rows, bricks)


class Grid:
    def __init__(self, span_y, span_z):
        self.span_y = span_y
        self.span_z = span_z
        self.per_row = span_z // 4
        self.bricks_y = span_y // 4
        self.groups = -(-self.bricks_y // GROUP)
        self.rows_z = span_z + 8
        self.rows = self.groups * FIELDS * self.rows_z
        self.pad_y = self.groups * SPAN

    def place(self, brick):
        z = brick % self.per_row
        y = (brick // self.per_row) % self.bricks_y
        group = y // GROUP
        first = group * (FIELDS * self.rows_z) + 4 * z
        return first, (4 * (y - group * GROUP)).astype(F32)


def plane_weights(block, shift_y):
    number = row_numbers((8, LANES)).astype(F32)
    x = hat(number - block[5:6])
    y = block[6:7] + shift_y
    parts = [hat(number + 8.0 * k - y) for k in range(SPAN // 8)]
    last = hat(float(SPAN) - y)
    pieces = [x[i : i + 1] * part for i in range(5) for part in parts]
    return split(jnp.concatenate(pieces + [x * last], 0))


def depth_weights(block):
    return hat(row_numbers((8, LANES)).astype(F32) - block[7:8])


def doubled(x):
    high, low = split(x)
    both = jnp.concatenate([high, low], 0).astype(BF16)
    return jnp.concatenate([both, both], 1)


def spread_block(block, weights):
    high, low = weights
    plane = jnp.concatenate([high.astype(BF16), low.astype(BF16)], 1)
    depth = depth_weights(block)
    loads = jnp.concatenate([block[f : f + 1] * depth for f in range(FIELDS)], 0)
    both = lax.dot_general(doubled(loads), plane, NT, preferred_element_type=F32)
    return both[: 8 * FIELDS] + both[8 * FIELDS :]


def add_block(grid, summed, brick, total):
    first, _ = grid.place(brick)
    for f in range(FIELDS):
        rows = pl.ds(first + f * grid.rows_z, 8)
        total[rows, :] += summed[8 * f : 8 * f + 8]


def sample_block(grid, block, brick, plane, held):
    first, _ = grid.place(brick)
    fields = jnp.concatenate(
        [held[pl.ds(first + f * grid.rows_z, 8), :] for f in range(FIELDS)], 0
    )
    both = jnp.dot(doubled(fields), plane, preferred_element_type=F32)
    summed = both[: 8 * FIELDS] + both[8 * FIELDS :]
    depth = depth_weights(block)
    return jnp.concatenate(
        [
            jnp.sum(summed[8 * f : 8 * f + 8] * depth, axis=0, keepdims=True)
            for f in range(FIELDS)
        ],
        0,
    )


UNROLL = 32


def deposit_kernel(grid, bricks, spread, lower, upper, total):
    total[...] = jnp.zeros_like(total)
    blocks = lower.shape[1] // LANES
    resident = bricks.shape[0] - 2 * blocks
    ratio = resident // (2 * blocks)
    for part, offset in ((lower, 0), (upper, blocks)):

        def step(turn, carry, part=part, offset=offset):
            for i in range(UNROLL):
                at = turn * UNROLL + i
                block = part[:, pl.ds(pl.multiple_of(at * LANES, LANES), LANES)]
                brick = bricks[resident + offset + at]
                weights = plane_weights(block, grid.place(brick)[1])
                add_block(grid, spread_block(block, weights), brick, total)
                for j in range(ratio):
                    own = (offset + at) * ratio + j
                    rows = pl.ds(pl.multiple_of(own * 8 * FIELDS, 8), 8 * FIELDS)
                    add_block(grid, spread[rows, :], bricks[own], total)
            return carry

        lax.fori_loop(0, blocks // UNROLL, step, 0)


def merge_selector():
    picked = row_numbers((160, LANES))
    lane = lax.broadcasted_iota(jnp.int32, (160, LANES), 1)
    edge = picked - 5 * SPAN
    wanted = jnp.where(
        picked < 5 * SPAN, picked, jnp.where(edge % 8 == 0, 5 * SPAN + edge // 8, -1)
    )
    select = jnp.where(lane == wanted, 1.0, 0.0).astype(BF16)
    return jnp.concatenate([select, select], 1)


def merge_field(grid, f, select, total, sums):
    carried = None
    for group in range(grid.groups):
        first = (group * FIELDS + f) * grid.rows_z
        high, low = split(total[first : first + grid.span_z, :])
        both = jnp.concatenate([high.astype(BF16), low.astype(BF16)], 1)
        turned = lax.dot_general(select, both, NT, preferred_element_type=F32)
        for x in range(5):
            piece = turned[x * SPAN : (x + 1) * SPAN]
            if carried is not None:
                head = piece[:8] + carried[8 * x : 8 * x + 8]
                piece = jnp.concatenate([head, piece[8:]], 0)
            sums[f, x, group * SPAN : (group + 1) * SPAN, :] = piece
        carried = turned[5 * SPAN :]


def fill_faces(grid, f, second_half, gas, sums, up, down, row):
    ny = grid.span_y
    up[f] = sums[f, 4]
    down[f, :ny] = COUPLE * sums[f, 0, :ny] + gas[f, 0]
    down[f, ny:] = COUPLE * sums[f, 0, ny:]
    for x in range(5):
        low_row = COUPLE * sums[f, x, 0:1, :]
        if x < 4:
            low_row = low_row + gas[f, x, 0:1, :]
        high_row = COUPLE * sums[f, x, ny : ny + 1, :]
        row[x, f : f + 1, :] = jnp.where(second_half, low_row, high_row)


def sample_kernel(
    grid, last, bricks, stay, lower, upper, gas, sums, from_up, from_down,
    from_row, corner_low, corner_high, weights, source, sampled, field, held
):
    ny = grid.span_y
    second_half = lax.axis_index("radial") == 1
    at_end = lax.axis_index("axial") == last
    face = jnp.where(second_half, 1.0, 0.0)
    for f in range(FIELDS):
        for x in range(5):
            extra = from_row[x, f : f + 1, :]
            if x == 0:
                extra = extra + corner_low[f : f + 1, :]
            if x == 4:
                extra = extra + corner_high[f : f + 1, :]
            first = row_numbers((8, grid.span_z)) == 0
            head = jnp.where(first, 2.0 * face * extra, 0.0)
            mine = sums[f, x, :ny, :]
            if x == 0:
                mine = mine + from_up[f, :ny, :]
            mine = jnp.concatenate([mine[:8] + head, mine[8:]], 0)
            tail = COUPLE * sums[f, x, ny : ny + 8, :]
            if x == 0:
                tail = tail + COUPLE * from_up[f, ny : ny + 8, :]
            if x < 4:
                source[f, x] = mine
                mine = gas[f, x] + COUPLE * mine
            else:
                mine = COUPLE * mine + from_down[f, :ny, :]
                mine = jnp.where(at_end, 0.0, mine)
                tail = tail + from_down[f, ny : ny + 8, :]
                tail = jnp.where(at_end, 0.0, tail)
                extra = jnp.where(at_end, 0.0, extra)
            tail = jnp.where(first & jnp.logical_not(second_half), tail + extra, 0.0)
            field[f, x, :ny, :] = mine
            field[f, x, ny : ny + 8, :] = tail
    for f in range(FIELDS):
        for group in range(grid.groups):
            edge = SPAN * (group + 1)
            pieces = [field[f, x, edge - SPAN : edge, :] for x in range(5)]
            if edge < grid.pad_y:
                pieces += [field[f, x, edge : edge + 1, :] for x in range(5)]
                pieces.append(jnp.zeros((3, grid.span_z), F32))
            else:
                pieces.append(jnp.zeros((8, grid.span_z), F32))
            turned = jnp.concatenate(pieces, 0).T
            at = (group * FIELDS + f) * grid.rows_z
            held[at : at + grid.span_z, :] = turned
            held[at + grid.span_z : at + grid.rows_z, :] = jnp.zeros((8, LANES), F32)

    offset = 0
    for part in (stay, lower, upper):
        blocks = part.shape[1] // LANES

        def step(turn, carry, part=part, offset=offset):
            for i in range(UNROLL):
                at = turn * UNROLL + i
                block = part[:, pl.ds(pl.multiple_of(at * LANES, LANES), LANES)]
                place_at = pl.multiple_of((offset + at) * 2 * LANES, 2 * LANES)
                plane = weights[pl.ds(place_at, 2 * LANES), :]
                values = sample_block(grid, block, bricks[offset + at], plane, held)
                lanes = pl.ds(pl.multiple_of((offset + at) * LANES, LANES), LANES)
                sampled[:, lanes] = values.astype(BF16)
            return carry

        lax.fori_loop(0, blocks // UNROLL, step, 0)
        offset += blocks


SMEM = pl.BlockSpec(memory_space=pltpu.SMEM)
VMEM = pl.BlockSpec(memory_space=pltpu.VMEM)


BIG = pltpu.CompilerParams(vmem_limit_bytes=12 * 2**20)


def deposit_call(grid, bricks, spread, lower, upper):
    return pl.pallas_call(
        functools.partial(deposit_kernel, grid),
        out_shape=jax.ShapeDtypeStruct((grid.rows, LANES), F32),
        in_specs=[SMEM, VMEM, VMEM, VMEM],
        compiler_params=BIG,
        name="deposit",
    )(bricks, spread, lower, upper)


def signal_entry(axial_at, radial_at):
    pl.semaphore_signal(
        pltpu.get_barrier_semaphore(), inc=1, device_id=(axial_at, radial_at),
        device_id_type=pl.DeviceIdType.MESH,
    )


def store_weights(target, at, weights):
    place = pl.multiple_of(at * 2 * LANES, 2 * LANES)
    target[pl.ds(place, 2 * LANES), :] = jnp.concatenate(weights, 0).astype(BF16)


FILLER = 1


def migrate_kernel(
    grid, last, bricks, up, down, stay, lower, upper, spread, sent, got
):
    a = lax.axis_index("axial")
    r = lax.axis_index("radial")
    has_above = a < last
    has_below = a > 0

    @pl.when(has_above)
    def _():
        signal_entry(a + 1, r)

    @pl.when(has_below)
    def _():
        signal_entry(a - 1, r)

    def copy(number, source, target, axial_at):
        return pltpu.make_async_remote_copy(
            src_ref=source, dst_ref=target, send_sem=sent.at[number],
            recv_sem=got.at[number], device_id=(axial_at, r),
            device_id_type=pl.DeviceIdType.MESH,
        )

    rising = copy(0, up, lower, a + 1)
    falling = copy(1, down, upper, a - 1)

    def step(turn, carry):
        for i in range(UNROLL):
            at = turn * UNROLL + i
            block = stay[:, pl.ds(pl.multiple_of(at * LANES, LANES), LANES)]
            plane = plane_weights(block, grid.place(bricks[at])[1])
            rows = pl.ds(pl.multiple_of(at * 8 * FIELDS, 8), 8 * FIELDS)
            spread[rows, :] = spread_block(block, plane)
        return carry

    lax.fori_loop(0, FILLER, step, 0)
    peers = has_above.astype(jnp.int32) + has_below.astype(jnp.int32)
    pl.semaphore_wait(pltpu.get_barrier_semaphore(), peers)

    @pl.when(has_above)
    def _():
        rising.start()

    @pl.when(has_below)
    def _():
        falling.start()

    @pl.when(jnp.logical_not(has_below))
    def _():
        lower[...] = jnp.zeros_like(lower)

    @pl.when(jnp.logical_not(has_above))
    def _():
        upper[...] = jnp.zeros_like(upper)

    lax.fori_loop(FILLER, stay.shape[1] // LANES // UNROLL, step, 0)

    @pl.when(has_above)
    def _():
        rising.wait_send()
        falling.wait_recv()

    @pl.when(has_below)
    def _():
        falling.wait_send()
        rising.wait_recv()


def migrate_call(grid, last, bricks, up, down, stay):
    blocks = stay.shape[1] // LANES
    return pl.pallas_call(
        functools.partial(migrate_kernel, grid, last),
        out_shape=(
            jax.ShapeDtypeStruct(up.shape, F32),
            jax.ShapeDtypeStruct(down.shape, F32),
            jax.ShapeDtypeStruct((blocks * 8 * FIELDS, LANES), F32),
        ),
        in_specs=[SMEM] + [VMEM] * 3,
        out_specs=(VMEM,) * 3,
        scratch_shapes=[pltpu.SemaphoreType.DMA((2,)), pltpu.SemaphoreType.DMA((2,))],
        compiler_params=pltpu.CompilerParams(
            collective_id=1, has_side_effects=True, vmem_limit_bytes=8 * 2**20
        ),
        name="migrate",
    )(bricks, up, down, stay)


def exchange_kernel(
    grid, last, bricks, stay, lower, upper, gas, total, sums, from_up, from_down, from_row,
    corner_low, corner_high, weights, up, down, edge, sent, got
):
    a = lax.axis_index("axial")
    r = lax.axis_index("radial")
    has_above = a < last
    has_below = a > 0
    signal_entry(a, 1 - r)

    @pl.when(has_above)
    def _():
        signal_entry(a + 1, r)
        signal_entry(a + 1, 1 - r)

    @pl.when(has_below)
    def _():
        signal_entry(a - 1, r)
        signal_entry(a - 1, 1 - r)

    peers = 1 + 2 * has_above.astype(jnp.int32) + 2 * has_below.astype(jnp.int32)

    def copy(number, source, target, axial_at, radial_at):
        return pltpu.make_async_remote_copy(
            src_ref=source, dst_ref=target, send_sem=sent.at[number],
            recv_sem=got.at[number], device_id=(axial_at, radial_at),
            device_id_type=pl.DeviceIdType.MESH,
        )

    row = copy(0, edge, from_row, a, 1 - r)
    corner_up = copy(1, edge.at[4], corner_low, a + 1, 1 - r)
    corner_down = copy(2, edge.at[0], corner_high, a - 1, 1 - r)
    faces_up = [copy(3 + f, up.at[f], from_up.at[f], a + 1, r) for f in range(FIELDS)]
    faces_down = [
        copy(3 + FIELDS + f, down.at[f], from_down.at[f], a - 1, r) for f in range(FIELDS)
    ]
    select = merge_selector()
    for x in range(5):
        edge[x, FIELDS:, :] = jnp.zeros((8 - FIELDS, grid.span_z), F32)
    def weigh(part, offset):
        def step(turn, carry):
            for i in range(UNROLL):
                at = turn * UNROLL + i
                block = part[:, pl.ds(pl.multiple_of(at * LANES, LANES), LANES)]
                plane = plane_weights(block, grid.place(bricks[offset + at])[1])
                store_weights(weights, offset + at, plane)
            return carry

        lax.fori_loop(0, part.shape[1] // LANES // UNROLL, step, 0)

    for f in range(FIELDS):
        merge_field(grid, f, select, total, sums)
        fill_faces(grid, f, r == 1, gas, sums, up, down, edge)
    weigh(stay, 0)
    pl.semaphore_wait(pltpu.get_barrier_semaphore(), peers)
    for f in range(FIELDS):

        @pl.when(has_above)
        def _(f=f):
            faces_up[f].start()

        @pl.when(has_below)
        def _(f=f):
            faces_down[f].start()

    row.start()

    @pl.when(has_above)
    def _():
        corner_up.start()

    @pl.when(has_below)
    def _():
        corner_down.start()

    @pl.when(jnp.logical_not(has_below))
    def _():
        from_up[...] = jnp.zeros_like(from_up)
        corner_low[...] = jnp.zeros_like(corner_low)

    @pl.when(jnp.logical_not(has_above))
    def _():
        from_down[...] = jnp.zeros_like(from_down)
        corner_high[...] = jnp.zeros_like(corner_high)

    resident = stay.shape[1] // LANES
    weigh(lower, resident)
    weigh(upper, resident + lower.shape[1] // LANES)
    row.wait()

    @pl.when(has_above)
    def _():
        for each in faces_up + [corner_up]:
            each.wait_send()
        for each in faces_down + [corner_down]:
            each.wait_recv()

    @pl.when(has_below)
    def _():
        for each in faces_down + [corner_down]:
            each.wait_send()
        for each in faces_up + [corner_up]:
            each.wait_recv()


def exchange_call(grid, last, bricks, stay, lower, upper, gas, total):
    plane = (FIELDS, grid.pad_y, grid.span_z)
    edge = (5, 8, grid.span_z)
    corner = jax.ShapeDtypeStruct(edge[1:], F32)
    copies = 3 + 2 * FIELDS
    return pl.pallas_call(
        functools.partial(exchange_kernel, grid, last),
        out_shape=(
            jax.ShapeDtypeStruct((FIELDS, 5, grid.pad_y, grid.span_z), F32),
            jax.ShapeDtypeStruct(plane, F32),
            jax.ShapeDtypeStruct(plane, F32),
            jax.ShapeDtypeStruct(edge, F32),
            corner,
            corner,
            jax.ShapeDtypeStruct((bricks.shape[0] * 2 * LANES, LANES), BF16),
        ),
        in_specs=[SMEM] + [VMEM] * 5,
        out_specs=(VMEM,) * 7,
        scratch_shapes=[
            pltpu.VMEM(plane, F32),
            pltpu.VMEM(plane, F32),
            pltpu.VMEM(edge, F32),
            pltpu.SemaphoreType.DMA((copies,)),
            pltpu.SemaphoreType.DMA((copies,)),
        ],
        compiler_params=pltpu.CompilerParams(
            collective_id=0, has_side_effects=True, vmem_limit_bytes=8 * 2**20
        ),
        name="exchange",
    )(bricks, stay, lower, upper, gas, total)


def sample_call(grid, last, bricks, *arrays):
    gas = arrays[3]
    return pl.pallas_call(
        functools.partial(sample_kernel, grid, last),
        out_shape=(
            jax.ShapeDtypeStruct(gas.shape, F32),
            jax.ShapeDtypeStruct((FIELDS, bricks.shape[0] * LANES), BF16),
        ),
        in_specs=[SMEM] + [VMEM] * 11,
        scratch_shapes=[
            pltpu.VMEM((FIELDS, 5, grid.pad_y, grid.span_z), F32),
            pltpu.VMEM((grid.rows, LANES), F32),
        ],
        compiler_params=BIG,
        name="sample",
    )(bricks, *arrays)


def per_device(load, offset, cell, rows, bricks, gas):
    axial = lax.axis_size("axial")
    span_y, span_z = gas.shape[2], gas.shape[3]
    grid = Grid(span_y, span_z)
    up, down, stay, bricks = gather_call(load, offset, cell, rows, bricks)
    lower, upper, spread = migrate_call(grid, axial - 1, bricks, up, down, stay)
    total = deposit_call(grid, bricks, spread, lower, upper)
    arrived = exchange_call(grid, axial - 1, bricks, stay, lower, upper, gas, total)
    return sample_call(
        grid, axial - 1, bricks, stay, lower, upper, gas, *arrived
    )


def solution(mesh):
    return jax.shard_map(
        per_device,
        mesh=mesh,
        in_specs=(
            P(None, ("axial", "radial")),
            P(None, ("axial", "radial")),
            P(("axial", "radial")),
            P(None, ("axial", "radial")),
            P(("axial", "radial")),
            P(None, "axial", "radial", None),
        ),
        out_specs=(P(None, "axial", "radial", None), P(None, ("axial", "radial"))),
        check_vma=False,
    )
```

```python
import functools

import jax
import jax.numpy as jnp
from jax import lax
from jax.experimental import pallas as pl
from jax.experimental.pallas import tpu as pltpu
from jax.sharding import PartitionSpec as P

COUPLE = 0.5
LANES = 128
TILE = 2048
CHUNK = 32
FIELDS = 5
GROUP = 6
SPAN = 4 * GROUP
NT = (((1,), (1,)), ((), ()))
SMEM = pl.BlockSpec(memory_space=pltpu.SMEM)
VMEM = pl.BlockSpec(memory_space=pltpu.VMEM)
F32 = jnp.float32
BF16 = jnp.bfloat16


def split(x):
    high = x.astype(BF16).astype(F32)
    return high, x - high


def hat(x):
    return jnp.maximum(1.0 - jnp.abs(x), 0.0)


def row_numbers(shape):
    return lax.broadcasted_iota(jnp.int32, shape, 0)


def clear_kernel(total, gone):
    total[...] = jnp.zeros_like(total)
    gone[...] = jnp.zeros_like(gone)


def clear_call(grid, blocks):
    return pl.pallas_call(
        clear_kernel,
        out_shape=(
            jax.ShapeDtypeStruct((grid.rows, LANES), F32),
            jax.ShapeDtypeStruct((blocks, LANES), F32),
        ),
        compiler_params=pltpu.CompilerParams(vmem_limit_bytes=2**20),
        cost_estimate=pl.CostEstimate(
            flops=10**10, bytes_accessed=2 * 10**6, transcendentals=0
        ),
        name="clear",
    )()


def gather_kernel(
    load, offset, cell, rows, none_gone, up, down, stay, table, base, corner, gone
):
    count = load.shape[1]
    blocks = count // LANES
    axis_row = row_numbers((3, count))
    coords = lax.shift_right_logical(
        jnp.broadcast_to(cell[...], (3, count)), 4 - 2 * axis_row
    ) & 3
    corner[...] = jnp.concatenate([jnp.zeros((5, count), F32), coords.astype(F32)], 0)
    base[...] = jnp.concatenate([load[...], offset[...]], 0)

    def fill(step, carry):
        at = pl.multiple_of(step * 2 * LANES, 2 * LANES)
        pair = base[:, pl.ds(at, 2 * LANES)] + corner[:, pl.ds(at, 2 * LANES)]
        both = jnp.concatenate([pair[:, :LANES], pair[:, LANES:]], 0)
        high, low = split(both)
        place = pl.multiple_of(step * 16, 16)
        table[pl.ds(place, 16), :] = jnp.concatenate([high, low], 1).astype(BF16)
        return carry

    lax.fori_loop(0, blocks // 2, fill, 0, unroll=8)
    gone[...] = none_gone[...]

    for side, out in ((0, up), (1, down)):
        out[...] = jnp.zeros_like(out)
        named = jnp.sum((rows[side : side + 1, :] >= 0).astype(F32)).astype(jnp.int32)

        def tile_step(step, carry, side=side, out=out):
            at = pl.multiple_of(step * TILE, TILE)
            row = rows[side : side + 1, pl.ds(at, TILE)]
            lane = row & (LANES - 1)
            block = lax.shift_right_arithmetic(row, 7)
            number = row_numbers((LANES, TILE))
            lane_hot = jnp.where(number == lane, 1.0, 0.0).astype(BF16)
            block_hot = jnp.where(number == block, 1.0, 0.0).astype(BF16)
            gone[...] += lax.dot_general(block_hot, lane_hot, NT, preferred_element_type=F32)
            wanted = jnp.concatenate([lane_hot, lane_hot], 0)
            block8 = jnp.broadcast_to(block, (8, TILE))
            found = jnp.zeros((8, TILE), F32)
            for chunk in range(blocks // CHUNK):
                part = jnp.dot(
                    table[8 * CHUNK * chunk : 8 * CHUNK * (chunk + 1), :], wanted,
                    preferred_element_type=F32,
                )
                for i in range(CHUNK):
                    found = jnp.where(
                        block8 == chunk * CHUNK + i, part[8 * i : 8 * i + 8, :], found
                    )
            out[:, pl.ds(at, TILE)] = found
            return carry

        lax.fori_loop(0, (named + TILE - 1) // TILE, tile_step, 0)

    def keep(step, carry):
        at = pl.multiple_of(step * LANES, LANES)
        left = 1.0 - gone[pl.ds(step, 1), :]
        stay[:, pl.ds(at, LANES)] = (
            base[:, pl.ds(at, LANES)] * left + corner[:, pl.ds(at, LANES)]
        )
        return carry

    lax.fori_loop(0, blocks, keep, 0, unroll=8)


def gather_call(load, offset, cell, rows, none_gone):
    count = load.shape[1]
    slots = rows.shape[1]
    moved = jax.ShapeDtypeStruct((8, slots), F32)
    return pl.pallas_call(
        gather_kernel,
        out_shape=(moved, moved, jax.ShapeDtypeStruct((8, count), F32)),
        in_specs=[VMEM] * 5,
        scratch_shapes=[
            pltpu.VMEM((8 * (count // LANES), 2 * LANES), BF16),
            pltpu.VMEM((8, count), F32),
            pltpu.VMEM((8, count), F32),
            pltpu.VMEM((count // LANES, LANES), F32),
        ],
        compiler_params=pltpu.CompilerParams(vmem_limit_bytes=16 * 2**20),
        cost_estimate=pl.CostEstimate(
            flops=10**10, bytes_accessed=2 * 10**6, transcendentals=0
        ),
        name="gather_rows",
    )(load, offset, cell.reshape(1, count), rows, none_gone)


class Grid:
    def __init__(self, span_y, span_z):
        self.span_y = span_y
        self.span_z = span_z
        self.per_row = span_z // 4
        self.bricks_y = span_y // 4
        self.groups = -(-self.bricks_y // GROUP)
        self.rows_z = span_z + 8
        self.rows = self.groups * FIELDS * self.rows_z
        self.pad_y = self.groups * SPAN
        self.shift = self.per_row.bit_length() - 1
        assert self.per_row == 1 << self.shift and self.bricks_y & (self.bricks_y - 1) == 0

    def place(self, brick):
        z = brick & (self.per_row - 1)
        y = lax.shift_right_logical(brick, self.shift) & (self.bricks_y - 1)
        group = sum((y >= GROUP * k).astype(jnp.int32) for k in range(1, self.groups))
        first = group * (FIELDS * self.rows_z) + 4 * z
        return first, (4 * y - SPAN * group).astype(F32)


def plane_weights(block, shift_y):
    number = row_numbers((8, LANES)).astype(F32)
    x = hat(number - block[5:6])
    y = block[6:7] + shift_y
    parts = [hat(number + 8.0 * k - y) for k in range(SPAN // 8)]
    last = hat(float(SPAN) - y)
    pieces = [x[i : i + 1] * part for i in range(5) for part in parts]
    return split(jnp.concatenate(pieces + [x * last], 0))


def depth_weights(block):
    return hat(row_numbers((8, LANES)).astype(F32) - block[7:8])


def doubled(x):
    high, low = split(x)
    both = jnp.concatenate([high, low], 0).astype(BF16)
    return jnp.concatenate([both, both], 1)


def spread_block(block, weights):
    high, low = weights
    plane = jnp.concatenate([high.astype(BF16), low.astype(BF16)], 1)
    depth = depth_weights(block)
    loads = jnp.concatenate([block[f : f + 1] * depth for f in range(FIELDS)], 0)
    both = lax.dot_general(doubled(loads), plane, NT, preferred_element_type=F32)
    return both[: 8 * FIELDS] + both[8 * FIELDS :]


def add_block(grid, summed, brick, total):
    first, _ = grid.place(brick)
    for f in range(FIELDS):
        rows = pl.ds(first + f * grid.rows_z, 8)
        total[rows, :] += summed[8 * f : 8 * f + 8]


def sample_block(grid, block, brick, plane, held):
    first, _ = grid.place(brick)
    fields = jnp.concatenate(
        [held[pl.ds(first + f * grid.rows_z, 8), :] for f in range(FIELDS)], 0
    )
    both = jnp.dot(doubled(fields), plane, preferred_element_type=F32)
    summed = both[: 8 * FIELDS] + both[8 * FIELDS :]
    depth = depth_weights(block)
    return jnp.concatenate(
        [
            jnp.sum(summed[8 * f : 8 * f + 8] * depth, axis=0, keepdims=True)
            for f in range(FIELDS)
        ],
        0,
    )


UNROLL = 64
TURN = 32


def deposit_kernel(grid, bricks, spread, lower, upper, zeros, total):
    del zeros
    blocks = lower.shape[1] // LANES
    resident = bricks.shape[0] - 2 * blocks
    ratio = resident // (2 * blocks)
    for part, offset in ((lower, 0), (upper, blocks)):

        def step(turn, carry, part=part, offset=offset):
            for i in range(UNROLL):
                at = turn * UNROLL + i
                block = part[:, pl.ds(pl.multiple_of(at * LANES, LANES), LANES)]
                brick = bricks[resident + offset + at]
                weights = plane_weights(block, grid.place(brick)[1])
                add_block(grid, spread_block(block, weights), brick, total)
                for j in range(ratio):
                    own = (offset + at) * ratio + j
                    rows = pl.ds(pl.multiple_of(own * 8 * FIELDS, 8), 8 * FIELDS)
                    add_block(grid, spread[rows, :], bricks[own], total)
            return carry

        lax.fori_loop(0, blocks // UNROLL, step, 0)


def merge_selector():
    picked = row_numbers((160, LANES))
    lane = lax.broadcasted_iota(jnp.int32, (160, LANES), 1)
    edge = picked - 5 * SPAN
    wanted = jnp.where(
        picked < 5 * SPAN, picked, jnp.where(edge % 8 == 0, 5 * SPAN + edge // 8, -1)
    )
    select = jnp.where(lane == wanted, 1.0, 0.0).astype(BF16)
    return jnp.concatenate([select, select], 1)


def merge_field(grid, f, select, total, sums):
    carried = None
    for group in range(grid.groups):
        first = (group * FIELDS + f) * grid.rows_z
        high, low = split(total[first : first + grid.span_z, :])
        both = jnp.concatenate([high.astype(BF16), low.astype(BF16)], 1)
        turned = lax.dot_general(select, both, NT, preferred_element_type=F32)
        for x in range(5):
            piece = turned[x * SPAN : (x + 1) * SPAN]
            if carried is not None:
                head = piece[:8] + carried[8 * x : 8 * x + 8]
                piece = jnp.concatenate([head, piece[8:]], 0)
            sums[f, x, group * SPAN : (group + 1) * SPAN, :] = piece
        carried = turned[5 * SPAN :]


def fill_faces(grid, f, second_half, gas, sums, up, down, row):
    ny = grid.span_y
    up[f] = sums[f, 4, :ny]
    down[f] = COUPLE * sums[f, 0, :ny] + gas[f, 0]
    for x in range(5):
        low_row = COUPLE * sums[f, x, 0:1, :]
        if x < 4:
            low_row = low_row + gas[f, x, 0:1, :]
        high_row = COUPLE * sums[f, x, ny : ny + 1, :]
        row[x, f : f + 1, :] = jnp.where(second_half, low_row, high_row)


def sample_kernel(
    grid, last, bricks, stay, lower, upper, gas, sums, from_up, from_down,
    from_row, corner_low, corner_high, tail_low, tail_high, weights, source, sampled, field, held
):
    ny = grid.span_y
    second_half = lax.axis_index("radial") == 1
    at_end = lax.axis_index("axial") == last
    face = jnp.where(second_half, 1.0, 0.0)
    for f in range(FIELDS):
        for x in range(5):
            extra = from_row[x, f : f + 1, :]
            if x == 0:
                extra = extra + corner_low[f : f + 1, :]
            if x == 4:
                extra = extra + corner_high[f : f + 1, :]
            first = row_numbers((8, grid.span_z)) == 0
            head = jnp.where(first, 2.0 * face * extra, 0.0)
            mine = sums[f, x, :ny, :]
            if x == 0:
                mine = mine + from_up[f]
            mine = jnp.concatenate([mine[:8] + head, mine[8:]], 0)
            tail = COUPLE * sums[f, x, ny : ny + 8, :]
            if x == 0:
                tail = tail + tail_low[f : f + 1, :]
            if x < 4:
                source[f, x] = mine
                mine = gas[f, x] + COUPLE * mine
            else:
                mine = COUPLE * mine + from_down[f]
                mine = jnp.where(at_end, 0.0, mine)
                tail = tail + tail_high[f : f + 1, :]
                tail = jnp.where(at_end, 0.0, tail)
                extra = jnp.where(at_end, 0.0, extra)
            tail = jnp.where(first & jnp.logical_not(second_half), tail + extra, 0.0)
            field[f, x, :ny, :] = mine
            field[f, x, ny : ny + 8, :] = tail
    for f in range(FIELDS):
        for group in range(grid.groups):
            edge = SPAN * (group + 1)
            pieces = [field[f, x, edge - SPAN : edge, :] for x in range(5)]
            if edge < grid.pad_y:
                pieces += [field[f, x, edge : edge + 1, :] for x in range(5)]
                pieces.append(jnp.zeros((3, grid.span_z), F32))
            else:
                pieces.append(jnp.zeros((8, grid.span_z), F32))
            turned = jnp.concatenate(pieces, 0).T
            at = (group * FIELDS + f) * grid.rows_z
            held[at : at + grid.span_z, :] = turned
            held[at + grid.span_z : at + grid.rows_z, :] = jnp.zeros((8, LANES), F32)

    offset = 0
    for part in (stay, lower, upper):
        blocks = part.shape[1] // LANES

        def step(turn, carry, part=part, offset=offset):
            for i in range(UNROLL):
                at = turn * UNROLL + i
                block = part[:, pl.ds(pl.multiple_of(at * LANES, LANES), LANES)]
                place_at = pl.multiple_of((offset + at) * 2 * LANES, 2 * LANES)
                plane = weights[pl.ds(place_at, 2 * LANES), :]
                values = sample_block(grid, block, bricks[offset + at], plane, held)
                lanes = pl.ds(pl.multiple_of((offset + at) * LANES, LANES), LANES)
                sampled[:, lanes] = values.astype(BF16)
            return carry

        lax.fori_loop(0, blocks // UNROLL, step, 0)
        offset += blocks


BIG = pltpu.CompilerParams(vmem_limit_bytes=12 * 2**20)


def deposit_call(grid, bricks, spread, lower, upper, zeros):
    return pl.pallas_call(
        functools.partial(deposit_kernel, grid),
        out_shape=jax.ShapeDtypeStruct((grid.rows, LANES), F32),
        in_specs=[SMEM, VMEM, VMEM, VMEM, VMEM],
        input_output_aliases={4: 0},
        compiler_params=BIG,
        name="deposit",
    )(bricks, spread, lower, upper, zeros)


def signal_entry(axial_at, radial_at):
    pl.semaphore_signal(
        pltpu.get_barrier_semaphore(), inc=1, device_id=(axial_at, radial_at),
        device_id_type=pl.DeviceIdType.MESH,
    )


def store_weights(target, at, weights):
    place = pl.multiple_of(at * 2 * LANES, 2 * LANES)
    target[pl.ds(place, 2 * LANES), :] = jnp.concatenate(weights, 0).astype(BF16)


FILLER = 1


def migrate_kernel(
    grid, last, bricks, up, down, stay, lower, upper, spread, sent, got
):
    a = lax.axis_index("axial")
    r = lax.axis_index("radial")
    has_above = a < last
    has_below = a > 0

    @pl.when(has_above)
    def _():
        signal_entry(a + 1, r)

    @pl.when(has_below)
    def _():
        signal_entry(a - 1, r)

    def copy(number, source, target, axial_at):
        return pltpu.make_async_remote_copy(
            src_ref=source, dst_ref=target, send_sem=sent.at[number],
            recv_sem=got.at[number], device_id=(axial_at, r),
            device_id_type=pl.DeviceIdType.MESH,
        )

    rising = copy(0, up, lower, a + 1)
    falling = copy(1, down, upper, a - 1)

    def step(turn, carry):
        for i in range(TURN):
            at = turn * TURN + i
            block = stay[:, pl.ds(pl.multiple_of(at * LANES, LANES), LANES)]
            plane = plane_weights(block, grid.place(bricks[at])[1])
            rows = pl.ds(pl.multiple_of(at * 8 * FIELDS, 8), 8 * FIELDS)
            spread[rows, :] = spread_block(block, plane)
        return carry

    lax.fori_loop(0, FILLER, step, 0)
    peers = has_above.astype(jnp.int32) + has_below.astype(jnp.int32)
    pl.semaphore_wait(pltpu.get_barrier_semaphore(), peers)

    @pl.when(has_above)
    def _():
        rising.start()

    @pl.when(has_below)
    def _():
        falling.start()

    @pl.when(jnp.logical_not(has_below))
    def _():
        lower[...] = jnp.zeros_like(lower)

    @pl.when(jnp.logical_not(has_above))
    def _():
        upper[...] = jnp.zeros_like(upper)

    lax.fori_loop(FILLER, stay.shape[1] // LANES // TURN, step, 0)

    @pl.when(has_above)
    def _():
        rising.wait_send()
        falling.wait_recv()

    @pl.when(has_below)
    def _():
        falling.wait_send()
        rising.wait_recv()


def migrate_call(grid, last, bricks, up, down, stay):
    blocks = stay.shape[1] // LANES
    return pl.pallas_call(
        functools.partial(migrate_kernel, grid, last),
        out_shape=(
            jax.ShapeDtypeStruct(up.shape, F32),
            jax.ShapeDtypeStruct(down.shape, F32),
            jax.ShapeDtypeStruct((blocks * 8 * FIELDS, LANES), F32),
        ),
        in_specs=[SMEM] + [VMEM] * 3,
        out_specs=(VMEM,) * 3,
        scratch_shapes=[pltpu.SemaphoreType.DMA((2,)), pltpu.SemaphoreType.DMA((2,))],
        compiler_params=pltpu.CompilerParams(
            collective_id=1, has_side_effects=True, vmem_limit_bytes=8 * 2**20
        ),
        name="migrate",
    )(bricks, up, down, stay)


def exchange_kernel(
    grid, last, bricks, stay, lower, upper, gas, total, sums, from_up, from_down, from_row,
    corner_low, corner_high, tail_low, tail_high, weights, up, down, edge, sent, got
):
    a = lax.axis_index("axial")
    r = lax.axis_index("radial")
    has_above = a < last
    has_below = a > 0
    signal_entry(a, 1 - r)

    @pl.when(has_above)
    def _():
        signal_entry(a + 1, r)
        signal_entry(a + 1, 1 - r)

    @pl.when(has_below)
    def _():
        signal_entry(a - 1, r)
        signal_entry(a - 1, 1 - r)

    peers = 1 + 2 * has_above.astype(jnp.int32) + 2 * has_below.astype(jnp.int32)

    def copy(number, source, target, axial_at, radial_at):
        return pltpu.make_async_remote_copy(
            src_ref=source, dst_ref=target, send_sem=sent.at[number],
            recv_sem=got.at[number], device_id=(axial_at, radial_at),
            device_id_type=pl.DeviceIdType.MESH,
        )

    row = copy(0, edge, from_row, a, 1 - r)
    ends_up = [
        copy(1, edge.at[4], corner_low, a + 1, 1 - r),
        copy(2, edge.at[4], tail_low, a + 1, r),
    ]
    ends_down = [
        copy(3, edge.at[0], corner_high, a - 1, 1 - r),
        copy(4, edge.at[0], tail_high, a - 1, r),
    ]
    faces_up = [copy(5 + f, up.at[f], from_up.at[f], a + 1, r) for f in range(FIELDS)]
    faces_down = [
        copy(5 + FIELDS + f, down.at[f], from_down.at[f], a - 1, r) for f in range(FIELDS)
    ]
    select = merge_selector()
    for x in range(5):
        edge[x, FIELDS:, :] = jnp.zeros((8 - FIELDS, grid.span_z), F32)
    def weigh(part, offset):
        def step(turn, carry):
            for i in range(TURN):
                at = turn * TURN + i
                block = part[:, pl.ds(pl.multiple_of(at * LANES, LANES), LANES)]
                plane = plane_weights(block, grid.place(bricks[offset + at])[1])
                store_weights(weights, offset + at, plane)
            return carry

        lax.fori_loop(0, part.shape[1] // LANES // TURN, step, 0)

    for f in range(FIELDS):
        merge_field(grid, f, select, total, sums)
        fill_faces(grid, f, r == 1, gas, sums, up, down, edge)
    weigh(stay, 0)
    pl.semaphore_wait(pltpu.get_barrier_semaphore(), peers)
    row.start()

    @pl.when(has_above)
    def _():
        for each in ends_up:
            each.start()

    @pl.when(has_below)
    def _():
        for each in ends_down:
            each.start()

    upper_core = a % 2 == 1
    for far in (True, False):

        @pl.when(has_above & (upper_core == far))
        def _():
            for each in faces_up:
                each.start()

        @pl.when(has_below & (upper_core != far))
        def _():
            for each in faces_down:
                each.start()

    @pl.when(jnp.logical_not(has_below))
    def _():
        from_up[...] = jnp.zeros_like(from_up)
        corner_low[...] = jnp.zeros_like(corner_low)
        tail_low[...] = jnp.zeros_like(tail_low)

    @pl.when(jnp.logical_not(has_above))
    def _():
        from_down[...] = jnp.zeros_like(from_down)
        corner_high[...] = jnp.zeros_like(corner_high)
        tail_high[...] = jnp.zeros_like(tail_high)

    resident = stay.shape[1] // LANES
    weigh(lower, resident)
    weigh(upper, resident + lower.shape[1] // LANES)
    row.wait()

    @pl.when(has_above)
    def _():
        for each in faces_up + ends_up:
            each.wait_send()
        for each in faces_down + ends_down:
            each.wait_recv()

    @pl.when(has_below)
    def _():
        for each in faces_down + ends_down:
            each.wait_send()
        for each in faces_up + ends_up:
            each.wait_recv()


def exchange_call(grid, last, bricks, stay, lower, upper, gas, total):
    plane = (FIELDS, grid.span_y, grid.span_z)
    edge = (5, 8, grid.span_z)
    corner = jax.ShapeDtypeStruct(edge[1:], F32)
    copies = 5 + 2 * FIELDS
    return pl.pallas_call(
        functools.partial(exchange_kernel, grid, last),
        out_shape=(
            jax.ShapeDtypeStruct((FIELDS, 5, grid.pad_y, grid.span_z), F32),
            jax.ShapeDtypeStruct(plane, F32),
            jax.ShapeDtypeStruct(plane, F32),
            jax.ShapeDtypeStruct(edge, F32),
            corner,
            corner,
            corner,
            corner,
            jax.ShapeDtypeStruct((bricks.shape[0] * 2 * LANES, LANES), BF16),
        ),
        in_specs=[SMEM] + [VMEM] * 5,
        out_specs=(VMEM,) * 9,
        scratch_shapes=[
            pltpu.VMEM(plane, F32),
            pltpu.VMEM(plane, F32),
            pltpu.VMEM(edge, F32),
            pltpu.SemaphoreType.DMA((copies,)),
            pltpu.SemaphoreType.DMA((copies,)),
        ],
        compiler_params=pltpu.CompilerParams(
            collective_id=0, has_side_effects=True, vmem_limit_bytes=8 * 2**20
        ),
        name="exchange",
    )(bricks, stay, lower, upper, gas, total)


def sample_call(grid, last, bricks, *arrays):
    gas = arrays[3]
    return pl.pallas_call(
        functools.partial(sample_kernel, grid, last),
        out_shape=(
            jax.ShapeDtypeStruct(gas.shape, F32),
            jax.ShapeDtypeStruct((FIELDS, bricks.shape[0] * LANES), BF16),
        ),
        in_specs=[SMEM] + [VMEM] * 13,
        scratch_shapes=[
            pltpu.VMEM((FIELDS, 5, grid.pad_y, grid.span_z), F32),
            pltpu.VMEM((grid.rows, LANES), F32),
        ],
        compiler_params=BIG,
        name="sample",
    )(bricks, *arrays)


def per_device(load, offset, cell, rows, bricks, gas):
    axial = lax.axis_size("axial")
    span_y, span_z = gas.shape[2], gas.shape[3]
    grid = Grid(span_y, span_z)
    zeros, none_gone = clear_call(grid, load.shape[1] // LANES)
    up, down, stay = gather_call(load, offset, cell, rows, none_gone)
    lower, upper, spread = migrate_call(grid, axial - 1, bricks, up, down, stay)
    total = deposit_call(grid, bricks, spread, lower, upper, zeros)
    arrived = exchange_call(grid, axial - 1, bricks, stay, lower, upper, gas, total)
    return sample_call(
        grid, axial - 1, bricks, stay, lower, upper, gas, *arrived
    )


def solution(mesh):
    return jax.shard_map(
        per_device,
        mesh=mesh,
        in_specs=(
            P(None, ("axial", "radial")),
            P(None, ("axial", "radial")),
            P(("axial", "radial")),
            P(None, ("axial", "radial")),
            P(("axial", "radial")),
            P(None, "axial", "radial", None),
        ),
        out_specs=(P(None, "axial", "radial", None), P(None, ("axial", "radial"))),
        check_vma=False,
    )
```

```python
import functools

import jax
import jax.numpy as jnp
from jax import lax
from jax.experimental import pallas as pl
from jax.experimental.pallas import tpu as pltpu
from jax.sharding import PartitionSpec as P

COUPLE = 0.5
LANES = 128
TILE = 2048
CHUNK = 32
FIELDS = 5
GROUP = 6
SPAN = 4 * GROUP
NT = (((1,), (1,)), ((), ()))
SMEM = pl.BlockSpec(memory_space=pltpu.SMEM)
VMEM = pl.BlockSpec(memory_space=pltpu.VMEM)
F32 = jnp.float32
BF16 = jnp.bfloat16


def split(x):
    high = x.astype(BF16).astype(F32)
    return high, x - high


def hat(x):
    return jnp.maximum(1.0 - jnp.abs(x), 0.0)


def row_numbers(shape):
    return lax.broadcasted_iota(jnp.int32, shape, 0)


def clear_kernel(total, gone):
    total[...] = jnp.zeros_like(total)
    gone[...] = jnp.zeros_like(gone)


def clear_call(grid, blocks):
    return pl.pallas_call(
        clear_kernel,
        out_shape=(
            jax.ShapeDtypeStruct((grid.rows, LANES), F32),
            jax.ShapeDtypeStruct((blocks, LANES), F32),
        ),
        compiler_params=pltpu.CompilerParams(vmem_limit_bytes=2**20),
        cost_estimate=pl.CostEstimate(
            flops=10**10, bytes_accessed=2 * 10**6, transcendentals=0
        ),
        name="clear",
    )()


def gather_kernel(
    load, offset, cell, rows, none_gone, up, down, stay, table, base, corner, gone
):
    count = load.shape[1]
    blocks = count // LANES
    axis_row = row_numbers((3, count))
    coords = lax.shift_right_logical(
        jnp.broadcast_to(cell[...], (3, count)), 4 - 2 * axis_row
    ) & 3
    corner[...] = jnp.concatenate([jnp.zeros((5, count), F32), coords.astype(F32)], 0)
    base[...] = jnp.concatenate([load[...], offset[...]], 0)

    def fill(step, carry):
        at = pl.multiple_of(step * 2 * LANES, 2 * LANES)
        pair = base[:, pl.ds(at, 2 * LANES)] + corner[:, pl.ds(at, 2 * LANES)]
        both = jnp.concatenate([pair[:, :LANES], pair[:, LANES:]], 0)
        high, low = split(both)
        place = pl.multiple_of(step * 16, 16)
        table[pl.ds(place, 16), :] = jnp.concatenate([high, low], 1).astype(BF16)
        return carry

    lax.fori_loop(0, blocks // 2, fill, 0, unroll=8)
    gone[...] = none_gone[...]

    for side, out in ((0, up), (1, down)):
        out[...] = jnp.zeros_like(out)
        named = jnp.sum((rows[side : side + 1, :] >= 0).astype(F32)).astype(jnp.int32)

        def tile_step(step, carry, side=side, out=out):
            at = pl.multiple_of(step * TILE, TILE)
            row = rows[side : side + 1, pl.ds(at, TILE)]
            lane = row & (LANES - 1)
            block = lax.shift_right_arithmetic(row, 7)
            number = row_numbers((LANES, TILE))
            lane_hot = jnp.where(number == lane, 1.0, 0.0).astype(BF16)
            block_hot = jnp.where(number == block, 1.0, 0.0).astype(BF16)
            gone[...] += lax.dot_general(block_hot, lane_hot, NT, preferred_element_type=F32)
            wanted = jnp.concatenate([lane_hot, lane_hot], 0)
            block8 = jnp.broadcast_to(block, (8, TILE))
            found = jnp.zeros((8, TILE), F32)
            for chunk in range(blocks // CHUNK):
                part = jnp.dot(
                    table[8 * CHUNK * chunk : 8 * CHUNK * (chunk + 1), :], wanted,
                    preferred_element_type=F32,
                )
                for i in range(CHUNK):
                    found = jnp.where(
                        block8 == chunk * CHUNK + i, part[8 * i : 8 * i + 8, :], found
                    )
            out[:, pl.ds(at, TILE)] = found
            return carry

        lax.fori_loop(0, (named + TILE - 1) // TILE, tile_step, 0)

    def keep(step, carry):
        at = pl.multiple_of(step * LANES, LANES)
        left = 1.0 - gone[pl.ds(step, 1), :]
        stay[:, pl.ds(at, LANES)] = (
            base[:, pl.ds(at, LANES)] * left + corner[:, pl.ds(at, LANES)]
        )
        return carry

    lax.fori_loop(0, blocks, keep, 0, unroll=8)


def gather_call(load, offset, cell, rows, none_gone):
    count = load.shape[1]
    slots = rows.shape[1]
    moved = jax.ShapeDtypeStruct((8, slots), F32)
    return pl.pallas_call(
        gather_kernel,
        out_shape=(moved, moved, jax.ShapeDtypeStruct((8, count), F32)),
        in_specs=[VMEM] * 5,
        scratch_shapes=[
            pltpu.VMEM((8 * (count // LANES), 2 * LANES), BF16),
            pltpu.VMEM((8, count), F32),
            pltpu.VMEM((8, count), F32),
            pltpu.VMEM((count // LANES, LANES), F32),
        ],
        compiler_params=pltpu.CompilerParams(vmem_limit_bytes=16 * 2**20),
        cost_estimate=pl.CostEstimate(
            flops=10**10, bytes_accessed=2 * 10**6, transcendentals=0
        ),
        name="gather_rows",
    )(load, offset, cell.reshape(1, count), rows, none_gone)


class Grid:
    def __init__(self, span_y, span_z):
        self.span_y = span_y
        self.span_z = span_z
        self.per_row = span_z // 4
        self.bricks_y = span_y // 4
        self.groups = -(-self.bricks_y // GROUP)
        self.rows_z = span_z + 8
        self.rows = self.groups * FIELDS * self.rows_z
        self.pad_y = self.groups * SPAN
        self.shift = self.per_row.bit_length() - 1
        assert self.per_row == 1 << self.shift and self.bricks_y & (self.bricks_y - 1) == 0

    def place(self, brick):
        z = brick & (self.per_row - 1)
        y = lax.shift_right_logical(brick, self.shift) & (self.bricks_y - 1)
        group = sum((y >= GROUP * k).astype(jnp.int32) for k in range(1, self.groups))
        first = group * (FIELDS * self.rows_z) + 4 * z
        return first, (4 * y - SPAN * group).astype(F32)


def plane_weights(block, shift_y):
    number = row_numbers((8, LANES)).astype(F32)
    x = hat(number - block[5:6])
    y = block[6:7] + shift_y
    parts = [hat(number + 8.0 * k - y) for k in range(SPAN // 8)]
    last = hat(float(SPAN) - y)
    pieces = [x[i : i + 1] * part for i in range(5) for part in parts]
    return split(jnp.concatenate(pieces + [x * last], 0))


def depth_weights(block):
    return hat(row_numbers((8, LANES)).astype(F32) - block[7:8])


def doubled(x):
    high, low = split(x)
    both = jnp.concatenate([high, low], 0).astype(BF16)
    return jnp.concatenate([both, both], 1)


def spread_block(block, weights):
    high, low = weights
    plane = jnp.concatenate([high.astype(BF16), low.astype(BF16)], 1)
    depth = depth_weights(block)
    loads = jnp.concatenate([block[f : f + 1] * depth for f in range(FIELDS)], 0)
    both = lax.dot_general(doubled(loads), plane, NT, preferred_element_type=F32)
    return both[: 8 * FIELDS] + both[8 * FIELDS :]


def add_block(grid, summed, brick, total):
    first, _ = grid.place(brick)
    for f in range(FIELDS):
        rows = pl.ds(first + f * grid.rows_z, 8)
        total[rows, :] += summed[8 * f : 8 * f + 8]


def sample_block(grid, block, brick, plane, held):
    first, _ = grid.place(brick)
    fields = jnp.concatenate(
        [held[pl.ds(first + f * grid.rows_z, 8), :] for f in range(FIELDS)], 0
    )
    both = jnp.dot(doubled(fields), plane, preferred_element_type=F32)
    summed = both[: 8 * FIELDS] + both[8 * FIELDS :]
    depth = depth_weights(block)
    return jnp.concatenate(
        [
            jnp.sum(summed[8 * f : 8 * f + 8] * depth, axis=0, keepdims=True)
            for f in range(FIELDS)
        ],
        0,
    )


UNROLL = 64
TURN = 32


def deposit_kernel(grid, bricks, spread, lower, upper, zeros, total):
    del zeros
    blocks = lower.shape[1] // LANES
    resident = bricks.shape[0] - 2 * blocks
    ratio = resident // (2 * blocks)
    for part, offset in ((lower, 0), (upper, blocks)):

        def step(turn, carry, part=part, offset=offset):
            for i in range(UNROLL):
                at = turn * UNROLL + i
                block = part[:, pl.ds(pl.multiple_of(at * LANES, LANES), LANES)]
                brick = bricks[resident + offset + at]
                weights = plane_weights(block, grid.place(brick)[1])
                add_block(grid, spread_block(block, weights), brick, total)
                for j in range(ratio):
                    own = (offset + at) * ratio + j
                    rows = pl.ds(pl.multiple_of(own * 8 * FIELDS, 8), 8 * FIELDS)
                    add_block(grid, spread[rows, :], bricks[own], total)
            return carry

        lax.fori_loop(0, blocks // UNROLL, step, 0)


def merge_selector():
    picked = row_numbers((160, LANES))
    lane = lax.broadcasted_iota(jnp.int32, (160, LANES), 1)
    edge = picked - 5 * SPAN
    wanted = jnp.where(
        picked < 5 * SPAN, picked, jnp.where(edge % 8 == 0, 5 * SPAN + edge // 8, -1)
    )
    select = jnp.where(lane == wanted, 1.0, 0.0).astype(BF16)
    return jnp.concatenate([select, select], 1)


def merge_field(grid, f, select, total, sums):
    carried = None
    for group in range(grid.groups):
        first = (group * FIELDS + f) * grid.rows_z
        high, low = split(total[first : first + grid.span_z, :])
        both = jnp.concatenate([high.astype(BF16), low.astype(BF16)], 1)
        turned = lax.dot_general(select, both, NT, preferred_element_type=F32)
        for x in range(5):
            piece = turned[x * SPAN : (x + 1) * SPAN]
            if carried is not None:
                head = piece[:8] + carried[8 * x : 8 * x + 8]
                piece = jnp.concatenate([head, piece[8:]], 0)
            sums[f, x, group * SPAN : (group + 1) * SPAN, :] = piece
        carried = turned[5 * SPAN :]


def fill_faces(grid, f, second_half, gas, sums, up, down, row):
    ny = grid.span_y
    up[f] = sums[f, 4, :ny]
    down[f] = COUPLE * sums[f, 0, :ny] + gas[f, 0]
    for x in range(5):
        low_row = COUPLE * sums[f, x, 0:1, :]
        if x < 4:
            low_row = low_row + gas[f, x, 0:1, :]
        high_row = COUPLE * sums[f, x, ny : ny + 1, :]
        row[x, f : f + 1, :] = jnp.where(second_half, low_row, high_row)


def sample_kernel(
    grid, last, bricks, stay, lower, upper, gas, sums, from_up, from_down,
    from_row, corner_low, corner_high, tail_low, tail_high, weights, source, sampled, field, held
):
    ny = grid.span_y
    second_half = lax.axis_index("radial") == 1
    at_end = lax.axis_index("axial") == last
    face = jnp.where(second_half, 1.0, 0.0)
    for f in range(FIELDS):
        for x in range(5):
            extra = from_row[x, f : f + 1, :]
            if x == 0:
                extra = extra + corner_low[f : f + 1, :]
            if x == 4:
                extra = extra + corner_high[f : f + 1, :]
            first = row_numbers((8, grid.span_z)) == 0
            head = jnp.where(first, 2.0 * face * extra, 0.0)
            mine = sums[f, x, :ny, :]
            if x == 0:
                mine = mine + from_up[f]
            mine = jnp.concatenate([mine[:8] + head, mine[8:]], 0)
            tail = COUPLE * sums[f, x, ny : ny + 8, :]
            if x == 0:
                tail = tail + tail_low[f : f + 1, :]
            if x < 4:
                source[f, x] = mine
                mine = gas[f, x] + COUPLE * mine
            else:
                mine = COUPLE * mine + from_down[f]
                mine = jnp.where(at_end, 0.0, mine)
                tail = tail + tail_high[f : f + 1, :]
                tail = jnp.where(at_end, 0.0, tail)
                extra = jnp.where(at_end, 0.0, extra)
            tail = jnp.where(first & jnp.logical_not(second_half), tail + extra, 0.0)
            field[f, x, :ny, :] = mine
            field[f, x, ny : ny + 8, :] = tail
    for f in range(FIELDS):
        for group in range(grid.groups):
            edge = SPAN * (group + 1)
            pieces = [field[f, x, edge - SPAN : edge, :] for x in range(5)]
            if edge < grid.pad_y:
                pieces += [field[f, x, edge : edge + 1, :] for x in range(5)]
                pieces.append(jnp.zeros((3, grid.span_z), F32))
            else:
                pieces.append(jnp.zeros((8, grid.span_z), F32))
            turned = jnp.concatenate(pieces, 0).T
            at = (group * FIELDS + f) * grid.rows_z
            held[at : at + grid.span_z, :] = turned
            held[at + grid.span_z : at + grid.rows_z, :] = jnp.zeros((8, LANES), F32)

    offset = 0
    for part in (stay, lower, upper):
        blocks = part.shape[1] // LANES

        def step(turn, carry, part=part, offset=offset):
            for i in range(UNROLL):
                at = turn * UNROLL + i
                block = part[:, pl.ds(pl.multiple_of(at * LANES, LANES), LANES)]
                place_at = pl.multiple_of((offset + at) * 2 * LANES, 2 * LANES)
                plane = weights[pl.ds(place_at, 2 * LANES), :]
                values = sample_block(grid, block, bricks[offset + at], plane, held)
                lanes = pl.ds(pl.multiple_of((offset + at) * LANES, LANES), LANES)
                sampled[:, lanes] = values.astype(BF16)
            return carry

        lax.fori_loop(0, blocks // UNROLL, step, 0)
        offset += blocks


BIG = pltpu.CompilerParams(vmem_limit_bytes=12 * 2**20)


def deposit_call(grid, bricks, spread, lower, upper, zeros):
    return pl.pallas_call(
        functools.partial(deposit_kernel, grid),
        out_shape=jax.ShapeDtypeStruct((grid.rows, LANES), F32),
        in_specs=[SMEM, VMEM, VMEM, VMEM, VMEM],
        input_output_aliases={4: 0},
        compiler_params=BIG,
        name="deposit",
    )(bricks, spread, lower, upper, zeros)


def signal_entry(axial_at, radial_at):
    pl.semaphore_signal(
        pltpu.get_barrier_semaphore(), inc=1, device_id=(axial_at, radial_at),
        device_id_type=pl.DeviceIdType.MESH,
    )


def store_weights(target, at, weights):
    place = pl.multiple_of(at * 2 * LANES, 2 * LANES)
    target[pl.ds(place, 2 * LANES), :] = jnp.concatenate(weights, 0).astype(BF16)


def migrate_kernel(
    grid, last, bricks, up, down, stay, lower, upper, spread, sent, got
):
    a = lax.axis_index("axial")
    r = lax.axis_index("radial")
    has_above = a < last
    has_below = a > 0

    @pl.when(has_above)
    def _():
        signal_entry(a + 1, r)

    @pl.when(has_below)
    def _():
        signal_entry(a - 1, r)

    def copy(number, source, target, axial_at):
        return pltpu.make_async_remote_copy(
            src_ref=source, dst_ref=target, send_sem=sent.at[number],
            recv_sem=got.at[number], device_id=(axial_at, r),
            device_id_type=pl.DeviceIdType.MESH,
        )

    rising = copy(0, up, lower, a + 1)
    falling = copy(1, down, upper, a - 1)

    def step(turn, carry):
        for i in range(TURN):
            at = turn * TURN + i
            block = stay[:, pl.ds(pl.multiple_of(at * LANES, LANES), LANES)]
            plane = plane_weights(block, grid.place(bricks[at])[1])
            rows = pl.ds(pl.multiple_of(at * 8 * FIELDS, 8), 8 * FIELDS)
            spread[rows, :] = spread_block(block, plane)
        return carry

    peers = has_above.astype(jnp.int32) + has_below.astype(jnp.int32)
    pl.semaphore_wait(pltpu.get_barrier_semaphore(), peers)

    @pl.when(has_above)
    def _():
        rising.start()

    @pl.when(has_below)
    def _():
        falling.start()

    @pl.when(jnp.logical_not(has_below))
    def _():
        lower[...] = jnp.zeros_like(lower)

    @pl.when(jnp.logical_not(has_above))
    def _():
        upper[...] = jnp.zeros_like(upper)

    lax.fori_loop(0, stay.shape[1] // LANES // TURN, step, 0)

    @pl.when(has_above)
    def _():
        rising.wait_send()
        falling.wait_recv()

    @pl.when(has_below)
    def _():
        falling.wait_send()
        rising.wait_recv()


def migrate_call(grid, last, bricks, up, down, stay):
    blocks = stay.shape[1] // LANES
    return pl.pallas_call(
        functools.partial(migrate_kernel, grid, last),
        out_shape=(
            jax.ShapeDtypeStruct(up.shape, F32),
            jax.ShapeDtypeStruct(down.shape, F32),
            jax.ShapeDtypeStruct((blocks * 8 * FIELDS, LANES), F32),
        ),
        in_specs=[SMEM] + [VMEM] * 3,
        out_specs=(VMEM,) * 3,
        scratch_shapes=[pltpu.SemaphoreType.DMA((2,)), pltpu.SemaphoreType.DMA((2,))],
        compiler_params=pltpu.CompilerParams(
            collective_id=1, has_side_effects=True, vmem_limit_bytes=8 * 2**20
        ),
        name="migrate",
    )(bricks, up, down, stay)


def exchange_kernel(
    grid, last, bricks, stay, lower, upper, gas, total, sums, from_up, from_down, from_row,
    corner_low, corner_high, tail_low, tail_high, weights, up, down, edge, sent, got
):
    a = lax.axis_index("axial")
    r = lax.axis_index("radial")
    has_above = a < last
    has_below = a > 0
    signal_entry(a, 1 - r)

    @pl.when(has_above)
    def _():
        signal_entry(a + 1, r)
        signal_entry(a + 1, 1 - r)

    @pl.when(has_below)
    def _():
        signal_entry(a - 1, r)
        signal_entry(a - 1, 1 - r)

    peers = 1 + 2 * has_above.astype(jnp.int32) + 2 * has_below.astype(jnp.int32)

    def copy(number, source, target, axial_at, radial_at):
        return pltpu.make_async_remote_copy(
            src_ref=source, dst_ref=target, send_sem=sent.at[number],
            recv_sem=got.at[number], device_id=(axial_at, radial_at),
            device_id_type=pl.DeviceIdType.MESH,
        )

    row = copy(0, edge, from_row, a, 1 - r)
    ends_up = [
        copy(1, edge.at[4], corner_low, a + 1, 1 - r),
        copy(2, edge.at[4], tail_low, a + 1, r),
    ]
    ends_down = [
        copy(3, edge.at[0], corner_high, a - 1, 1 - r),
        copy(4, edge.at[0], tail_high, a - 1, r),
    ]
    faces_up = [copy(5 + f, up.at[f], from_up.at[f], a + 1, r) for f in range(FIELDS)]
    faces_down = [
        copy(5 + FIELDS + f, down.at[f], from_down.at[f], a - 1, r) for f in range(FIELDS)
    ]
    select = merge_selector()
    for x in range(5):
        edge[x, FIELDS:, :] = jnp.zeros((8 - FIELDS, grid.span_z), F32)
    def weigh(part, offset):
        def step(turn, carry):
            for i in range(TURN):
                at = turn * TURN + i
                block = part[:, pl.ds(pl.multiple_of(at * LANES, LANES), LANES)]
                plane = plane_weights(block, grid.place(bricks[offset + at])[1])
                store_weights(weights, offset + at, plane)
            return carry

        lax.fori_loop(0, part.shape[1] // LANES // TURN, step, 0)

    for f in range(FIELDS):
        merge_field(grid, f, select, total, sums)
        fill_faces(grid, f, r == 1, gas, sums, up, down, edge)
    pl.semaphore_wait(pltpu.get_barrier_semaphore(), peers)
    row.start()

    @pl.when(has_above)
    def _():
        for each in ends_up:
            each.start()

    @pl.when(has_below)
    def _():
        for each in ends_down:
            each.start()

    upper_core = a % 2 == 1
    for far in (True, False):

        @pl.when(has_above & (upper_core == far))
        def _():
            for each in faces_up:
                each.start()

        @pl.when(has_below & (upper_core != far))
        def _():
            for each in faces_down:
                each.start()

    @pl.when(jnp.logical_not(has_below))
    def _():
        from_up[...] = jnp.zeros_like(from_up)
        corner_low[...] = jnp.zeros_like(corner_low)
        tail_low[...] = jnp.zeros_like(tail_low)

    @pl.when(jnp.logical_not(has_above))
    def _():
        from_down[...] = jnp.zeros_like(from_down)
        corner_high[...] = jnp.zeros_like(corner_high)
        tail_high[...] = jnp.zeros_like(tail_high)

    resident = stay.shape[1] // LANES
    weigh(stay, 0)
    weigh(lower, resident)
    weigh(upper, resident + lower.shape[1] // LANES)
    row.wait()

    @pl.when(has_above)
    def _():
        for each in faces_up + ends_up:
            each.wait_send()
        for each in faces_down + ends_down:
            each.wait_recv()

    @pl.when(has_below)
    def _():
        for each in faces_down + ends_down:
            each.wait_send()
        for each in faces_up + ends_up:
            each.wait_recv()


def exchange_call(grid, last, bricks, stay, lower, upper, gas, total):
    plane = (FIELDS, grid.span_y, grid.span_z)
    edge = (5, 8, grid.span_z)
    corner = jax.ShapeDtypeStruct(edge[1:], F32)
    copies = 5 + 2 * FIELDS
    return pl.pallas_call(
        functools.partial(exchange_kernel, grid, last),
        out_shape=(
            jax.ShapeDtypeStruct((FIELDS, 5, grid.pad_y, grid.span_z), F32),
            jax.ShapeDtypeStruct(plane, F32),
            jax.ShapeDtypeStruct(plane, F32),
            jax.ShapeDtypeStruct(edge, F32),
            corner,
            corner,
            corner,
            corner,
            jax.ShapeDtypeStruct((bricks.shape[0] * 2 * LANES, LANES), BF16),
        ),
        in_specs=[SMEM] + [VMEM] * 5,
        out_specs=(VMEM,) * 9,
        scratch_shapes=[
            pltpu.VMEM(plane, F32),
            pltpu.VMEM(plane, F32),
            pltpu.VMEM(edge, F32),
            pltpu.SemaphoreType.DMA((copies,)),
            pltpu.SemaphoreType.DMA((copies,)),
        ],
        compiler_params=pltpu.CompilerParams(
            collective_id=0, has_side_effects=True, vmem_limit_bytes=8 * 2**20
        ),
        name="exchange",
    )(bricks, stay, lower, upper, gas, total)


def sample_call(grid, last, bricks, *arrays):
    gas = arrays[3]
    return pl.pallas_call(
        functools.partial(sample_kernel, grid, last),
        out_shape=(
            jax.ShapeDtypeStruct(gas.shape, F32),
            jax.ShapeDtypeStruct((FIELDS, bricks.shape[0] * LANES), BF16),
        ),
        in_specs=[SMEM] + [VMEM] * 13,
        scratch_shapes=[
            pltpu.VMEM((FIELDS, 5, grid.pad_y, grid.span_z), F32),
            pltpu.VMEM((grid.rows, LANES), F32),
        ],
        compiler_params=BIG,
        name="sample",
    )(bricks, *arrays)


def per_device(load, offset, cell, rows, bricks, gas):
    axial = lax.axis_size("axial")
    span_y, span_z = gas.shape[2], gas.shape[3]
    grid = Grid(span_y, span_z)
    zeros, none_gone = clear_call(grid, load.shape[1] // LANES)
    up, down, stay = gather_call(load, offset, cell, rows, none_gone)
    lower, upper, spread = migrate_call(grid, axial - 1, bricks, up, down, stay)
    total = deposit_call(grid, bricks, spread, lower, upper, zeros)
    arrived = exchange_call(grid, axial - 1, bricks, stay, lower, upper, gas, total)
    return sample_call(
        grid, axial - 1, bricks, stay, lower, upper, gas, *arrived
    )


def solution(mesh):
    return jax.shard_map(
        per_device,
        mesh=mesh,
        in_specs=(
            P(None, ("axial", "radial")),
            P(None, ("axial", "radial")),
            P(("axial", "radial")),
            P(None, ("axial", "radial")),
            P(("axial", "radial")),
            P(None, "axial", "radial", None),
        ),
        out_specs=(P(None, "axial", "radial", None), P(None, ("axial", "radial"))),
        check_vma=False,
    )
```

```python
import functools

import jax
import jax.numpy as jnp
from jax import lax
from jax.experimental import pallas as pl
from jax.experimental.pallas import tpu as pltpu
from jax.sharding import PartitionSpec as P

COUPLE = 0.5
LANES = 128
TILE = 2048
MATRIX_BLOCKS = 80
CHUNK = 16
FIELDS = 5
GROUP = 6
SPAN = 4 * GROUP
NT = (((1,), (1,)), ((), ()))
SMEM = pl.BlockSpec(memory_space=pltpu.SMEM)
VMEM = pl.BlockSpec(memory_space=pltpu.VMEM)
F32 = jnp.float32
BF16 = jnp.bfloat16


def split(x):
    high = x.astype(BF16).astype(F32)
    return high, x - high


def hat(x):
    return jnp.maximum(1.0 - jnp.abs(x), 0.0)


def row_numbers(shape):
    return lax.broadcasted_iota(jnp.int32, shape, 0)


def clear_kernel(total, gone):
    total[...] = jnp.zeros_like(total)
    gone[...] = jnp.zeros_like(gone)


def clear_call(grid, blocks):
    return pl.pallas_call(
        clear_kernel,
        out_shape=(
            jax.ShapeDtypeStruct((grid.rows, LANES), F32),
            jax.ShapeDtypeStruct((blocks, LANES), F32),
        ),
        compiler_params=pltpu.CompilerParams(vmem_limit_bytes=2**20),
        cost_estimate=pl.CostEstimate(
            flops=10**10, bytes_accessed=2 * 10**6, transcendentals=0
        ),
        name="clear",
    )()


def gather_kernel(
    load, offset, cell, rows, none_gone, up, down, stay, table, base, corner, gone,
    attributes
):
    count = load.shape[1]
    blocks = count // LANES
    axis_row = row_numbers((3, count))
    coords = lax.shift_right_logical(
        jnp.broadcast_to(cell[...], (3, count)), 4 - 2 * axis_row
    ) & 3
    corner[...] = jnp.concatenate([jnp.zeros((5, count), F32), coords.astype(F32)], 0)
    base[...] = jnp.concatenate([load[...], offset[...]], 0)
    attributes[...] = base[...] + corner[...]

    def fill(step, carry):
        at = pl.multiple_of(step * 2 * LANES, 2 * LANES)
        pair = base[:, pl.ds(at, 2 * LANES)] + corner[:, pl.ds(at, 2 * LANES)]
        both = jnp.concatenate([pair[:, :LANES], pair[:, LANES:]], 0)
        high, low = split(both)
        place = pl.multiple_of(step * 16, 16)
        table[pl.ds(place, 16), :] = jnp.concatenate([high, low], 1).astype(BF16)
        return carry

    lax.fori_loop(0, blocks // 2, fill, 0, unroll=8)
    gone[...] = none_gone[...]

    for side, out in ((0, up), (1, down)):
        out[...] = jnp.zeros_like(out)
        named = jnp.sum((rows[side : side + 1, :] >= 0).astype(F32)).astype(jnp.int32)

        def tile_step(step, carry, side=side, out=out):
            at = pl.multiple_of(step * TILE, TILE)
            row = rows[side : side + 1, pl.ds(at, TILE)]
            lane = row & (LANES - 1)
            block = lax.shift_right_arithmetic(row, 7)
            number = row_numbers((LANES, TILE))
            lane_hot = jnp.where(number == lane, 1.0, 0.0).astype(BF16)
            block_hot = jnp.where(number == block, 1.0, 0.0).astype(BF16)
            gone[...] += lax.dot_general(block_hot, lane_hot, NT, preferred_element_type=F32)
            wanted = jnp.concatenate([lane_hot, lane_hot], 0)
            block8 = jnp.broadcast_to(block, (8, TILE))
            lane8 = jnp.broadcast_to(lane, (8, TILE))
            found = jnp.zeros((8, TILE), F32)
            pieces = []
            chunks = MATRIX_BLOCKS // CHUNK
            columns = TILE // LANES
            for chunk in range(chunks):
                part = jnp.dot(
                    table[8 * CHUNK * chunk : 8 * CHUNK * (chunk + 1), :], wanted,
                    preferred_element_type=F32,
                )
                for i in range(CHUNK):
                    found = jnp.where(
                        block8 == chunk * CHUNK + i, part[8 * i : 8 * i + 8, :], found
                    )
                for j in range(columns * chunk // chunks, columns * (chunk + 1) // chunks):
                    column = slice(LANES * j, LANES * (j + 1))
                    piece = jnp.zeros((8, LANES), F32)
                    for i in range(MATRIX_BLOCKS, blocks):
                        taken = jnp.take_along_axis(
                            attributes[:, i * LANES : (i + 1) * LANES], lane8[:, column],
                            axis=1, mode="promise_in_bounds",
                        )
                        piece = jnp.where(block8[:, column] == i, taken, piece)
                    pieces.append(piece)
            if pieces and MATRIX_BLOCKS < blocks:
                found = jnp.where(
                    block8 < MATRIX_BLOCKS, found, jnp.concatenate(pieces, 1)
                )
            out[:, pl.ds(at, TILE)] = found
            return carry

        lax.fori_loop(0, (named + TILE - 1) // TILE, tile_step, 0)

    def keep(step, carry):
        at = pl.multiple_of(step * LANES, LANES)
        left = 1.0 - gone[pl.ds(step, 1), :]
        stay[:, pl.ds(at, LANES)] = (
            base[:, pl.ds(at, LANES)] * left + corner[:, pl.ds(at, LANES)]
        )
        return carry

    lax.fori_loop(0, blocks, keep, 0, unroll=8)


def gather_call(load, offset, cell, rows, none_gone):
    count = load.shape[1]
    slots = rows.shape[1]
    moved = jax.ShapeDtypeStruct((8, slots), F32)
    return pl.pallas_call(
        gather_kernel,
        out_shape=(moved, moved, jax.ShapeDtypeStruct((8, count), F32)),
        in_specs=[VMEM] * 5,
        scratch_shapes=[
            pltpu.VMEM((8 * (count // LANES), 2 * LANES), BF16),
            pltpu.VMEM((8, count), F32),
            pltpu.VMEM((8, count), F32),
            pltpu.VMEM((count // LANES, LANES), F32),
            pltpu.VMEM((8, count), F32),
        ],
        compiler_params=pltpu.CompilerParams(vmem_limit_bytes=16 * 2**20),
        cost_estimate=pl.CostEstimate(
            flops=10**10, bytes_accessed=2 * 10**6, transcendentals=0
        ),
        name="gather_rows",
    )(load, offset, cell.reshape(1, count), rows, none_gone)


class Grid:
    def __init__(self, span_y, span_z):
        self.span_y = span_y
        self.span_z = span_z
        self.per_row = span_z // 4
        self.bricks_y = span_y // 4
        self.groups = -(-self.bricks_y // GROUP)
        self.rows_z = span_z + 8
        self.rows = self.groups * FIELDS * self.rows_z
        self.pad_y = self.groups * SPAN
        self.shift = self.per_row.bit_length() - 1
        assert self.per_row == 1 << self.shift and self.bricks_y & (self.bricks_y - 1) == 0

    def place(self, brick):
        z = brick & (self.per_row - 1)
        y = lax.shift_right_logical(brick, self.shift) & (self.bricks_y - 1)
        group = sum((y >= GROUP * k).astype(jnp.int32) for k in range(1, self.groups))
        first = group * (FIELDS * self.rows_z) + 4 * z
        return first, (4 * y - SPAN * group).astype(F32)


def plane_weights(block, shift_y):
    number = row_numbers((8, LANES)).astype(F32)
    x = hat(number - block[5:6])
    y = block[6:7] + shift_y
    parts = [hat(number + 8.0 * k - y) for k in range(SPAN // 8)]
    last = hat(float(SPAN) - y)
    pieces = [x[i : i + 1] * part for i in range(5) for part in parts]
    return split(jnp.concatenate(pieces + [x * last], 0))


def depth_weights(block):
    return hat(row_numbers((8, LANES)).astype(F32) - block[7:8])


def doubled(x):
    high, low = split(x)
    both = jnp.concatenate([high, low], 0).astype(BF16)
    return jnp.concatenate([both, both], 1)


def spread_block(block, weights):
    high, low = weights
    plane = jnp.concatenate([high.astype(BF16), low.astype(BF16)], 1)
    depth = depth_weights(block)
    loads = jnp.concatenate([block[f : f + 1] * depth for f in range(FIELDS)], 0)
    both = lax.dot_general(doubled(loads), plane, NT, preferred_element_type=F32)
    return both[: 8 * FIELDS] + both[8 * FIELDS :]


def add_block(grid, summed, brick, total):
    first, _ = grid.place(brick)
    for f in range(FIELDS):
        rows = pl.ds(first + f * grid.rows_z, 8)
        total[rows, :] += summed[8 * f : 8 * f + 8]


def sample_block(grid, block, brick, plane, held):
    first, _ = grid.place(brick)
    fields = jnp.concatenate(
        [held[pl.ds(first + f * grid.rows_z, 8), :] for f in range(FIELDS)], 0
    )
    both = jnp.dot(doubled(fields), plane, preferred_element_type=F32)
    summed = both[: 8 * FIELDS] + both[8 * FIELDS :]
    depth = depth_weights(block)
    return jnp.concatenate(
        [
            jnp.sum(summed[8 * f : 8 * f + 8] * depth, axis=0, keepdims=True)
            for f in range(FIELDS)
        ],
        0,
    )


UNROLL = 64
TURN = 32


def deposit_kernel(grid, bricks, spread, lower, upper, zeros, total):
    del zeros
    blocks = lower.shape[1] // LANES
    resident = bricks.shape[0] - 2 * blocks
    ratio = resident // (2 * blocks)
    for part, offset in ((lower, 0), (upper, blocks)):

        def step(turn, carry, part=part, offset=offset):
            for i in range(UNROLL):
                at = turn * UNROLL + i
                block = part[:, pl.ds(pl.multiple_of(at * LANES, LANES), LANES)]
                brick = bricks[resident + offset + at]
                weights = plane_weights(block, grid.place(brick)[1])
                add_block(grid, spread_block(block, weights), brick, total)
                for j in range(ratio):
                    own = (offset + at) * ratio + j
                    rows = pl.ds(pl.multiple_of(own * 8 * FIELDS, 8), 8 * FIELDS)
                    add_block(grid, spread[rows, :], bricks[own], total)
            return carry

        lax.fori_loop(0, blocks // UNROLL, step, 0)


def merge_selector():
    picked = row_numbers((160, LANES))
    lane = lax.broadcasted_iota(jnp.int32, (160, LANES), 1)
    edge = picked - 5 * SPAN
    wanted = jnp.where(
        picked < 5 * SPAN, picked, jnp.where(edge % 8 == 0, 5 * SPAN + edge // 8, -1)
    )
    select = jnp.where(lane == wanted, 1.0, 0.0).astype(BF16)
    return jnp.concatenate([select, select], 1)


def merge_field(grid, f, select, total, sums):
    carried = None
    for group in range(grid.groups):
        first = (group * FIELDS + f) * grid.rows_z
        high, low = split(total[first : first + grid.span_z, :])
        both = jnp.concatenate([high.astype(BF16), low.astype(BF16)], 1)
        turned = lax.dot_general(select, both, NT, preferred_element_type=F32)
        for x in range(5):
            piece = turned[x * SPAN : (x + 1) * SPAN]
            if carried is not None:
                head = piece[:8] + carried[8 * x : 8 * x + 8]
                piece = jnp.concatenate([head, piece[8:]], 0)
            sums[f, x, group * SPAN : (group + 1) * SPAN, :] = piece
        carried = turned[5 * SPAN :]


def fill_faces(grid, f, second_half, gas, sums, up, down, row):
    ny = grid.span_y
    up[f] = sums[f, 4, :ny]
    down[f] = COUPLE * sums[f, 0, :ny] + gas[f, 0]
    for x in range(5):
        low_row = COUPLE * sums[f, x, 0:1, :]
        if x < 4:
            low_row = low_row + gas[f, x, 0:1, :]
        high_row = COUPLE * sums[f, x, ny : ny + 1, :]
        row[x, f : f + 1, :] = jnp.where(second_half, low_row, high_row)


def sample_kernel(
    grid, last, bricks, stay, lower, upper, gas, sums, from_up, from_down,
    from_row, corner_low, corner_high, tail_low, tail_high, weights, source, sampled, field, held
):
    ny = grid.span_y
    second_half = lax.axis_index("radial") == 1
    at_end = lax.axis_index("axial") == last
    face = jnp.where(second_half, 1.0, 0.0)
    for f in range(FIELDS):
        for x in range(5):
            extra = from_row[x, f : f + 1, :]
            if x == 0:
                extra = extra + corner_low[f : f + 1, :]
            if x == 4:
                extra = extra + corner_high[f : f + 1, :]
            first = row_numbers((8, grid.span_z)) == 0
            head = jnp.where(first, 2.0 * face * extra, 0.0)
            mine = sums[f, x, :ny, :]
            if x == 0:
                mine = mine + from_up[f]
            mine = jnp.concatenate([mine[:8] + head, mine[8:]], 0)
            tail = COUPLE * sums[f, x, ny : ny + 8, :]
            if x == 0:
                tail = tail + tail_low[f : f + 1, :]
            if x < 4:
                source[f, x] = mine
                mine = gas[f, x] + COUPLE * mine
            else:
                mine = COUPLE * mine + from_down[f]
                mine = jnp.where(at_end, 0.0, mine)
                tail = tail + tail_high[f : f + 1, :]
                tail = jnp.where(at_end, 0.0, tail)
                extra = jnp.where(at_end, 0.0, extra)
            tail = jnp.where(first & jnp.logical_not(second_half), tail + extra, 0.0)
            field[f, x, :ny, :] = mine
            field[f, x, ny : ny + 8, :] = tail
    for f in range(FIELDS):
        for group in range(grid.groups):
            edge = SPAN * (group + 1)
            pieces = [field[f, x, edge - SPAN : edge, :] for x in range(5)]
            if edge < grid.pad_y:
                pieces += [field[f, x, edge : edge + 1, :] for x in range(5)]
                pieces.append(jnp.zeros((3, grid.span_z), F32))
            else:
                pieces.append(jnp.zeros((8, grid.span_z), F32))
            turned = jnp.concatenate(pieces, 0).T
            at = (group * FIELDS + f) * grid.rows_z
            held[at : at + grid.span_z, :] = turned
            held[at + grid.span_z : at + grid.rows_z, :] = jnp.zeros((8, LANES), F32)

    offset = 0
    for part in (stay, lower, upper):
        blocks = part.shape[1] // LANES

        def step(turn, carry, part=part, offset=offset):
            for i in range(UNROLL):
                at = turn * UNROLL + i
                block = part[:, pl.ds(pl.multiple_of(at * LANES, LANES), LANES)]
                place_at = pl.multiple_of((offset + at) * 2 * LANES, 2 * LANES)
                plane = weights[pl.ds(place_at, 2 * LANES), :]
                values = sample_block(grid, block, bricks[offset + at], plane, held)
                lanes = pl.ds(pl.multiple_of((offset + at) * LANES, LANES), LANES)
                sampled[:, lanes] = values.astype(BF16)
            return carry

        lax.fori_loop(0, blocks // UNROLL, step, 0)
        offset += blocks


BIG = pltpu.CompilerParams(vmem_limit_bytes=12 * 2**20)


def deposit_call(grid, bricks, spread, lower, upper, zeros):
    return pl.pallas_call(
        functools.partial(deposit_kernel, grid),
        out_shape=jax.ShapeDtypeStruct((grid.rows, LANES), F32),
        in_specs=[SMEM, VMEM, VMEM, VMEM, VMEM],
        input_output_aliases={4: 0},
        compiler_params=BIG,
        name="deposit",
    )(bricks, spread, lower, upper, zeros)


def signal_entry(axial_at, radial_at):
    pl.semaphore_signal(
        pltpu.get_barrier_semaphore(), inc=1, device_id=(axial_at, radial_at),
        device_id_type=pl.DeviceIdType.MESH,
    )


def store_weights(target, at, weights):
    place = pl.multiple_of(at * 2 * LANES, 2 * LANES)
    target[pl.ds(place, 2 * LANES), :] = jnp.concatenate(weights, 0).astype(BF16)


def migrate_kernel(
    grid, last, bricks, up, down, stay, lower, upper, spread, sent, got
):
    a = lax.axis_index("axial")
    r = lax.axis_index("radial")
    has_above = a < last
    has_below = a > 0

    @pl.when(has_above)
    def _():
        signal_entry(a + 1, r)

    @pl.when(has_below)
    def _():
        signal_entry(a - 1, r)

    def copy(number, source, target, axial_at):
        return pltpu.make_async_remote_copy(
            src_ref=source, dst_ref=target, send_sem=sent.at[number],
            recv_sem=got.at[number], device_id=(axial_at, r),
            device_id_type=pl.DeviceIdType.MESH,
        )

    rising = copy(0, up, lower, a + 1)
    falling = copy(1, down, upper, a - 1)

    def step(turn, carry):
        for i in range(TURN):
            at = turn * TURN + i
            block = stay[:, pl.ds(pl.multiple_of(at * LANES, LANES), LANES)]
            plane = plane_weights(block, grid.place(bricks[at])[1])
            rows = pl.ds(pl.multiple_of(at * 8 * FIELDS, 8), 8 * FIELDS)
            spread[rows, :] = spread_block(block, plane)
        return carry

    peers = has_above.astype(jnp.int32) + has_below.astype(jnp.int32)
    pl.semaphore_wait(pltpu.get_barrier_semaphore(), peers)

    @pl.when(has_above)
    def _():
        rising.start()

    @pl.when(has_below)
    def _():
        falling.start()

    @pl.when(jnp.logical_not(has_below))
    def _():
        lower[...] = jnp.zeros_like(lower)

    @pl.when(jnp.logical_not(has_above))
    def _():
        upper[...] = jnp.zeros_like(upper)

    lax.fori_loop(0, stay.shape[1] // LANES // TURN, step, 0)

    @pl.when(has_above)
    def _():
        rising.wait_send()
        falling.wait_recv()

    @pl.when(has_below)
    def _():
        falling.wait_send()
        rising.wait_recv()


def migrate_call(grid, last, bricks, up, down, stay):
    blocks = stay.shape[1] // LANES
    return pl.pallas_call(
        functools.partial(migrate_kernel, grid, last),
        out_shape=(
            jax.ShapeDtypeStruct(up.shape, F32),
            jax.ShapeDtypeStruct(down.shape, F32),
            jax.ShapeDtypeStruct((blocks * 8 * FIELDS, LANES), F32),
        ),
        in_specs=[SMEM] + [VMEM] * 3,
        out_specs=(VMEM,) * 3,
        scratch_shapes=[pltpu.SemaphoreType.DMA((2,)), pltpu.SemaphoreType.DMA((2,))],
        compiler_params=pltpu.CompilerParams(
            collective_id=1, has_side_effects=True, vmem_limit_bytes=8 * 2**20
        ),
        name="migrate",
    )(bricks, up, down, stay)


def exchange_kernel(
    grid, last, bricks, stay, lower, upper, gas, total, sums, from_up, from_down, from_row,
    corner_low, corner_high, tail_low, tail_high, weights, up, down, edge, sent, got
):
    a = lax.axis_index("axial")
    r = lax.axis_index("radial")
    has_above = a < last
    has_below = a > 0
    signal_entry(a, 1 - r)

    @pl.when(has_above)
    def _():
        signal_entry(a + 1, r)
        signal_entry(a + 1, 1 - r)

    @pl.when(has_below)
    def _():
        signal_entry(a - 1, r)
        signal_entry(a - 1, 1 - r)

    peers = 1 + 2 * has_above.astype(jnp.int32) + 2 * has_below.astype(jnp.int32)

    def copy(number, source, target, axial_at, radial_at):
        return pltpu.make_async_remote_copy(
            src_ref=source, dst_ref=target, send_sem=sent.at[number],
            recv_sem=got.at[number], device_id=(axial_at, radial_at),
            device_id_type=pl.DeviceIdType.MESH,
        )

    row = copy(0, edge, from_row, a, 1 - r)
    ends_up = [
        copy(1, edge.at[4], corner_low, a + 1, 1 - r),
        copy(2, edge.at[4], tail_low, a + 1, r),
    ]
    ends_down = [
        copy(3, edge.at[0], corner_high, a - 1, 1 - r),
        copy(4, edge.at[0], tail_high, a - 1, r),
    ]
    faces_up = [copy(5 + f, up.at[f], from_up.at[f], a + 1, r) for f in range(FIELDS)]
    faces_down = [
        copy(5 + FIELDS + f, down.at[f], from_down.at[f], a - 1, r) for f in range(FIELDS)
    ]
    select = merge_selector()
    for x in range(5):
        edge[x, FIELDS:, :] = jnp.zeros((8 - FIELDS, grid.span_z), F32)
    def weigh(part, offset):
        def step(turn, carry):
            for i in range(TURN):
                at = turn * TURN + i
                block = part[:, pl.ds(pl.multiple_of(at * LANES, LANES), LANES)]
                plane = plane_weights(block, grid.place(bricks[offset + at])[1])
                store_weights(weights, offset + at, plane)
            return carry

        lax.fori_loop(0, part.shape[1] // LANES // TURN, step, 0)

    for f in range(FIELDS):
        merge_field(grid, f, select, total, sums)
        fill_faces(grid, f, r == 1, gas, sums, up, down, edge)
    pl.semaphore_wait(pltpu.get_barrier_semaphore(), peers)
    row.start()

    @pl.when(has_above)
    def _():
        for each in ends_up:
            each.start()

    @pl.when(has_below)
    def _():
        for each in ends_down:
            each.start()

    upper_core = a % 2 == 1
    for far in (True, False):

        @pl.when(has_above & (upper_core == far))
        def _():
            for each in faces_up:
                each.start()

        @pl.when(has_below & (upper_core != far))
        def _():
            for each in faces_down:
                each.start()

    @pl.when(jnp.logical_not(has_below))
    def _():
        from_up[...] = jnp.zeros_like(from_up)
        corner_low[...] = jnp.zeros_like(corner_low)
        tail_low[...] = jnp.zeros_like(tail_low)

    @pl.when(jnp.logical_not(has_above))
    def _():
        from_down[...] = jnp.zeros_like(from_down)
        corner_high[...] = jnp.zeros_like(corner_high)
        tail_high[...] = jnp.zeros_like(tail_high)

    resident = stay.shape[1] // LANES
    weigh(stay, 0)
    weigh(lower, resident)
    weigh(upper, resident + lower.shape[1] // LANES)
    row.wait()

    @pl.when(has_above)
    def _():
        for each in faces_up + ends_up:
            each.wait_send()
        for each in faces_down + ends_down:
            each.wait_recv()

    @pl.when(has_below)
    def _():
        for each in faces_down + ends_down:
            each.wait_send()
        for each in faces_up + ends_up:
            each.wait_recv()


def exchange_call(grid, last, bricks, stay, lower, upper, gas, total):
    plane = (FIELDS, grid.span_y, grid.span_z)
    edge = (5, 8, grid.span_z)
    corner = jax.ShapeDtypeStruct(edge[1:], F32)
    copies = 5 + 2 * FIELDS
    return pl.pallas_call(
        functools.partial(exchange_kernel, grid, last),
        out_shape=(
            jax.ShapeDtypeStruct((FIELDS, 5, grid.pad_y, grid.span_z), F32),
            jax.ShapeDtypeStruct(plane, F32),
            jax.ShapeDtypeStruct(plane, F32),
            jax.ShapeDtypeStruct(edge, F32),
            corner,
            corner,
            corner,
            corner,
            jax.ShapeDtypeStruct((bricks.shape[0] * 2 * LANES, LANES), BF16),
        ),
        in_specs=[SMEM] + [VMEM] * 5,
        out_specs=(VMEM,) * 9,
        scratch_shapes=[
            pltpu.VMEM(plane, F32),
            pltpu.VMEM(plane, F32),
            pltpu.VMEM(edge, F32),
            pltpu.SemaphoreType.DMA((copies,)),
            pltpu.SemaphoreType.DMA((copies,)),
        ],
        compiler_params=pltpu.CompilerParams(
            collective_id=0, has_side_effects=True, vmem_limit_bytes=8 * 2**20
        ),
        name="exchange",
    )(bricks, stay, lower, upper, gas, total)


def sample_call(grid, last, bricks, *arrays):
    gas = arrays[3]
    return pl.pallas_call(
        functools.partial(sample_kernel, grid, last),
        out_shape=(
            jax.ShapeDtypeStruct(gas.shape, F32),
            jax.ShapeDtypeStruct((FIELDS, bricks.shape[0] * LANES), BF16),
        ),
        in_specs=[SMEM] + [VMEM] * 13,
        scratch_shapes=[
            pltpu.VMEM((FIELDS, 5, grid.pad_y, grid.span_z), F32),
            pltpu.VMEM((grid.rows, LANES), F32),
        ],
        compiler_params=BIG,
        name="sample",
    )(bricks, *arrays)


def per_device(load, offset, cell, rows, bricks, gas):
    axial = lax.axis_size("axial")
    span_y, span_z = gas.shape[2], gas.shape[3]
    grid = Grid(span_y, span_z)
    zeros, none_gone = clear_call(grid, load.shape[1] // LANES)
    up, down, stay = gather_call(load, offset, cell, rows, none_gone)
    lower, upper, spread = migrate_call(grid, axial - 1, bricks, up, down, stay)
    total = deposit_call(grid, bricks, spread, lower, upper, zeros)
    arrived = exchange_call(grid, axial - 1, bricks, stay, lower, upper, gas, total)
    return sample_call(
        grid, axial - 1, bricks, stay, lower, upper, gas, *arrived
    )


def solution(mesh):
    return jax.shard_map(
        per_device,
        mesh=mesh,
        in_specs=(
            P(None, ("axial", "radial")),
            P(None, ("axial", "radial")),
            P(("axial", "radial")),
            P(None, ("axial", "radial")),
            P(("axial", "radial")),
            P(None, "axial", "radial", None),
        ),
        out_specs=(P(None, "axial", "radial", None), P(None, ("axial", "radial"))),
        check_vma=False,
    )
```

```python
import functools

import jax
import jax.numpy as jnp
from jax import lax
from jax.experimental import pallas as pl
from jax.experimental.pallas import tpu as pltpu
from jax.sharding import PartitionSpec as P

COUPLE = 0.5
LANES = 128
TILE = 2048
MATRIX_BLOCKS = 80
CHUNK = 16
FIELDS = 5
GROUP = 6
SPAN = 4 * GROUP
NT = (((1,), (1,)), ((), ()))
SMEM = pl.BlockSpec(memory_space=pltpu.SMEM)
VMEM = pl.BlockSpec(memory_space=pltpu.VMEM)
F32 = jnp.float32
BF16 = jnp.bfloat16


def split(x):
    high = x.astype(BF16).astype(F32)
    return high, x - high


def hat(x):
    return jnp.maximum(1.0 - jnp.abs(x), 0.0)


def row_numbers(shape):
    return lax.broadcasted_iota(jnp.int32, shape, 0)


def clear_kernel(total, gone):
    total[...] = jnp.zeros_like(total)
    gone[...] = jnp.zeros_like(gone)


def clear_call(grid, blocks):
    return pl.pallas_call(
        clear_kernel,
        out_shape=(
            jax.ShapeDtypeStruct((grid.rows, LANES), F32),
            jax.ShapeDtypeStruct((blocks, LANES), F32),
        ),
        compiler_params=pltpu.CompilerParams(vmem_limit_bytes=2**20),
        cost_estimate=pl.CostEstimate(
            flops=10**10, bytes_accessed=2 * 10**6, transcendentals=0
        ),
        name="clear",
    )()


def gather_kernel(
    load, offset, cell, rows, none_gone, up, down, stay, table, base, corner, gone,
    attributes
):
    count = load.shape[1]
    blocks = count // LANES
    axis_row = row_numbers((3, count))
    coords = lax.shift_right_logical(
        jnp.broadcast_to(cell[...], (3, count)), 4 - 2 * axis_row
    ) & 3
    corner[...] = jnp.concatenate([jnp.zeros((5, count), F32), coords.astype(F32)], 0)
    base[...] = jnp.concatenate([load[...], offset[...]], 0)
    attributes[...] = base[...] + corner[...]

    def fill(step, carry):
        at = pl.multiple_of(step * 2 * LANES, 2 * LANES)
        pair = base[:, pl.ds(at, 2 * LANES)] + corner[:, pl.ds(at, 2 * LANES)]
        both = jnp.concatenate([pair[:, :LANES], pair[:, LANES:]], 0)
        high, low = split(both)
        place = pl.multiple_of(step * 16, 16)
        table[pl.ds(place, 16), :] = jnp.concatenate([high, low], 1).astype(BF16)
        return carry

    lax.fori_loop(0, blocks // 2, fill, 0, unroll=8)
    gone[...] = none_gone[...]

    for side, out in ((0, up), (1, down)):
        out[...] = jnp.zeros_like(out)
        named = jnp.sum((rows[side : side + 1, :] >= 0).astype(F32)).astype(jnp.int32)

        def tile_step(step, carry, side=side, out=out):
            at = pl.multiple_of(step * TILE, TILE)
            row = rows[side : side + 1, pl.ds(at, TILE)]
            lane = row & (LANES - 1)
            block = lax.shift_right_arithmetic(row, 7)
            number = row_numbers((LANES, TILE))
            lane_hot = jnp.where(number == lane, 1.0, 0.0).astype(BF16)
            block_hot = jnp.where(number == block, 1.0, 0.0).astype(BF16)
            gone[...] += lax.dot_general(block_hot, lane_hot, NT, preferred_element_type=F32)
            wanted = jnp.concatenate([lane_hot, lane_hot], 0)
            block8 = jnp.broadcast_to(block, (8, TILE))
            lane8 = jnp.broadcast_to(lane, (8, TILE))
            found = jnp.zeros((8, TILE), F32)
            pieces = []
            chunks = MATRIX_BLOCKS // CHUNK
            columns = TILE // LANES
            for chunk in range(chunks):
                part = jnp.dot(
                    table[8 * CHUNK * chunk : 8 * CHUNK * (chunk + 1), :], wanted,
                    preferred_element_type=F32,
                )
                for i in range(CHUNK):
                    found = jnp.where(
                        block8 == chunk * CHUNK + i, part[8 * i : 8 * i + 8, :], found
                    )
                for j in range(columns * chunk // chunks, columns * (chunk + 1) // chunks):
                    column = slice(LANES * j, LANES * (j + 1))
                    piece = jnp.zeros((8, LANES), F32)
                    for i in range(MATRIX_BLOCKS, blocks):
                        taken = jnp.take_along_axis(
                            attributes[:, i * LANES : (i + 1) * LANES], lane8[:, column],
                            axis=1, mode="promise_in_bounds",
                        )
                        piece = jnp.where(block8[:, column] == i, taken, piece)
                    pieces.append(piece)
            if pieces and MATRIX_BLOCKS < blocks:
                found = jnp.where(
                    block8 < MATRIX_BLOCKS, found, jnp.concatenate(pieces, 1)
                )
            out[:, pl.ds(at, TILE)] = found
            return carry

        lax.fori_loop(0, (named + TILE - 1) // TILE, tile_step, 0)

    def keep(step, carry):
        at = pl.multiple_of(step * LANES, LANES)
        left = 1.0 - gone[pl.ds(step, 1), :]
        stay[:, pl.ds(at, LANES)] = (
            base[:, pl.ds(at, LANES)] * left + corner[:, pl.ds(at, LANES)]
        )
        return carry

    lax.fori_loop(0, blocks, keep, 0, unroll=8)


def gather_call(load, offset, cell, rows, none_gone):
    count = load.shape[1]
    slots = rows.shape[1]
    moved = jax.ShapeDtypeStruct((8, slots), F32)
    return pl.pallas_call(
        gather_kernel,
        out_shape=(moved, moved, jax.ShapeDtypeStruct((8, count), F32)),
        in_specs=[VMEM] * 5,
        scratch_shapes=[
            pltpu.VMEM((8 * (count // LANES), 2 * LANES), BF16),
            pltpu.VMEM((8, count), F32),
            pltpu.VMEM((8, count), F32),
            pltpu.VMEM((count // LANES, LANES), F32),
            pltpu.VMEM((8, count), F32),
        ],
        compiler_params=pltpu.CompilerParams(vmem_limit_bytes=16 * 2**20),
        cost_estimate=pl.CostEstimate(
            flops=10**10, bytes_accessed=2 * 10**6, transcendentals=0
        ),
        name="gather_rows",
    )(load, offset, cell.reshape(1, count), rows, none_gone)


class Grid:
    def __init__(self, span_y, span_z):
        self.span_y = span_y
        self.span_z = span_z
        self.per_row = span_z // 4
        self.bricks_y = span_y // 4
        self.groups = -(-self.bricks_y // GROUP)
        self.rows_z = span_z + 8
        self.rows = self.groups * FIELDS * self.rows_z
        self.pad_y = self.groups * SPAN
        self.shift = self.per_row.bit_length() - 1
        assert self.per_row == 1 << self.shift and self.bricks_y & (self.bricks_y - 1) == 0

    def place(self, brick):
        z = brick & (self.per_row - 1)
        y = lax.shift_right_logical(brick, self.shift) & (self.bricks_y - 1)
        group = sum((y >= GROUP * k).astype(jnp.int32) for k in range(1, self.groups))
        first = group * (FIELDS * self.rows_z) + 4 * z
        return first, (4 * y - SPAN * group).astype(F32)


def plane_weights(block, shift_y):
    number = row_numbers((8, LANES)).astype(F32)
    x = hat(number - block[5:6])
    y = block[6:7] + shift_y
    parts = [hat(number + 8.0 * k - y) for k in range(SPAN // 8)]
    last = hat(float(SPAN) - y)
    pieces = [x[i : i + 1] * part for i in range(5) for part in parts]
    return split(jnp.concatenate(pieces + [x * last], 0))


def depth_weights(block):
    return hat(row_numbers((8, LANES)).astype(F32) - block[7:8])


def doubled(x):
    high, low = split(x)
    both = jnp.concatenate([high, low], 0).astype(BF16)
    return jnp.concatenate([both, both], 1)


def spread_block(block, weights):
    high, low = weights
    plane = jnp.concatenate([high.astype(BF16), low.astype(BF16)], 1)
    depth = depth_weights(block)
    loads = jnp.concatenate([block[f : f + 1] * depth for f in range(FIELDS)], 0)
    both = lax.dot_general(doubled(loads), plane, NT, preferred_element_type=F32)
    return both[: 8 * FIELDS] + both[8 * FIELDS :]


def add_block(grid, summed, brick, total):
    first, _ = grid.place(brick)
    for f in range(FIELDS):
        rows = pl.ds(first + f * grid.rows_z, 8)
        total[rows, :] += summed[8 * f : 8 * f + 8]


def sample_block(grid, block, brick, plane, held):
    first, _ = grid.place(brick)
    fields = jnp.concatenate(
        [held[pl.ds(first + f * grid.rows_z, 8), :] for f in range(FIELDS)], 0
    )
    both = jnp.dot(doubled(fields), plane, preferred_element_type=F32)
    summed = both[: 8 * FIELDS] + both[8 * FIELDS :]
    depth = depth_weights(block)
    return jnp.concatenate(
        [
            jnp.sum(summed[8 * f : 8 * f + 8] * depth, axis=0, keepdims=True)
            for f in range(FIELDS)
        ],
        0,
    )


UNROLL = 64
CHUNK_BLOCKS = 16


def filled_chunks(part):
    wide = CHUNK_BLOCKS * LANES
    return [
        (at // LANES, jnp.max(jnp.abs(part[:, at : at + wide])) > 0.0)
        for at in range(0, part.shape[1], wide)
    ]


TURN = 32


def deposit_kernel(grid, bricks, spread, lower, upper, zeros, total):
    del zeros
    blocks = lower.shape[1] // LANES
    resident = bricks.shape[0] - 2 * blocks
    ratio = resident // (2 * blocks)
    for part, offset in ((lower, 0), (upper, blocks)):
        for first, filled in filled_chunks(part):

            def own_blocks(at, offset=offset):
                for j in range(ratio):
                    own = (offset + at) * ratio + j
                    rows = pl.ds(own * 8 * FIELDS, 8 * FIELDS)
                    add_block(grid, spread[rows, :], bricks[own], total)

            @pl.when(filled)
            def _(part=part, offset=offset, first=first, own_blocks=own_blocks):
                for at in range(first, first + CHUNK_BLOCKS):
                    block = part[:, at * LANES : (at + 1) * LANES]
                    brick = bricks[resident + offset + at]
                    weights = plane_weights(block, grid.place(brick)[1])
                    add_block(grid, spread_block(block, weights), brick, total)
                    own_blocks(at)

            @pl.when(jnp.logical_not(filled))
            def _(first=first, own_blocks=own_blocks):
                for at in range(first, first + CHUNK_BLOCKS):
                    own_blocks(at)


def merge_selector():
    picked = row_numbers((160, LANES))
    lane = lax.broadcasted_iota(jnp.int32, (160, LANES), 1)
    edge = picked - 5 * SPAN
    wanted = jnp.where(
        picked < 5 * SPAN, picked, jnp.where(edge % 8 == 0, 5 * SPAN + edge // 8, -1)
    )
    select = jnp.where(lane == wanted, 1.0, 0.0).astype(BF16)
    return jnp.concatenate([select, select], 1)


def merge_field(grid, f, select, total, sums):
    carried = None
    for group in range(grid.groups):
        first = (group * FIELDS + f) * grid.rows_z
        high, low = split(total[first : first + grid.span_z, :])
        both = jnp.concatenate([high.astype(BF16), low.astype(BF16)], 1)
        turned = lax.dot_general(select, both, NT, preferred_element_type=F32)
        for x in range(5):
            piece = turned[x * SPAN : (x + 1) * SPAN]
            if carried is not None:
                head = piece[:8] + carried[8 * x : 8 * x + 8]
                piece = jnp.concatenate([head, piece[8:]], 0)
            sums[f, x, group * SPAN : (group + 1) * SPAN, :] = piece
        carried = turned[5 * SPAN :]


def fill_faces(grid, f, second_half, gas, sums, up, down, row):
    ny = grid.span_y
    up[f] = sums[f, 4, :ny]
    down[f] = COUPLE * sums[f, 0, :ny] + gas[f, 0]
    for x in range(5):
        low_row = COUPLE * sums[f, x, 0:1, :]
        if x < 4:
            low_row = low_row + gas[f, x, 0:1, :]
        high_row = COUPLE * sums[f, x, ny : ny + 1, :]
        row[x, f : f + 1, :] = jnp.where(second_half, low_row, high_row)


def sample_kernel(
    grid, last, bricks, stay, lower, upper, gas, sums, from_up, from_down,
    from_row, corner_low, corner_high, tail_low, tail_high, weights, source, sampled, field, held
):
    ny = grid.span_y
    second_half = lax.axis_index("radial") == 1
    at_end = lax.axis_index("axial") == last
    face = jnp.where(second_half, 1.0, 0.0)
    for f in range(FIELDS):
        for x in range(5):
            extra = from_row[x, f : f + 1, :]
            if x == 0:
                extra = extra + corner_low[f : f + 1, :]
            if x == 4:
                extra = extra + corner_high[f : f + 1, :]
            first = row_numbers((8, grid.span_z)) == 0
            head = jnp.where(first, 2.0 * face * extra, 0.0)
            mine = sums[f, x, :ny, :]
            if x == 0:
                mine = mine + from_up[f]
            mine = jnp.concatenate([mine[:8] + head, mine[8:]], 0)
            tail = COUPLE * sums[f, x, ny : ny + 8, :]
            if x == 0:
                tail = tail + tail_low[f : f + 1, :]
            if x < 4:
                source[f, x] = mine
                mine = gas[f, x] + COUPLE * mine
            else:
                mine = COUPLE * mine + from_down[f]
                mine = jnp.where(at_end, 0.0, mine)
                tail = tail + tail_high[f : f + 1, :]
                tail = jnp.where(at_end, 0.0, tail)
                extra = jnp.where(at_end, 0.0, extra)
            tail = jnp.where(first & jnp.logical_not(second_half), tail + extra, 0.0)
            field[f, x, :ny, :] = mine
            field[f, x, ny : ny + 8, :] = tail
    for f in range(FIELDS):
        for group in range(grid.groups):
            edge = SPAN * (group + 1)
            pieces = [field[f, x, edge - SPAN : edge, :] for x in range(5)]
            if edge < grid.pad_y:
                pieces += [field[f, x, edge : edge + 1, :] for x in range(5)]
                pieces.append(jnp.zeros((3, grid.span_z), F32))
            else:
                pieces.append(jnp.zeros((8, grid.span_z), F32))
            turned = jnp.concatenate(pieces, 0).T
            at = (group * FIELDS + f) * grid.rows_z
            held[at : at + grid.span_z, :] = turned
            held[at + grid.span_z : at + grid.rows_z, :] = jnp.zeros((8, LANES), F32)

    offset = 0
    for part in (stay, lower, upper):
        blocks = part.shape[1] // LANES

        def step(turn, carry, part=part, offset=offset):
            for i in range(UNROLL):
                at = turn * UNROLL + i
                block = part[:, pl.ds(pl.multiple_of(at * LANES, LANES), LANES)]
                place_at = pl.multiple_of((offset + at) * 2 * LANES, 2 * LANES)
                plane = weights[pl.ds(place_at, 2 * LANES), :]
                values = sample_block(grid, block, bricks[offset + at], plane, held)
                lanes = pl.ds(pl.multiple_of((offset + at) * LANES, LANES), LANES)
                sampled[:, lanes] = values.astype(BF16)
            return carry

        lax.fori_loop(0, blocks // UNROLL, step, 0)
        offset += blocks


BIG = pltpu.CompilerParams(vmem_limit_bytes=12 * 2**20)


def deposit_call(grid, bricks, spread, lower, upper, zeros):
    return pl.pallas_call(
        functools.partial(deposit_kernel, grid),
        out_shape=jax.ShapeDtypeStruct((grid.rows, LANES), F32),
        in_specs=[SMEM, VMEM, VMEM, VMEM, VMEM],
        input_output_aliases={4: 0},
        compiler_params=BIG,
        name="deposit",
    )(bricks, spread, lower, upper, zeros)


def signal_entry(axial_at, radial_at):
    pl.semaphore_signal(
        pltpu.get_barrier_semaphore(), inc=1, device_id=(axial_at, radial_at),
        device_id_type=pl.DeviceIdType.MESH,
    )


def store_weights(target, at, weights):
    place = pl.multiple_of(at * 2 * LANES, 2 * LANES)
    target[pl.ds(place, 2 * LANES), :] = jnp.concatenate(weights, 0).astype(BF16)


def migrate_kernel(
    grid, last, bricks, up, down, stay, lower, upper, spread, sent, got
):
    a = lax.axis_index("axial")
    r = lax.axis_index("radial")
    has_above = a < last
    has_below = a > 0

    @pl.when(has_above)
    def _():
        signal_entry(a + 1, r)

    @pl.when(has_below)
    def _():
        signal_entry(a - 1, r)

    def copy(number, source, target, axial_at):
        return pltpu.make_async_remote_copy(
            src_ref=source, dst_ref=target, send_sem=sent.at[number],
            recv_sem=got.at[number], device_id=(axial_at, r),
            device_id_type=pl.DeviceIdType.MESH,
        )

    rising = copy(0, up, lower, a + 1)
    falling = copy(1, down, upper, a - 1)

    def step(turn, carry):
        for i in range(TURN):
            at = turn * TURN + i
            block = stay[:, pl.ds(pl.multiple_of(at * LANES, LANES), LANES)]
            plane = plane_weights(block, grid.place(bricks[at])[1])
            rows = pl.ds(pl.multiple_of(at * 8 * FIELDS, 8), 8 * FIELDS)
            spread[rows, :] = spread_block(block, plane)
        return carry

    peers = has_above.astype(jnp.int32) + has_below.astype(jnp.int32)
    pl.semaphore_wait(pltpu.get_barrier_semaphore(), peers)

    @pl.when(has_above)
    def _():
        rising.start()

    @pl.when(has_below)
    def _():
        falling.start()

    @pl.when(jnp.logical_not(has_below))
    def _():
        lower[...] = jnp.zeros_like(lower)

    @pl.when(jnp.logical_not(has_above))
    def _():
        upper[...] = jnp.zeros_like(upper)

    lax.fori_loop(0, stay.shape[1] // LANES // TURN, step, 0)

    @pl.when(has_above)
    def _():
        rising.wait_send()
        falling.wait_recv()

    @pl.when(has_below)
    def _():
        falling.wait_send()
        rising.wait_recv()


def migrate_call(grid, last, bricks, up, down, stay):
    blocks = stay.shape[1] // LANES
    return pl.pallas_call(
        functools.partial(migrate_kernel, grid, last),
        out_shape=(
            jax.ShapeDtypeStruct(up.shape, F32),
            jax.ShapeDtypeStruct(down.shape, F32),
            jax.ShapeDtypeStruct((blocks * 8 * FIELDS, LANES), F32),
        ),
        in_specs=[SMEM] + [VMEM] * 3,
        out_specs=(VMEM,) * 3,
        scratch_shapes=[pltpu.SemaphoreType.DMA((2,)), pltpu.SemaphoreType.DMA((2,))],
        compiler_params=pltpu.CompilerParams(
            collective_id=1, has_side_effects=True, vmem_limit_bytes=8 * 2**20
        ),
        name="migrate",
    )(bricks, up, down, stay)


def exchange_kernel(
    grid, last, bricks, stay, lower, upper, gas, total, sums, from_up, from_down, from_row,
    corner_low, corner_high, tail_low, tail_high, weights, up, down, edge, sent, got
):
    a = lax.axis_index("axial")
    r = lax.axis_index("radial")
    has_above = a < last
    has_below = a > 0
    signal_entry(a, 1 - r)

    @pl.when(has_above)
    def _():
        signal_entry(a + 1, r)
        signal_entry(a + 1, 1 - r)

    @pl.when(has_below)
    def _():
        signal_entry(a - 1, r)
        signal_entry(a - 1, 1 - r)

    peers = 1 + 2 * has_above.astype(jnp.int32) + 2 * has_below.astype(jnp.int32)

    def copy(number, source, target, axial_at, radial_at):
        return pltpu.make_async_remote_copy(
            src_ref=source, dst_ref=target, send_sem=sent.at[number],
            recv_sem=got.at[number], device_id=(axial_at, radial_at),
            device_id_type=pl.DeviceIdType.MESH,
        )

    row = copy(0, edge, from_row, a, 1 - r)
    ends_up = [
        copy(1, edge.at[4], corner_low, a + 1, 1 - r),
        copy(2, edge.at[4], tail_low, a + 1, r),
    ]
    ends_down = [
        copy(3, edge.at[0], corner_high, a - 1, 1 - r),
        copy(4, edge.at[0], tail_high, a - 1, r),
    ]
    faces_up = [copy(5 + f, up.at[f], from_up.at[f], a + 1, r) for f in range(FIELDS)]
    faces_down = [
        copy(5 + FIELDS + f, down.at[f], from_down.at[f], a - 1, r) for f in range(FIELDS)
    ]
    select = merge_selector()
    for x in range(5):
        edge[x, FIELDS:, :] = jnp.zeros((8 - FIELDS, grid.span_z), F32)
    def weigh(part, offset):
        def step(turn, carry):
            for i in range(TURN):
                at = turn * TURN + i
                block = part[:, pl.ds(pl.multiple_of(at * LANES, LANES), LANES)]
                plane = plane_weights(block, grid.place(bricks[offset + at])[1])
                store_weights(weights, offset + at, plane)
            return carry

        lax.fori_loop(0, part.shape[1] // LANES // TURN, step, 0)

    for f in range(FIELDS):
        merge_field(grid, f, select, total, sums)
        fill_faces(grid, f, r == 1, gas, sums, up, down, edge)
    pl.semaphore_wait(pltpu.get_barrier_semaphore(), peers)
    row.start()

    @pl.when(has_above)
    def _():
        for each in ends_up:
            each.start()

    @pl.when(has_below)
    def _():
        for each in ends_down:
            each.start()

    upper_core = a % 2 == 1
    for far in (True, False):

        @pl.when(has_above & (upper_core == far))
        def _():
            for each in faces_up:
                each.start()

        @pl.when(has_below & (upper_core != far))
        def _():
            for each in faces_down:
                each.start()

    @pl.when(jnp.logical_not(has_below))
    def _():
        from_up[...] = jnp.zeros_like(from_up)
        corner_low[...] = jnp.zeros_like(corner_low)
        tail_low[...] = jnp.zeros_like(tail_low)

    @pl.when(jnp.logical_not(has_above))
    def _():
        from_down[...] = jnp.zeros_like(from_down)
        corner_high[...] = jnp.zeros_like(corner_high)
        tail_high[...] = jnp.zeros_like(tail_high)

    resident = stay.shape[1] // LANES
    weigh(stay, 0)
    weigh(lower, resident)
    weigh(upper, resident + lower.shape[1] // LANES)
    row.wait()

    @pl.when(has_above)
    def _():
        for each in faces_up + ends_up:
            each.wait_send()
        for each in faces_down + ends_down:
            each.wait_recv()

    @pl.when(has_below)
    def _():
        for each in faces_down + ends_down:
            each.wait_send()
        for each in faces_up + ends_up:
            each.wait_recv()


def exchange_call(grid, last, bricks, stay, lower, upper, gas, total):
    plane = (FIELDS, grid.span_y, grid.span_z)
    edge = (5, 8, grid.span_z)
    corner = jax.ShapeDtypeStruct(edge[1:], F32)
    copies = 5 + 2 * FIELDS
    return pl.pallas_call(
        functools.partial(exchange_kernel, grid, last),
        out_shape=(
            jax.ShapeDtypeStruct((FIELDS, 5, grid.pad_y, grid.span_z), F32),
            jax.ShapeDtypeStruct(plane, F32),
            jax.ShapeDtypeStruct(plane, F32),
            jax.ShapeDtypeStruct(edge, F32),
            corner,
            corner,
            corner,
            corner,
            jax.ShapeDtypeStruct((bricks.shape[0] * 2 * LANES, LANES), BF16),
        ),
        in_specs=[SMEM] + [VMEM] * 5,
        out_specs=(VMEM,) * 9,
        scratch_shapes=[
            pltpu.VMEM(plane, F32),
            pltpu.VMEM(plane, F32),
            pltpu.VMEM(edge, F32),
            pltpu.SemaphoreType.DMA((copies,)),
            pltpu.SemaphoreType.DMA((copies,)),
        ],
        compiler_params=pltpu.CompilerParams(
            collective_id=0, has_side_effects=True, vmem_limit_bytes=8 * 2**20
        ),
        name="exchange",
    )(bricks, stay, lower, upper, gas, total)


def sample_call(grid, last, bricks, *arrays):
    gas = arrays[3]
    return pl.pallas_call(
        functools.partial(sample_kernel, grid, last),
        out_shape=(
            jax.ShapeDtypeStruct(gas.shape, F32),
            jax.ShapeDtypeStruct((FIELDS, bricks.shape[0] * LANES), BF16),
        ),
        in_specs=[SMEM] + [VMEM] * 13,
        scratch_shapes=[
            pltpu.VMEM((FIELDS, 5, grid.pad_y, grid.span_z), F32),
            pltpu.VMEM((grid.rows, LANES), F32),
        ],
        compiler_params=BIG,
        name="sample",
    )(bricks, *arrays)


def per_device(load, offset, cell, rows, bricks, gas):
    axial = lax.axis_size("axial")
    span_y, span_z = gas.shape[2], gas.shape[3]
    grid = Grid(span_y, span_z)
    zeros, none_gone = clear_call(grid, load.shape[1] // LANES)
    up, down, stay = gather_call(load, offset, cell, rows, none_gone)
    lower, upper, spread = migrate_call(grid, axial - 1, bricks, up, down, stay)
    total = deposit_call(grid, bricks, spread, lower, upper, zeros)
    arrived = exchange_call(grid, axial - 1, bricks, stay, lower, upper, gas, total)
    return sample_call(
        grid, axial - 1, bricks, stay, lower, upper, gas, *arrived
    )


def solution(mesh):
    return jax.shard_map(
        per_device,
        mesh=mesh,
        in_specs=(
            P(None, ("axial", "radial")),
            P(None, ("axial", "radial")),
            P(("axial", "radial")),
            P(None, ("axial", "radial")),
            P(("axial", "radial")),
            P(None, "axial", "radial", None),
        ),
        out_specs=(P(None, "axial", "radial", None), P(None, ("axial", "radial"))),
        check_vma=False,
    )
```

```python
import functools

import jax
import jax.numpy as jnp
from jax import lax
from jax.experimental import pallas as pl
from jax.experimental.pallas import tpu as pltpu
from jax.sharding import PartitionSpec as P

COUPLE = 0.5
LANES = 128
TILE = 2048
MATRIX_BLOCKS = 80
CHUNK = 16
FIELDS = 5
GROUP = 6
SPAN = 4 * GROUP
NT = (((1,), (1,)), ((), ()))
SMEM = pl.BlockSpec(memory_space=pltpu.SMEM)
VMEM = pl.BlockSpec(memory_space=pltpu.VMEM)
F32 = jnp.float32
BF16 = jnp.bfloat16


def split(x):
    high = x.astype(BF16).astype(F32)
    return high, x - high


def hat(x):
    return jnp.maximum(1.0 - jnp.abs(x), 0.0)


def row_numbers(shape):
    return lax.broadcasted_iota(jnp.int32, shape, 0)


def clear_kernel(total, gone):
    total[...] = jnp.zeros_like(total)
    gone[...] = jnp.zeros_like(gone)


def clear_call(grid, blocks):
    return pl.pallas_call(
        clear_kernel,
        out_shape=(
            jax.ShapeDtypeStruct((grid.rows, LANES), F32),
            jax.ShapeDtypeStruct((blocks, LANES), F32),
        ),
        compiler_params=pltpu.CompilerParams(vmem_limit_bytes=2**20),
        cost_estimate=pl.CostEstimate(
            flops=10**10, bytes_accessed=2 * 10**6, transcendentals=0
        ),
        name="clear",
    )()


def gather_kernel(
    load, offset, cell, rows, none_gone, up, down, stay, table, base, corner, gone,
    attributes
):
    count = load.shape[1]
    blocks = count // LANES
    axis_row = row_numbers((3, count))
    coords = lax.shift_right_logical(
        jnp.broadcast_to(cell[...], (3, count)), 4 - 2 * axis_row
    ) & 3
    corner[...] = jnp.concatenate([jnp.zeros((5, count), F32), coords.astype(F32)], 0)
    base[...] = jnp.concatenate([load[...], offset[...]], 0)
    attributes[...] = base[...] + corner[...]

    def fill(step, carry):
        at = pl.multiple_of(step * 2 * LANES, 2 * LANES)
        pair = base[:, pl.ds(at, 2 * LANES)] + corner[:, pl.ds(at, 2 * LANES)]
        both = jnp.concatenate([pair[:, :LANES], pair[:, LANES:]], 0)
        high, low = split(both)
        place = pl.multiple_of(step * 16, 16)
        table[pl.ds(place, 16), :] = jnp.concatenate([high, low], 1).astype(BF16)
        return carry

    lax.fori_loop(0, blocks // 2, fill, 0, unroll=8)
    gone[...] = none_gone[...]

    for side, out in ((0, up), (1, down)):
        out[...] = jnp.zeros_like(out)
        named = jnp.sum((rows[side : side + 1, :] >= 0).astype(F32)).astype(jnp.int32)

        def tile_step(step, carry, side=side, out=out):
            at = pl.multiple_of(step * TILE, TILE)
            row = rows[side : side + 1, pl.ds(at, TILE)]
            lane = row & (LANES - 1)
            block = lax.shift_right_arithmetic(row, 7)
            number = row_numbers((LANES, TILE))
            lane_hot = jnp.where(number == lane, 1.0, 0.0).astype(BF16)
            block_hot = jnp.where(number == block, 1.0, 0.0).astype(BF16)
            gone[...] += lax.dot_general(block_hot, lane_hot, NT, preferred_element_type=F32)
            wanted = jnp.concatenate([lane_hot, lane_hot], 0)
            block8 = jnp.broadcast_to(block, (8, TILE))
            lane8 = jnp.broadcast_to(lane, (8, TILE))
            found = jnp.zeros((8, TILE), F32)
            pieces = []
            chunks = MATRIX_BLOCKS // CHUNK
            columns = TILE // LANES
            for chunk in range(chunks):
                part = jnp.dot(
                    table[8 * CHUNK * chunk : 8 * CHUNK * (chunk + 1), :], wanted,
                    preferred_element_type=F32,
                )
                for i in range(CHUNK):
                    found = jnp.where(
                        block8 == chunk * CHUNK + i, part[8 * i : 8 * i + 8, :], found
                    )
                for j in range(columns * chunk // chunks, columns * (chunk + 1) // chunks):
                    column = slice(LANES * j, LANES * (j + 1))
                    piece = jnp.zeros((8, LANES), F32)
                    for i in range(MATRIX_BLOCKS, blocks):
                        taken = jnp.take_along_axis(
                            attributes[:, i * LANES : (i + 1) * LANES], lane8[:, column],
                            axis=1, mode="promise_in_bounds",
                        )
                        piece = jnp.where(block8[:, column] == i, taken, piece)
                    pieces.append(piece)
            if pieces and MATRIX_BLOCKS < blocks:
                found = jnp.where(
                    block8 < MATRIX_BLOCKS, found, jnp.concatenate(pieces, 1)
                )
            out[:, pl.ds(at, TILE)] = found
            return carry

        lax.fori_loop(0, (named + TILE - 1) // TILE, tile_step, 0)

    def keep(step, carry):
        at = pl.multiple_of(step * LANES, LANES)
        left = 1.0 - gone[pl.ds(step, 1), :]
        stay[:, pl.ds(at, LANES)] = (
            base[:, pl.ds(at, LANES)] * left + corner[:, pl.ds(at, LANES)]
        )
        return carry

    lax.fori_loop(0, blocks, keep, 0, unroll=8)


def gather_call(load, offset, cell, rows, none_gone):
    count = load.shape[1]
    slots = rows.shape[1]
    moved = jax.ShapeDtypeStruct((8, slots), F32)
    return pl.pallas_call(
        gather_kernel,
        out_shape=(moved, moved, jax.ShapeDtypeStruct((8, count), F32)),
        in_specs=[VMEM] * 5,
        scratch_shapes=[
            pltpu.VMEM((8 * (count // LANES), 2 * LANES), BF16),
            pltpu.VMEM((8, count), F32),
            pltpu.VMEM((8, count), F32),
            pltpu.VMEM((count // LANES, LANES), F32),
            pltpu.VMEM((8, count), F32),
        ],
        compiler_params=pltpu.CompilerParams(vmem_limit_bytes=16 * 2**20),
        cost_estimate=pl.CostEstimate(
            flops=10**10, bytes_accessed=2 * 10**6, transcendentals=0
        ),
        name="gather_rows",
    )(load, offset, cell.reshape(1, count), rows, none_gone)


class Grid:
    def __init__(self, span_y, span_z):
        self.span_y = span_y
        self.span_z = span_z
        self.per_row = span_z // 4
        self.bricks_y = span_y // 4
        self.groups = -(-self.bricks_y // GROUP)
        self.rows_z = span_z + 8
        self.rows = self.groups * FIELDS * self.rows_z
        self.pad_y = self.groups * SPAN
        self.shift = self.per_row.bit_length() - 1
        assert self.per_row == 1 << self.shift and self.bricks_y & (self.bricks_y - 1) == 0

    def place(self, brick):
        z = brick & (self.per_row - 1)
        y = lax.shift_right_logical(brick, self.shift) & (self.bricks_y - 1)
        group = sum((y >= GROUP * k).astype(jnp.int32) for k in range(1, self.groups))
        first = group * (FIELDS * self.rows_z) + 4 * z
        return first, (4 * y - SPAN * group).astype(F32)


def plane_weights(block, shift_y):
    number = row_numbers((8, LANES)).astype(F32)
    x = hat(number - block[5:6])
    y = block[6:7] + shift_y
    parts = [hat(number + 8.0 * k - y) for k in range(SPAN // 8)]
    last = hat(float(SPAN) - y)
    pieces = [x[i : i + 1] * part for i in range(5) for part in parts]
    return split(jnp.concatenate(pieces + [x * last], 0))


def depth_weights(block):
    return hat(row_numbers((8, LANES)).astype(F32) - block[7:8])


def doubled(x):
    high, low = split(x)
    both = jnp.concatenate([high, low], 0).astype(BF16)
    return jnp.concatenate([both, both], 1)


def spread_block(block, weights):
    high, low = weights
    plane = jnp.concatenate([high.astype(BF16), low.astype(BF16)], 1)
    depth = depth_weights(block)
    loads = jnp.concatenate([block[f : f + 1] * depth for f in range(FIELDS)], 0)
    both = lax.dot_general(doubled(loads), plane, NT, preferred_element_type=F32)
    return both[: 8 * FIELDS] + both[8 * FIELDS :]


def add_block(grid, summed, brick, total):
    first, _ = grid.place(brick)
    for f in range(FIELDS):
        rows = pl.ds(first + f * grid.rows_z, 8)
        total[rows, :] += summed[8 * f : 8 * f + 8]


def sample_block(grid, block, brick, plane, held):
    first, _ = grid.place(brick)
    fields = jnp.concatenate(
        [held[pl.ds(first + f * grid.rows_z, 8), :] for f in range(FIELDS)], 0
    )
    both = jnp.dot(doubled(fields), plane, preferred_element_type=F32)
    summed = both[: 8 * FIELDS] + both[8 * FIELDS :]
    depth = depth_weights(block)
    return jnp.concatenate(
        [
            jnp.sum(summed[8 * f : 8 * f + 8] * depth, axis=0, keepdims=True)
            for f in range(FIELDS)
        ],
        0,
    )


UNROLL = 64
CHUNK_BLOCKS = 16


def filled_chunks(part):
    wide = CHUNK_BLOCKS * LANES
    return [
        (at // LANES, jnp.max(jnp.abs(part[:, at : at + wide])) > 0.0)
        for at in range(0, part.shape[1], wide)
    ]


TURN = 32


def deposit_kernel(grid, bricks, spread, lower, upper, zeros, total):
    del zeros
    blocks = lower.shape[1] // LANES
    resident = bricks.shape[0] - 2 * blocks
    ratio = resident // (2 * blocks)
    for part, offset in ((lower, 0), (upper, blocks)):
        for first, filled in filled_chunks(part):

            def own_blocks(at, offset=offset):
                for j in range(ratio):
                    own = (offset + at) * ratio + j
                    rows = pl.ds(own * 8 * FIELDS, 8 * FIELDS)
                    add_block(grid, spread[rows, :], bricks[own], total)

            @pl.when(filled)
            def _(part=part, offset=offset, first=first, own_blocks=own_blocks):
                for at in range(first, first + CHUNK_BLOCKS):
                    block = part[:, at * LANES : (at + 1) * LANES]
                    brick = bricks[resident + offset + at]
                    weights = plane_weights(block, grid.place(brick)[1])
                    add_block(grid, spread_block(block, weights), brick, total)
                    own_blocks(at)

            @pl.when(jnp.logical_not(filled))
            def _(first=first, own_blocks=own_blocks):
                for at in range(first, first + CHUNK_BLOCKS):
                    own_blocks(at)


def merge_selector():
    picked = row_numbers((160, LANES))
    lane = lax.broadcasted_iota(jnp.int32, (160, LANES), 1)
    edge = picked - 5 * SPAN
    wanted = jnp.where(
        picked < 5 * SPAN, picked, jnp.where(edge % 8 == 0, 5 * SPAN + edge // 8, -1)
    )
    select = jnp.where(lane == wanted, 1.0, 0.0).astype(BF16)
    return jnp.concatenate([select, select], 1)


def merge_field(grid, f, select, total, sums):
    carried = None
    for group in range(grid.groups):
        first = (group * FIELDS + f) * grid.rows_z
        high, low = split(total[first : first + grid.span_z, :])
        both = jnp.concatenate([high.astype(BF16), low.astype(BF16)], 1)
        turned = lax.dot_general(select, both, NT, preferred_element_type=F32)
        for x in range(5):
            piece = turned[x * SPAN : (x + 1) * SPAN]
            if carried is not None:
                head = piece[:8] + carried[8 * x : 8 * x + 8]
                piece = jnp.concatenate([head, piece[8:]], 0)
            sums[f, x, group * SPAN : (group + 1) * SPAN, :] = piece
        carried = turned[5 * SPAN :]


def fill_faces(grid, f, second_half, gas, sums, up, down, row):
    ny = grid.span_y
    up[f] = sums[f, 4, :ny]
    down[f] = COUPLE * sums[f, 0, :ny] + gas[f, 0]
    for x in range(5):
        low_row = COUPLE * sums[f, x, 0:1, :]
        if x < 4:
            low_row = low_row + gas[f, x, 0:1, :]
        high_row = COUPLE * sums[f, x, ny : ny + 1, :]
        row[x, f : f + 1, :] = jnp.where(second_half, low_row, high_row)


def sample_kernel(
    grid, last, bricks, stay, lower, upper, gas, sums, from_up, from_down,
    from_row, corner_low, corner_high, tail_low, tail_high, weights, source, sampled, field, held
):
    ny = grid.span_y
    second_half = lax.axis_index("radial") == 1
    at_end = lax.axis_index("axial") == last
    face = jnp.where(second_half, 1.0, 0.0)
    for f in range(FIELDS):
        for x in range(5):
            extra = from_row[x, f : f + 1, :]
            if x == 0:
                extra = extra + corner_low[f : f + 1, :]
            if x == 4:
                extra = extra + corner_high[f : f + 1, :]
            first = row_numbers((8, grid.span_z)) == 0
            head = jnp.where(first, 2.0 * face * extra, 0.0)
            mine = sums[f, x, :ny, :]
            if x == 0:
                mine = mine + from_up[f]
            mine = jnp.concatenate([mine[:8] + head, mine[8:]], 0)
            tail = COUPLE * sums[f, x, ny : ny + 8, :]
            if x == 0:
                tail = tail + tail_low[f : f + 1, :]
            if x < 4:
                source[f, x] = mine
                mine = gas[f, x] + COUPLE * mine
            else:
                mine = COUPLE * mine + from_down[f]
                mine = jnp.where(at_end, 0.0, mine)
                tail = tail + tail_high[f : f + 1, :]
                tail = jnp.where(at_end, 0.0, tail)
                extra = jnp.where(at_end, 0.0, extra)
            tail = jnp.where(first & jnp.logical_not(second_half), tail + extra, 0.0)
            field[f, x, :ny, :] = mine
            field[f, x, ny : ny + 8, :] = tail
    for f in range(FIELDS):
        for group in range(grid.groups):
            edge = SPAN * (group + 1)
            pieces = [field[f, x, edge - SPAN : edge, :] for x in range(5)]
            if edge < grid.pad_y:
                pieces += [field[f, x, edge : edge + 1, :] for x in range(5)]
                pieces.append(jnp.zeros((3, grid.span_z), F32))
            else:
                pieces.append(jnp.zeros((8, grid.span_z), F32))
            turned = jnp.concatenate(pieces, 0).T
            at = (group * FIELDS + f) * grid.rows_z
            held[at : at + grid.span_z, :] = turned
            held[at + grid.span_z : at + grid.rows_z, :] = jnp.zeros((8, LANES), F32)

    offset = 0
    for part in (stay, lower, upper):
        blocks = part.shape[1] // LANES

        def step(turn, carry, part=part, offset=offset):
            for i in range(UNROLL):
                at = turn * UNROLL + i
                block = part[:, pl.ds(pl.multiple_of(at * LANES, LANES), LANES)]
                place_at = pl.multiple_of((offset + at) * 2 * LANES, 2 * LANES)
                plane = weights[pl.ds(place_at, 2 * LANES), :]
                values = sample_block(grid, block, bricks[offset + at], plane, held)
                lanes = pl.ds(pl.multiple_of((offset + at) * LANES, LANES), LANES)
                sampled[:, lanes] = values.astype(BF16)
            return carry

        lax.fori_loop(0, blocks // UNROLL, step, 0)
        offset += blocks


BIG = pltpu.CompilerParams(vmem_limit_bytes=12 * 2**20)


def deposit_call(grid, bricks, spread, lower, upper, zeros):
    return pl.pallas_call(
        functools.partial(deposit_kernel, grid),
        out_shape=jax.ShapeDtypeStruct((grid.rows, LANES), F32),
        in_specs=[SMEM, VMEM, VMEM, VMEM, VMEM],
        input_output_aliases={4: 0},
        compiler_params=BIG,
        name="deposit",
    )(bricks, spread, lower, upper, zeros)


def signal_entry(axial_at, radial_at):
    pl.semaphore_signal(
        pltpu.get_barrier_semaphore(), inc=1, device_id=(axial_at, radial_at),
        device_id_type=pl.DeviceIdType.MESH,
    )


def store_weights(target, at, weights):
    place = pl.multiple_of(at * 2 * LANES, 2 * LANES)
    target[pl.ds(place, 2 * LANES), :] = jnp.concatenate(weights, 0).astype(BF16)


def migrate_kernel(
    grid, last, bricks, up, down, stay, lower, upper, spread, sent, got
):
    a = lax.axis_index("axial")
    r = lax.axis_index("radial")
    has_above = a < last
    has_below = a > 0

    @pl.when(has_above)
    def _():
        signal_entry(a + 1, r)

    @pl.when(has_below)
    def _():
        signal_entry(a - 1, r)

    def copy(number, source, target, axial_at):
        return pltpu.make_async_remote_copy(
            src_ref=source, dst_ref=target, send_sem=sent.at[number],
            recv_sem=got.at[number], device_id=(axial_at, r),
            device_id_type=pl.DeviceIdType.MESH,
        )

    rising = copy(0, up, lower, a + 1)
    falling = copy(1, down, upper, a - 1)

    def step(turn, carry):
        for i in range(TURN):
            at = turn * TURN + i
            block = stay[:, pl.ds(pl.multiple_of(at * LANES, LANES), LANES)]
            plane = plane_weights(block, grid.place(bricks[at])[1])
            rows = pl.ds(pl.multiple_of(at * 8 * FIELDS, 8), 8 * FIELDS)
            spread[rows, :] = spread_block(block, plane)
        return carry

    peers = has_above.astype(jnp.int32) + has_below.astype(jnp.int32)
    pl.semaphore_wait(pltpu.get_barrier_semaphore(), peers)

    upper_core = a % 2 == 1
    for far in (True, False):

        @pl.when(has_above & (upper_core == far))
        def _():
            rising.start()

        @pl.when(has_below & (upper_core != far))
        def _():
            falling.start()

    @pl.when(jnp.logical_not(has_below))
    def _():
        lower[...] = jnp.zeros_like(lower)

    @pl.when(jnp.logical_not(has_above))
    def _():
        upper[...] = jnp.zeros_like(upper)

    lax.fori_loop(0, stay.shape[1] // LANES // TURN, step, 0)

    @pl.when(has_above)
    def _():
        rising.wait_send()
        falling.wait_recv()

    @pl.when(has_below)
    def _():
        falling.wait_send()
        rising.wait_recv()


def migrate_call(grid, last, bricks, up, down, stay):
    blocks = stay.shape[1] // LANES
    return pl.pallas_call(
        functools.partial(migrate_kernel, grid, last),
        out_shape=(
            jax.ShapeDtypeStruct(up.shape, F32),
            jax.ShapeDtypeStruct(down.shape, F32),
            jax.ShapeDtypeStruct((blocks * 8 * FIELDS, LANES), F32),
        ),
        in_specs=[SMEM] + [VMEM] * 3,
        out_specs=(VMEM,) * 3,
        scratch_shapes=[pltpu.SemaphoreType.DMA((2,)), pltpu.SemaphoreType.DMA((2,))],
        compiler_params=pltpu.CompilerParams(
            collective_id=1, has_side_effects=True, vmem_limit_bytes=8 * 2**20
        ),
        name="migrate",
    )(bricks, up, down, stay)


def exchange_kernel(
    grid, last, bricks, stay, lower, upper, gas, total, sums, from_up, from_down, from_row,
    corner_low, corner_high, tail_low, tail_high, weights, up, down, edge, sent, got
):
    a = lax.axis_index("axial")
    r = lax.axis_index("radial")
    has_above = a < last
    has_below = a > 0
    signal_entry(a, 1 - r)

    @pl.when(has_above)
    def _():
        signal_entry(a + 1, r)
        signal_entry(a + 1, 1 - r)

    @pl.when(has_below)
    def _():
        signal_entry(a - 1, r)
        signal_entry(a - 1, 1 - r)

    peers = 1 + 2 * has_above.astype(jnp.int32) + 2 * has_below.astype(jnp.int32)

    def copy(number, source, target, axial_at, radial_at):
        return pltpu.make_async_remote_copy(
            src_ref=source, dst_ref=target, send_sem=sent.at[number],
            recv_sem=got.at[number], device_id=(axial_at, radial_at),
            device_id_type=pl.DeviceIdType.MESH,
        )

    row = copy(0, edge, from_row, a, 1 - r)
    ends_up = [
        copy(1, edge.at[4], corner_low, a + 1, 1 - r),
        copy(2, edge.at[4], tail_low, a + 1, r),
    ]
    ends_down = [
        copy(3, edge.at[0], corner_high, a - 1, 1 - r),
        copy(4, edge.at[0], tail_high, a - 1, r),
    ]
    faces_up = [copy(5 + f, up.at[f], from_up.at[f], a + 1, r) for f in range(FIELDS)]
    faces_down = [
        copy(5 + FIELDS + f, down.at[f], from_down.at[f], a - 1, r) for f in range(FIELDS)
    ]
    select = merge_selector()
    for x in range(5):
        edge[x, FIELDS:, :] = jnp.zeros((8 - FIELDS, grid.span_z), F32)
    def weigh(part, offset):
        def step(turn, carry):
            for i in range(TURN):
                at = turn * TURN + i
                block = part[:, pl.ds(pl.multiple_of(at * LANES, LANES), LANES)]
                plane = plane_weights(block, grid.place(bricks[offset + at])[1])
                store_weights(weights, offset + at, plane)
            return carry

        lax.fori_loop(0, part.shape[1] // LANES // TURN, step, 0)

    for f in range(FIELDS):
        merge_field(grid, f, select, total, sums)
        fill_faces(grid, f, r == 1, gas, sums, up, down, edge)
    pl.semaphore_wait(pltpu.get_barrier_semaphore(), peers)
    row.start()

    @pl.when(has_above)
    def _():
        for each in ends_up:
            each.start()

    @pl.when(has_below)
    def _():
        for each in ends_down:
            each.start()

    upper_core = a % 2 == 1
    for far in (True, False):

        @pl.when(has_above & (upper_core == far))
        def _():
            for each in faces_up:
                each.start()

        @pl.when(has_below & (upper_core != far))
        def _():
            for each in faces_down:
                each.start()

    @pl.when(jnp.logical_not(has_below))
    def _():
        from_up[...] = jnp.zeros_like(from_up)
        corner_low[...] = jnp.zeros_like(corner_low)
        tail_low[...] = jnp.zeros_like(tail_low)

    @pl.when(jnp.logical_not(has_above))
    def _():
        from_down[...] = jnp.zeros_like(from_down)
        corner_high[...] = jnp.zeros_like(corner_high)
        tail_high[...] = jnp.zeros_like(tail_high)

    resident = stay.shape[1] // LANES
    weigh(stay, 0)
    weigh(lower, resident)
    weigh(upper, resident + lower.shape[1] // LANES)
    row.wait()

    @pl.when(has_above)
    def _():
        for each in faces_up + ends_up:
            each.wait_send()
        for each in faces_down + ends_down:
            each.wait_recv()

    @pl.when(has_below)
    def _():
        for each in faces_down + ends_down:
            each.wait_send()
        for each in faces_up + ends_up:
            each.wait_recv()


def exchange_call(grid, last, bricks, stay, lower, upper, gas, total):
    plane = (FIELDS, grid.span_y, grid.span_z)
    edge = (5, 8, grid.span_z)
    corner = jax.ShapeDtypeStruct(edge[1:], F32)
    copies = 5 + 2 * FIELDS
    return pl.pallas_call(
        functools.partial(exchange_kernel, grid, last),
        out_shape=(
            jax.ShapeDtypeStruct((FIELDS, 5, grid.pad_y, grid.span_z), F32),
            jax.ShapeDtypeStruct(plane, F32),
            jax.ShapeDtypeStruct(plane, F32),
            jax.ShapeDtypeStruct(edge, F32),
            corner,
            corner,
            corner,
            corner,
            jax.ShapeDtypeStruct((bricks.shape[0] * 2 * LANES, LANES), BF16),
        ),
        in_specs=[SMEM] + [VMEM] * 5,
        out_specs=(VMEM,) * 9,
        scratch_shapes=[
            pltpu.VMEM(plane, F32),
            pltpu.VMEM(plane, F32),
            pltpu.VMEM(edge, F32),
            pltpu.SemaphoreType.DMA((copies,)),
            pltpu.SemaphoreType.DMA((copies,)),
        ],
        compiler_params=pltpu.CompilerParams(
            collective_id=0, has_side_effects=True, vmem_limit_bytes=8 * 2**20
        ),
        name="exchange",
    )(bricks, stay, lower, upper, gas, total)


def sample_call(grid, last, bricks, *arrays):
    gas = arrays[3]
    return pl.pallas_call(
        functools.partial(sample_kernel, grid, last),
        out_shape=(
            jax.ShapeDtypeStruct(gas.shape, F32),
            jax.ShapeDtypeStruct((FIELDS, bricks.shape[0] * LANES), BF16),
        ),
        in_specs=[SMEM] + [VMEM] * 13,
        scratch_shapes=[
            pltpu.VMEM((FIELDS, 5, grid.pad_y, grid.span_z), F32),
            pltpu.VMEM((grid.rows, LANES), F32),
        ],
        compiler_params=BIG,
        name="sample",
    )(bricks, *arrays)


def per_device(load, offset, cell, rows, bricks, gas):
    axial = lax.axis_size("axial")
    span_y, span_z = gas.shape[2], gas.shape[3]
    grid = Grid(span_y, span_z)
    zeros, none_gone = clear_call(grid, load.shape[1] // LANES)
    up, down, stay = gather_call(load, offset, cell, rows, none_gone)
    lower, upper, spread = migrate_call(grid, axial - 1, bricks, up, down, stay)
    total = deposit_call(grid, bricks, spread, lower, upper, zeros)
    arrived = exchange_call(grid, axial - 1, bricks, stay, lower, upper, gas, total)
    return sample_call(
        grid, axial - 1, bricks, stay, lower, upper, gas, *arrived
    )


def solution(mesh):
    return jax.shard_map(
        per_device,
        mesh=mesh,
        in_specs=(
            P(None, ("axial", "radial")),
            P(None, ("axial", "radial")),
            P(("axial", "radial")),
            P(None, ("axial", "radial")),
            P(("axial", "radial")),
            P(None, "axial", "radial", None),
        ),
        out_specs=(P(None, "axial", "radial", None), P(None, ("axial", "radial"))),
        check_vma=False,
    )
```
